32 devices in a mesh: dp: 8 (over y, x, core), grid: 4 (over z).
Axes of the slice: x: 2, y: 2, z: 4, core: 2. Of those that a mesh axis runs over, the one named last changes fastest.
Arguments:
- tokens: bfloat16 [32, 1024, 768], P(('dp', 'grid')), may hold values from -6 to 6
- boxes: int32 [32, 2, 1024], P(('dp', 'grid')), may hold values from 0 to 999
- segments: int32 [32, 448], P(('dp', 'grid')), may hold values from 0 to 63, never falling along the last dimension, each value on 1 to 14 neighbouring positions
- patches: int32 [32], P(('dp', 'grid')), may hold values from 256 to 576, as said below
- cot_out: bfloat16 [32, 1024, 768], P(('dp', 'grid')), may hold values from -6 to 6
- cot_pair: float32 [32, 64, 64], P(('dp', 'grid')), may hold values from -6 to 6
- weights: float32 [10752, 768], P(('dp', 'grid')), may hold values from -4 to 4
- weight_momentum: float32 [10752, 768], P(('dp', 'grid')), may hold values from -320 to 320
- weight_average: float32 [10752, 768], P(('dp', 'grid')), may hold values from -4 to 4
- vectors: float32 [12, 768], replicated, may hold values from -4 to 4
- vector_momentum: float32 [12, 768], replicated, may hold values from -512 to 512
- vector_average: float32 [12, 768], replicated, may hold values from -4 to 4
- box_coef: float32 [2, 12], replicated, may hold values from -0.1 to 0.1
- coef_momentum: float32 [2, 12], replicated, may hold values from -5120 to 5120
- coef_average: float32 [2, 12], replicated, may hold values from -0.1 to 0.1
Outputs:
- mixed: bfloat16 [32, 1024, 768], P(('dp', 'grid'))
- pair_scores: float32 [32, 64, 64], P(('dp', 'grid'))
- token_grad: bfloat16 [32, 1024, 768], P(('dp', 'grid'))
- weight_grad: float32 [10752, 768], P(('dp', 'grid'))
- new_weights: float32 [10752, 768], P(('dp', 'grid'))
- new_weight_momentum: float32 [10752, 768], P(('dp', 'grid'))
- new_weight_average: float32 [10752, 768], P(('dp', 'grid'))
- new_weights_low: bfloat16 [10752, 768], P(('dp', 'grid'))
- vector_grad: float32 [12, 768], replicated
- new_vectors: float32 [12, 768], replicated
- new_vector_momentum: float32 [12, 768], replicated
- new_vector_average: float32 [12, 768], replicated
- coef_grad: float32 [2, 12], replicated
- new_coef: float32 [2, 12], replicated
- new_coef_momentum: float32 [2, 12], replicated
- new_coef_average: float32 [2, 12], replicated
The draws below stay inside these ranges and needn't reach their ends.
Inputs may be any that keep to these rules, and one draw needn't show every extreme that they name: Each page has 256 or 576 patches; both occur in every draw. `segments`: segment numbers never fall along a page; every segment holds 1 to 14 text tokens, some exactly 14.
All inputs are finite; a program needn't handle non-finite values.
Results may differ from the reference program's by a relative error of at most 0.022.
Values may be sent and summed in bfloat16 or wider, within the bound.
No kernel may reach another device: no remote copies, remote signals or barrier semaphores. Data moves between devices by JAX's collectives and lax.ppermute only.
A program may use at most 256 MiB of HBM per device.

```python
import math
import jax
import jax.numpy as jnp
import numpy as np
from jax import lax

D = 768
HEADS = 12
HDIM = 64
FF = 3072
TEXT = 448
PATCH_MAX = 576
PATCH_MIN = 256
SEGS = 64
BLOCK = 512
SLOTS = 1024
PAGES = 32
COLS = 10752
VROWS = 12
SEG_MOST = 14


def row_factor():
    row_ids = jnp.arange(COLS)[:, None]
    factor = jnp.where((row_ids >= 3 * D) & (row_ids < 4 * D), 5.0, 1.0)
    factor = jnp.where(row_ids >= 4 * D + 2 * FF, 2.0, factor)
    return factor * D ** (-0.5)


def vector_rows(noise):
    row_ids = jnp.arange(VROWS)[:, None]
    is_gain = (row_ids == 0) | (row_ids == 5)
    return jnp.clip(jnp.where(is_gain, 1.0 + 0.1 * noise, 0.2 * noise), -4.0, 4.0)


def draw_weights(key, part):
    key = jax.random.fold_in(key, 11)
    noise = jax.random.normal(key, (COLS, D), jnp.float32)
    return jnp.clip(noise * row_factor(), -4.0, 4.0)


def draw_weight_average(key, part):
    key = jax.random.fold_in(key, 13)
    noise = jax.random.normal(key, (COLS, D), jnp.float32)
    return jnp.clip(noise * row_factor(), -4.0, 4.0)


def draw_vectors(key, part):
    key = jax.random.fold_in(key, 12)
    noise = jax.random.normal(key, (VROWS, D), jnp.float32)
    return vector_rows(noise)


def draw_vector_average(key, part):
    key = jax.random.fold_in(key, 14)
    noise = jax.random.normal(key, (VROWS, D), jnp.float32)
    return vector_rows(noise)


def draw_patches(key, part):
    key = jax.random.fold_in(key, 15)
    picked = jax.random.randint(key, (PAGES,), 0, 2, jnp.int32)
    counts = PATCH_MIN + picked * (PATCH_MAX - PATCH_MIN)
    return counts.at[0].set(PATCH_MAX).at[1].set(PATCH_MIN).astype(jnp.int32)


def touch_ends(result, key, least, high):
    dims = result.shape
    index_at = [jax.random.randint(jax.random.fold_in(key, axis), (), 0, dims[axis]) for axis in range(len(dims))]
    result = result.at[tuple(index_at)].set(least)
    longest = dims.index(max(dims))
    index_at[longest] = (index_at[longest] + 1) % dims[longest]
    return result.at[tuple(index_at)].set(high)


def levels(own_key, shape, cuts, low, largest):
    def one(axis_at, blocks):
        heights = jax.random.uniform(jax.random.fold_in(jax.random.fold_in(own_key, 6), axis_at), (blocks,), jnp.float32, low / len(cuts), largest / len(cuts))
        return jnp.repeat(jnp.exp(heights), shape[axis_at] // blocks).reshape((-1,) + (1,) * (len(shape) - axis_at - 1))

    level = one(*cuts[0])
    for cut in cuts[1:]:
        level = level * one(*cut)
    return level


def length_profile(number_of, total, bound, slope):
    portions = [(1 << 20) // math.isqrt(rank ** slope) + 1 for rank in range(2, number_of + 1)]
    spare, holding = total - bound - (number_of - 1), [1] * (number_of - 1)
    while spare > 0:
        movable = [i for i in range(number_of - 1) if holding[i] < bound]
        whole, left = sum([portions[i] for i in movable]), spare
        for i in movable:
            extra = min(bound - holding[i], max(1, left * portions[i] // whole), spare)
            holding[i] = holding[i] + extra
            spare = spare - extra
    return np.array([bound] + holding)


def uneven(stream_key, count, total, reach, slope):
    if count == 2:
        one = jax.random.randint(stream_key, (), max(1, total - reach), min(reach, total - 1) + 1)
        return jnp.stack([one, total - one])
    lengths = jnp.asarray(length_profile(count, total, reach, slope), jnp.int32)
    pairs = (count - 1) // 2
    source_of, receiver = lengths[1:1 + 2 * pairs:2], lengths[2:2 + 2 * pairs:2]
    room = jnp.minimum(source_of - 1, reach - receiver)
    shifted = jax.random.randint(jax.random.fold_in(stream_key, 1), (pairs,), 0, 1 << 20) % (room + 1)
    lengths = lengths.at[1:1 + 2 * pairs:2].set(source_of - shifted).at[2:2 + 2 * pairs:2].set(receiver + shifted)
    return lengths[jax.random.permutation(jax.random.fold_in(stream_key, 2), count)]


def centred(own_key, shape, width, most, cuts=(), kind=jnp.bfloat16):
    factor_of = levels(own_key, shape, cuts, -0.22, 0.18) if cuts else 1.0
    result = jax.random.normal(own_key, shape, jnp.float32) * width * factor_of
    return jnp.minimum(jnp.maximum(result, -most), most).astype(kind)


def setup_inputs(seed: int = 0) -> dict:
    arg_keys = jax.random.split(jax.random.key(seed), 16)
    tokens = centred(arg_keys[0], (PAGES, SLOTS, D), 1.0, 6.0, ((0, 32),))
    boxes = touch_ends(jax.random.randint(arg_keys[1], (PAGES, 2, SLOTS), 0, 1000), jax.random.fold_in(arg_keys[1], 1), 0, 999).astype(jnp.int32)
    segments = jax.vmap(lambda own: jnp.searchsorted(jnp.cumsum(uneven(own, SEGS, TEXT, SEG_MOST, 0)), jnp.arange(TEXT), side="right"))(jax.random.split(arg_keys[2], PAGES)).reshape((PAGES, TEXT)).astype(jnp.int32)
    patches = draw_patches(jax.random.fold_in(arg_keys[15], 71), 0)
    cot_out = centred(arg_keys[4], (PAGES, SLOTS, D), 1.0, 6.0, ((0, 32),))
    cot_pair = centred(arg_keys[5], (PAGES, SEGS, SEGS), 1.0, 6.0, ((0, 32),), jnp.float32)
    weights = draw_weights(jax.random.fold_in(arg_keys[15], 71), 0)
    weight_momentum = centred(arg_keys[7], (COLS, D), (0.3 * (PAGES * SLOTS) ** 0.5), 320.0, ((0, 32),), jnp.float32)
    weight_average = draw_weight_average(jax.random.fold_in(arg_keys[15], 71), 0)
    vectors = draw_vectors(jax.random.fold_in(arg_keys[15], 71), 0)
    vector_momentum = centred(arg_keys[10], (VROWS, D), (0.5 * (PAGES * SLOTS) ** 0.5), 512.0, (), jnp.float32)
    vector_average = draw_vector_average(jax.random.fold_in(arg_keys[15], 71), 0)
    box_coef = jnp.clip(jax.random.uniform(arg_keys[12], (2, HEADS), jnp.float32, -0.1, 0.1), -0.1, 0.1)
    coef_momentum = centred(arg_keys[13], (2, HEADS), (0.15 * (PAGES * SLOTS * SLOTS) ** 0.5), 5120.0, (), jnp.float32)
    coef_average = jnp.clip(jax.random.uniform(arg_keys[14], (2, HEADS), jnp.float32, -0.1, 0.1), -0.1, 0.1)
    return {"tokens": tokens, "boxes": boxes, "segments": segments, "patches": patches, "cot_out": cot_out, "cot_pair": cot_pair, "weights": weights, "weight_momentum": weight_momentum, "weight_average": weight_average, "vectors": vectors, "vector_momentum": vector_momentum, "vector_average": vector_average, "box_coef": box_coef, "coef_momentum": coef_momentum, "coef_average": coef_average}


@jax.custom_vjp
def low(v):
    return lax.optimization_barrier(v.astype(jnp.bfloat16)).astype(jnp.float32)

@jax.custom_vjp
def low_back(v):
    return v

def low_keep(v):
    return (low(v), None)

def low_pass(kept, grad):
    return (grad,)

def back_keep(v):
    return (v, None)

def back_low(kept, grad):
    return (low(grad),)
low.defvjp(low_keep, low_pass)
low_back.defvjp(back_keep, back_low)
highest = lax.Precision.HIGHEST

def normalize(values, gain, shift):
    row_mean = lax.optimization_barrier(jnp.mean(values, axis=-1, keepdims=True))
    centered = values - row_mean
    variance = lax.optimization_barrier(jnp.mean(centered * centered, axis=-1, keepdims=True))
    return centered * lax.rsqrt(variance + 1e-05) * gain + shift

def buckets(row_boxes, col_boxes):
    spread = jnp.abs(row_boxes[:, :, None] - col_boxes[:, None, :])
    return jnp.minimum(spread // 32, 31).astype(jnp.float32)

def page_layer(params, page_data):
    weight_qkv, weight_out, weight_up, weight_down, weight_left, weight_right, vectors, box_coef = params
    page_tokens, page_boxes, page_segments, page_patches = page_data
    bias_qkv = jnp.concatenate([vectors[2], jnp.zeros((D,), jnp.float32), vectors[3]])
    packed = low(low_back(jnp.dot(page_tokens, weight_qkv.T, precision=highest) + bias_qkv))
    queries = packed[:, :D].reshape(SLOTS, HEADS, HDIM)
    keys_all = packed[:, D:2 * D].reshape(SLOTS, HEADS, HDIM)
    values_all = packed[:, 2 * D:].reshape(SLOTS, HEADS, HDIM)
    key_live = jnp.arange(SLOTS, dtype=jnp.int32) < TEXT + page_patches

    def attend(block_index):
        start = (block_index * BLOCK).astype(jnp.int32)
        query_block = lax.dynamic_slice_in_dim(queries, start, BLOCK, 0)
        row_boxes = lax.dynamic_slice_in_dim(page_boxes, start, BLOCK, 1)
        bucket = buckets(row_boxes, page_boxes)
        scores = jnp.einsum('qhd,khd->hqk', query_block, keys_all, precision=highest) * HDIM ** (-0.5)
        scores = scores + box_coef[0][:, None, None] * bucket[0] + box_coef[1][:, None, None] * bucket[1]
        scores = low_back(jnp.where(key_live, scores, -1e+30))
        top = lax.optimization_barrier(jnp.max(scores, axis=-1, keepdims=True))
        exponent = jnp.exp(scores - top)
        softmax_out = exponent / lax.optimization_barrier(jnp.sum(exponent, axis=-1, keepdims=True))
        blended = jnp.einsum('hqk,khd->qhd', low(softmax_out), values_all, precision=highest)
        return blended.reshape(BLOCK, D)
    attended = lax.map(jax.checkpoint(attend), jnp.arange(SLOTS // BLOCK, dtype=jnp.int32))
    attended = low(low_back(attended.reshape(SLOTS, D)))
    branch = low_back(jnp.dot(attended, weight_out.T, precision=highest) + vectors[4])
    hidden_one = normalize(page_tokens + branch, vectors[0], vectors[1])
    pre_act = low_back(jnp.dot(low(hidden_one), weight_up.T, precision=highest) + vectors[8:].reshape(FF))
    activated = low(jax.nn.gelu(pre_act, approximate=False))
    feed = low_back(jnp.dot(activated, weight_down, precision=highest) + vectors[7])
    output = normalize(hidden_one + feed, vectors[5], vectors[6])
    member = (page_segments[None, :] == jnp.arange(SEGS, dtype=jnp.int32)[:, None]).astype(jnp.float32)
    counted = lax.optimization_barrier(jnp.sum(member, axis=1, keepdims=True))
    pooled = low(jnp.dot(member, output[:TEXT], precision=highest) / counted)
    left_side = low(low_back(jnp.dot(pooled, weight_left.T, precision=highest)))
    right_side = low(low_back(jnp.dot(pooled, weight_right.T, precision=highest)))
    pair = jnp.dot(left_side, right_side.T, precision=highest) * D ** (-0.5)
    return (output, pair)

def momentum_step(grad, param, moment, average, rate):
    new_moment = 0.5 * moment + grad
    new_param = param - rate * (grad + 0.5 * new_moment)
    new_average = 0.5 * average + 0.5 * new_param
    return (new_moment, new_param, new_average)

def reference(tokens, boxes, segments, patches, cot_out, cot_pair, weights, weight_momentum, weight_average, vectors, vector_momentum, vector_average, box_coef, coef_momentum, coef_average):

    def forward(weight_all, vector_all, coef_all, token_all):
        rounded = low(weight_all)
        pieces = jnp.split(rounded, [3 * D, 4 * D, 4 * D + FF, 4 * D + 2 * FF, 5 * D + 2 * FF])
        params = (pieces[0], pieces[1], pieces[2], pieces[3], pieces[4], pieces[5], vector_all, coef_all)

        def one_page(page_data):
            return page_layer(params, page_data)
        return lax.map(jax.checkpoint(one_page), (token_all, boxes, segments, patches))
    token_float = tokens.astype(jnp.float32)
    (output, pair_scores), pull_back = jax.vjp(forward, weights, vectors, box_coef, token_float)
    live = (jnp.arange(SLOTS, dtype=jnp.int32)[None, :] < (TEXT + patches)[:, None]).astype(jnp.float32)
    weight_grad, vector_grad, coef_grad, token_grad = pull_back((cot_out.astype(jnp.float32) * live[:, :, None], cot_pair))
    rate_scale = (PAGES * SLOTS) ** (-0.5)
    new_weight_momentum, new_weights, new_weight_average = momentum_step(weight_grad, weights, weight_momentum, weight_average, 0.1 * rate_scale)
    new_vector_momentum, new_vectors, new_vector_average = momentum_step(vector_grad, vectors, vector_momentum, vector_average, 0.1 * rate_scale)
    new_coef_momentum, new_coef, new_coef_average = momentum_step(coef_grad, box_coef, coef_momentum, coef_average, 0.01 * rate_scale)
    return (output.astype(jnp.bfloat16), pair_scores, token_grad.astype(jnp.bfloat16), weight_grad, new_weights, new_weight_momentum, new_weight_average, new_weights.astype(jnp.bfloat16), vector_grad, new_vectors, new_vector_momentum, new_vector_average, coef_grad, new_coef, new_coef_momentum, new_coef_average)
```

```python
import math

import jax
import jax.numpy as jnp
from jax import lax
from jax.experimental import pallas as pl
from jax.experimental.pallas import tpu as pltpu
from jax.sharding import PartitionSpec as P

D = 768
HEADS = 12
HDIM = 64
FF = 3072
TEXT = 448
SEGS = 64
GROUP = 4
GW = GROUP * HDIM
TILE = 256
VMEM_LIMIT = 60 * 1024 * 1024
NT = (((1,), (1,)), ((), ()))
NN = (((1,), (0,)), ((), ()))
TN = (((0,), (0,)), ((), ()))

def dot(a, b, dims):
    return lax.dot_general(a, b, dims, preferred_element_type=jnp.float32)


def split_dot(exact, b, dims):
    high = b.astype(jnp.bfloat16)
    rest = b - high.astype(jnp.float32)
    middle = rest.astype(jnp.bfloat16)
    last = (rest - middle.astype(jnp.float32)).astype(jnp.bfloat16)
    return dot(exact, high, dims) + dot(exact, middle, dims) + dot(exact, last, dims)


def params():
    return pltpu.CompilerParams(vmem_limit_bytes=VMEM_LIMIT)


def cost(flops, nbytes):
    return pl.CostEstimate(flops=int(flops), bytes_accessed=int(nbytes), transcendentals=0)


def tile_rows(step):
    return pl.ds(pl.multiple_of(step * TILE, TILE), TILE)


def fixed(shape):
    return pl.BlockSpec(shape, lambda *_: (0,) * len(shape))


def write_buckets(box_row_ref, box_col_ref, bucket_refs):
    def fill(step):
        rows = tile_rows(step)
        for c in range(2):
            spread = jnp.abs(box_col_ref[rows, c : c + 1] - box_row_ref[c : c + 1, :])
            bucket_refs[c][rows, :] = jnp.minimum(spread >> 5, 31).astype(jnp.float32)

    pl.loop(0, box_row_ref.shape[1] // TILE)(fill)


def attention_forward_kernel(
    coef_ref,
    patches_ref,
    tokens_ref,
    wq_ref,
    wk_ref,
    wv_ref,
    bq_ref,
    bv_ref,
    box_row_ref,
    box_col_ref,
    q_ref,
    k_ref,
    v_ref,
    grown_ref,
    att_ref,
    inv_ref,
    bucket0_ref,
    bucket1_ref,
    key_ref,
    value_ref,
):
    head = pl.program_id(0)
    slots = tokens_ref.shape[0]
    own = head % GROUP

    @pl.when(head == 0)
    def _():
        write_buckets(box_row_ref, box_col_ref, (bucket0_ref, bucket1_ref))

    @pl.when(own == 0)
    def _():
        q_ref[...] = (dot(tokens_ref[...], wq_ref[...], NT) + bq_ref[...]).astype(jnp.bfloat16)
        k_ref[...] = dot(tokens_ref[...], wk_ref[...], NT).astype(jnp.bfloat16)
        v_ref[...] = (dot(tokens_ref[...], wv_ref[...], NT) + bv_ref[...]).astype(jnp.bfloat16)

    lanes = lax.broadcasted_iota(jnp.int32, (1, GW), 1)
    mine = lanes // HDIM == own
    mask_lane = lanes == (own * HDIM + HDIM) % GW
    empty = lax.broadcasted_iota(jnp.int32, (slots, 1), 0) >= TEXT + patches_ref[0]
    empty_term = jnp.where(empty, -1e30, 0.0)
    key_ref[...] = jnp.where(
        mine, k_ref[...].astype(jnp.float32), jnp.where(mask_lane, empty_term, 0.0)
    ).astype(jnp.bfloat16)
    value_ref[...] = jnp.where(mine, v_ref[...].astype(jnp.float32), 1.0).astype(jnp.bfloat16)
    coef0 = coef_ref[0, head]
    coef1 = coef_ref[1, head]
    lead = jnp.where(mask_lane, 1.0, 0.0)
    later = own > 0

    def rows_step(step):
        rows = tile_rows(step)
        query = jnp.where(
            mine, q_ref[rows, :].astype(jnp.float32) * HDIM ** (-0.5), lead
        ).astype(jnp.bfloat16)
        score = dot(query, key_ref[...], NT)
        score = score + coef0 * bucket0_ref[rows, :] + coef1 * bucket1_ref[rows, :]
        top = jnp.max(score, axis=1, keepdims=True)
        grown = jnp.exp(score - top).astype(jnp.bfloat16)
        grown_ref[0, rows, :] = grown
        both = dot(grown, value_ref[...], NN)
        inv = 1.0 / pltpu.roll(both, HDIM, 1)
        kept = jnp.where(later, att_ref[rows, :].astype(jnp.float32), 0.0)
        att_ref[rows, :] = jnp.where(mine, both * inv, kept).astype(jnp.bfloat16)
        inv_ref[rows, :] = jnp.where(mine, inv, jnp.where(later, inv_ref[rows, :], 0.0))

    pl.loop(0, slots // TILE, unroll=4)(rows_step)


def attention_forward(tokens, weight_qkv, vectors, boxes, patches, box_coef):
    slots = tokens.shape[0]
    blocks = D // GW
    smem = pl.BlockSpec(memory_space=pltpu.SMEM)
    lane_block = pl.BlockSpec((slots, GW), lambda h: (0, h // GROUP))
    bias = pl.BlockSpec((1, GW), lambda h: (0, h // GROUP))
    wide = jax.ShapeDtypeStruct((slots, D), jnp.bfloat16)

    def weight(at):
        return pl.BlockSpec((GW, D), lambda h: (at * blocks + h // GROUP, 0))

    return pl.pallas_call(
        attention_forward_kernel,
        grid=(HEADS,),
        in_specs=[
            smem,
            smem,
            fixed((slots, D)),
            weight(0),
            weight(1),
            weight(2),
            bias,
            bias,
            fixed((2, slots)),
            fixed((slots, 2)),
        ],
        out_specs=[lane_block] * 3
        + [pl.BlockSpec((1, slots, slots), lambda h: (h, 0, 0)), lane_block, lane_block],
        out_shape=[wide] * 3
        + [
            jax.ShapeDtypeStruct((HEADS, slots, slots), jnp.bfloat16),
            wide,
            jax.ShapeDtypeStruct((slots, D), jnp.float32),
        ],
        scratch_shapes=[pltpu.VMEM((slots, slots), jnp.float32)] * 2
        + [pltpu.VMEM((slots, GW), jnp.bfloat16)] * 2,
        compiler_params=params(),
        cost_estimate=cost(10e9, 40e6),
        name="attention_forward",
    )(
        box_coef,
        patches,
        tokens,
        weight_qkv,
        weight_qkv,
        weight_qkv,
        vectors[2:3],
        vectors[3:4],
        boxes,
        boxes.T,
    )


def normalize(values):
    centered = values - jnp.mean(values, axis=-1, keepdims=True)
    inv_std = lax.rsqrt(jnp.mean(centered * centered, axis=-1, keepdims=True) + 1e-05)
    return (centered * inv_std, inv_std)


def normalize_back(grad_normed, normed, inv_std):
    first_mean = jnp.mean(grad_normed, axis=-1, keepdims=True)
    second_mean = jnp.mean(grad_normed * normed, axis=-1, keepdims=True)
    return inv_std * (grad_normed - first_mean - normed * second_mean)


def gelu_pair(values):
    half = values * (0.5**0.5)
    size = jnp.abs(half)
    fraction = 1.0 / (1.0 + 0.3275911 * size)
    series = fraction * (
        0.254829592
        + fraction
        * (
            -0.284496736
            + fraction * (1.421413741 + fraction * (-1.453152027 + fraction * 1.061405429))
        )
    )
    bell = jnp.exp(-half * half)
    tail = 0.5 * series * bell
    below = jnp.where(values >= 0, 1.0 - tail, tail)
    return (values * below, below + values * bell * (0.5 / math.pi) ** 0.5)


def feed_forward_kernel(
    att_ref,
    tokens_ref,
    wo_ref,
    wu_ref,
    wd_ref,
    wl_ref,
    wr_ref,
    vectors_ref,
    segments_ref,
    cot_pair_ref,
    mixed_ref,
    normed1_ref,
    inv1_ref,
    hidden_ref,
    act_ref,
    slope_ref,
    normed2_ref,
    inv2_ref,
    pair_ref,
    spread_ref,
    dleft_ref,
    dright_ref,
    total_ref,
):
    step = pl.program_id(0)
    tile = att_ref.shape[0]
    branch = dot(att_ref[...], wo_ref[...], NT) + vectors_ref[4:5, :]
    normed1, inv1 = normalize(tokens_ref[...].astype(jnp.float32) + branch)
    hidden = normed1 * vectors_ref[0:1, :] + vectors_ref[1:2, :]
    low = hidden.astype(jnp.bfloat16)
    normed1_ref[...] = normed1
    inv1_ref[...] = inv1
    hidden_ref[...] = low
    feed = hidden + vectors_ref[7:8, :]
    for part in range(FF // D):
        cols = slice(part * D, (part + 1) * D)
        pre = dot(low, wu_ref[cols, :], NT) + vectors_ref[8 + part : 9 + part, :]
        act, slope = gelu_pair(pre)
        act = act.astype(jnp.bfloat16)
        act_ref[:, cols] = act
        slope_ref[:, cols] = slope.astype(jnp.bfloat16)
        feed = feed + dot(act, wd_ref[cols, :], NN)
    normed2, inv2 = normalize(feed)
    output = normed2 * vectors_ref[5:6, :] + vectors_ref[6:7, :]
    normed2_ref[...] = normed2
    inv2_ref[...] = inv2
    mixed_ref[...] = output.astype(jnp.bfloat16)

    @pl.when(step == 0)
    def _():
        total_ref[...] = jnp.zeros_like(total_ref)

    slot = step * tile + lax.broadcasted_iota(jnp.int32, (1, tile), 1)
    numbers = lax.broadcasted_iota(jnp.int32, (SEGS, 1), 0)

    @pl.when(step * tile < TEXT)
    def _():
        member = (segments_ref[:, pl.ds(pl.multiple_of(step * tile, tile), tile)] == numbers) & (slot < TEXT)
        total_ref[...] += split_dot(member.astype(jnp.bfloat16), output, NN)

    @pl.when(step == pl.num_programs(0) - 1)
    def _():
        member = (segments_ref[...] == numbers) & (
            lax.broadcasted_iota(jnp.int32, (1, segments_ref.shape[1]), 1) < TEXT
        )
        counted = jnp.sum(member.astype(jnp.float32), axis=1, keepdims=True)
        pooled = (total_ref[...] / counted).astype(jnp.bfloat16)
        scale = D ** (-0.5)
        left = dot(pooled, wl_ref[...], NT).astype(jnp.bfloat16)
        right = dot(pooled, wr_ref[...], NT).astype(jnp.bfloat16)
        pair_ref[...] = dot(left, right, NT) * scale
        cot = cot_pair_ref[...]
        grad_left = (split_dot_left(cot, right, NN) * scale).astype(jnp.bfloat16)
        grad_right = (split_dot_left(cot, left, TN) * scale).astype(jnp.bfloat16)
        grad_pooled = dot(grad_left, wl_ref[...], NN) + dot(grad_right, wr_ref[...], NN)
        spread_ref[...] = grad_pooled / counted
        dleft_ref[...] = dot(grad_left, pooled, TN).astype(jnp.bfloat16)
        dright_ref[...] = dot(grad_right, pooled, TN).astype(jnp.bfloat16)


def split_dot_left(a, exact, dims):
    high = a.astype(jnp.bfloat16)
    rest = a - high.astype(jnp.float32)
    middle = rest.astype(jnp.bfloat16)
    last = (rest - middle.astype(jnp.float32)).astype(jnp.bfloat16)
    return dot(high, exact, dims) + dot(middle, exact, dims) + dot(last, exact, dims)


def feed_forward(att, tokens, weights, vectors, segments, cot_pair):
    slots = att.shape[0]
    tile = pl.BlockSpec((TILE, D), lambda i: (i, 0))
    wide = pl.BlockSpec((TILE, FF), lambda i: (i, 0))
    column = pl.BlockSpec((TILE, 1), lambda i: (i, 0))

    def weight(rows, at):
        return pl.BlockSpec((rows, D), lambda i: (at // rows, 0), pipeline_mode=pl.Buffered(1))

    def shape(dims, dtype=jnp.float32):
        return jax.ShapeDtypeStruct(dims, dtype)

    return pl.pallas_call(
        feed_forward_kernel,
        grid=(slots // TILE,),
        in_specs=[
            tile,
            tile,
            weight(D, 3 * D),
            pl.BlockSpec((pl.Element(FF), pl.Element(D)), lambda i: (4 * D, 0), pipeline_mode=pl.Buffered(1)),
            pl.BlockSpec((pl.Element(FF), pl.Element(D)), lambda i: (4 * D + FF, 0), pipeline_mode=pl.Buffered(1)),
            weight(D, 4 * D + 2 * FF),
            weight(D, 5 * D + 2 * FF),
            fixed(vectors.shape),
            fixed((1, 512)),
            fixed((SEGS, SEGS)),
        ],
        out_specs=[tile, tile, column, tile, wide, wide, tile, column, fixed((SEGS, SEGS)), fixed((SEGS, D)), fixed((D, D)), fixed((D, D))],
        out_shape=[
            shape((slots, D), jnp.bfloat16),
            shape((slots, D)),
            shape((slots, 1)),
            shape((slots, D), jnp.bfloat16),
            shape((slots, FF), jnp.bfloat16),
            shape((slots, FF), jnp.bfloat16),
            shape((slots, D)),
            shape((slots, 1)),
            shape((SEGS, SEGS)),
            shape((SEGS, D)),
            shape((D, D), jnp.bfloat16),
            shape((D, D), jnp.bfloat16),
        ],
        scratch_shapes=[pltpu.VMEM((SEGS, D), jnp.float32)],
        compiler_params=params(),
        cost_estimate=cost(11e9, 50e6),
        name="feed_forward",
    )(
        att,
        tokens,
        weights,
        weights,
        weights,
        weights,
        weights,
        vectors,
        jnp.pad(segments, ((0, 0), (0, 512 - segments.shape[1])), constant_values=SEGS),
        cot_pair,
    )


def feed_backward_kernel(
    patches_ref,
    cot_ref,
    segments_ref,
    spread_ref,
    normed2_ref,
    inv2_ref,
    normed1_ref,
    inv1_ref,
    hidden_ref,
    att_ref,
    inv_sum_ref,
    vectors_ref,
    act_ref,
    slope_ref,
    wd_ref,
    wu_ref,
    wo_ref,
    dwd_ref,
    dwu_ref,
    dbu_ref,
    sums_ref,
    dwo_ref,
    dres_ref,
    datt_ref,
    grad_ref,
    total_ref,
):
    step = pl.program_id(0)
    slots = cot_ref.shape[0]

    @pl.when(step == 0)
    def _():
        sums_ref[...] = jnp.zeros_like(sums_ref)
        numbers = lax.broadcasted_iota(jnp.int32, (1, SEGS), 1)

        def rows_step(at):
            rows = tile_rows(at)
            slot = at * TILE + lax.broadcasted_iota(jnp.int32, (TILE, 1), 0)
            live = (slot < TEXT + patches_ref[0]).astype(jnp.float32)
            member = (segments_ref[rows, :] == numbers) & (slot < TEXT)
            grad = cot_ref[rows, :].astype(jnp.float32) * live
            grad = grad + split_dot(member.astype(jnp.bfloat16), spread_ref[...], NN)
            normed = normed2_ref[rows, :]
            sums_ref[5:6, :] += jnp.sum(grad * normed, axis=0, keepdims=True)
            sums_ref[6:7, :] += jnp.sum(grad, axis=0, keepdims=True)
            dres = normalize_back(grad * vectors_ref[5:6, :], normed, inv2_ref[rows, :])
            low = dres.astype(jnp.bfloat16)
            sums_ref[7:8, :] += jnp.sum(low.astype(jnp.float32), axis=0, keepdims=True)
            total_ref[rows, :] = dres
            grad_ref[rows, :] = low

        pl.loop(0, slots // TILE)(rows_step)

    dwd_ref[...] = dot(act_ref[...], grad_ref[...], TN).astype(jnp.bfloat16)
    dact = dot(grad_ref[...], wd_ref[...], NT)
    dpre = (dact * slope_ref[...].astype(jnp.float32)).astype(jnp.bfloat16)
    dbu_ref[...] = jnp.sum(dpre.astype(jnp.float32), axis=0, keepdims=True)
    dwu_ref[...] = dot(dpre, hidden_ref[...], TN).astype(jnp.bfloat16)
    total_ref[...] += dot(dpre, wu_ref[...], NN)

    @pl.when(step == pl.num_programs(0) - 1)
    def _():
        def rows_step(at):
            rows = tile_rows(at)
            grad = total_ref[rows, :]
            normed = normed1_ref[rows, :]
            sums_ref[0:1, :] += jnp.sum(grad * normed, axis=0, keepdims=True)
            sums_ref[1:2, :] += jnp.sum(grad, axis=0, keepdims=True)
            dres = normalize_back(grad * vectors_ref[0:1, :], normed, inv1_ref[rows, :])
            low = dres.astype(jnp.bfloat16)
            sums_ref[4:5, :] += jnp.sum(low.astype(jnp.float32), axis=0, keepdims=True)
            dres_ref[rows, :] = dres
            grad_ref[rows, :] = low
            datt = dot(low, wo_ref[...], NN).astype(jnp.bfloat16).astype(jnp.float32)
            datt_ref[rows, :] = (datt * inv_sum_ref[rows, :]).astype(jnp.bfloat16)

        pl.loop(0, slots // TILE)(rows_step)
        dwo_ref[...] = dot(grad_ref[...], att_ref[...], TN).astype(jnp.bfloat16)


def feed_backward(patches, cot_out, segments, spread, forward, att, inv_sum, vectors, weights):
    _, normed1, inv1, hidden, act, slope, normed2, inv2 = forward
    slots = cot_out.shape[0]
    chunk = 512

    def once(shape):
        return pl.BlockSpec(shape, lambda *_: (0,) * len(shape), pipeline_mode=pl.Buffered(1))

    def weight(at):
        return pl.BlockSpec((chunk, D), lambda i: (at // chunk + i, 0))

    def shape(dims, dtype=jnp.float32):
        return jax.ShapeDtypeStruct(dims, dtype)

    lane_block = pl.BlockSpec((slots, chunk), lambda i: (0, i))
    row_block = pl.BlockSpec((chunk, D), lambda i: (i, 0))
    full = once((slots, D))
    column = once((slots, 1))
    return pl.pallas_call(
        feed_backward_kernel,
        grid=(FF // chunk,),
        in_specs=[
            pl.BlockSpec(memory_space=pltpu.SMEM),
            full,
            column,
            once((SEGS, D)),
            full,
            column,
            full,
            column,
            full,
            full,
            full,
            once(vectors.shape),
            lane_block,
            lane_block,
            weight(4 * D + FF),
            weight(4 * D),
            pl.BlockSpec((D, D), lambda i: (3, 0), pipeline_mode=pl.Buffered(1)),
        ],
        out_specs=[row_block, row_block, pl.BlockSpec((1, chunk), lambda i: (0, i)), fixed((8, D)), fixed((D, D)), full, full],
        out_shape=[
            shape((FF, D), jnp.bfloat16),
            shape((FF, D), jnp.bfloat16),
            shape((1, FF)),
            shape((8, D)),
            shape((D, D), jnp.bfloat16),
            shape((slots, D)),
            shape((slots, D), jnp.bfloat16),
        ],
        scratch_shapes=[pltpu.VMEM((slots, D), jnp.bfloat16), pltpu.VMEM((slots, D), jnp.float32)],
        compiler_params=params(),
        cost_estimate=cost(22e9, 60e6),
        name="feed_backward",
    )(
        patches,
        cot_out,
        jnp.pad(segments, ((0, 0), (0, slots - segments.shape[1])), constant_values=SEGS).reshape(slots, 1),
        spread,
        normed2,
        inv2,
        normed1,
        inv1,
        hidden,
        att,
        inv_sum,
        vectors,
        act,
        slope,
        weights,
        weights,
        weights,
    )


def attention_backward_kernel(
    grown_ref,
    datt_ref,
    att_ref,
    v_ref,
    k_ref,
    q_ref,
    box_row_ref,
    box_col_ref,
    dqkv_ref,
    dcoef_ref,
    bucket0_ref,
    bucket1_ref,
    value_ref,
    lead_ref,
    qt_ref,
    dt_ref,
    kt_ref,
    dscore_ref,
):
    head = pl.program_id(0)
    slots = datt_ref.shape[0]
    own = head % GROUP

    @pl.when(head == 0)
    def _():
        write_buckets(box_row_ref, box_col_ref, (bucket0_ref, bucket1_ref))

    @pl.when(own == 0)
    def _():
        scale = HDIM ** (-0.5)
        qt_ref[...] = (q_ref[...].astype(jnp.float32) * scale).T.astype(jnp.bfloat16)
        kt_ref[...] = (k_ref[...].astype(jnp.float32) * scale).T.astype(jnp.bfloat16)
        dt_ref[...] = datt_ref[...].astype(jnp.float32).T.astype(jnp.bfloat16)

    lanes = lax.broadcasted_iota(jnp.int32, (1, GW), 1)
    mine = lanes // HDIM == own
    at = (own * HDIM + HDIM) % GW
    value_ref[...] = jnp.where(
        mine,
        v_ref[...].astype(jnp.float32),
        jnp.where((lanes >= at) & (lanes < at + 3), -1.0, 0.0),
    ).astype(jnp.bfloat16)
    grad = datt_ref[...].astype(jnp.float32)
    delta = jnp.sum(
        jnp.where(mine, grad * att_ref[...].astype(jnp.float32), 0.0), axis=1, keepdims=True
    )
    high = delta.astype(jnp.bfloat16).astype(jnp.float32)
    middle = (delta - high).astype(jnp.bfloat16).astype(jnp.float32)
    last = delta - high - middle
    terms = jnp.where(lanes == at, high, jnp.where(lanes == at + 1, middle, last))
    terms = jnp.where((lanes >= at) & (lanes < at + 3), terms, 0.0)
    lead_ref[...] = jnp.where(mine, grad, terms).astype(jnp.bfloat16)
    dcoef_ref[...] = jnp.zeros_like(dcoef_ref)

    def rows_step(step):
        rows = tile_rows(step)
        diff = dot(lead_ref[rows, :], value_ref[...], NT)
        dscore = grown_ref[0, rows, :].astype(jnp.float32) * diff
        dscore_ref[rows, :] = dscore.astype(jnp.bfloat16)
        dcoef_ref[0, 0:1, :] += jnp.sum(dscore * bucket0_ref[rows, :], axis=0, keepdims=True)
        dcoef_ref[0, 1:2, :] += jnp.sum(dscore * bucket1_ref[rows, :], axis=0, keepdims=True)

    pl.loop(0, slots // TILE, unroll=4)(rows_step)
    head_rows = pl.ds(pl.multiple_of(own * HDIM, HDIM), HDIM)
    dqkv_ref[0] = dot(kt_ref[head_rows, :], dscore_ref[...], NT).astype(jnp.bfloat16)
    dqkv_ref[1] = dot(qt_ref[head_rows, :], dscore_ref[...], NN).astype(jnp.bfloat16)
    dqkv_ref[2] = dot(dt_ref[head_rows, :], grown_ref[0], NN).astype(jnp.bfloat16)


def attention_backward(grown, datt, att, q, k, v, boxes):
    slots = datt.shape[0]
    lane_block = pl.BlockSpec((slots, GW), lambda h: (0, h // GROUP))
    return pl.pallas_call(
        attention_backward_kernel,
        grid=(HEADS,),
        in_specs=[pl.BlockSpec((1, slots, slots), lambda h: (h, 0, 0))]
        + [lane_block] * 5
        + [fixed((2, slots)), fixed((slots, 2))],
        out_specs=[
            pl.BlockSpec((3, HDIM, slots), lambda h: (0, h, 0)),
            pl.BlockSpec((1, 2, slots), lambda h: (h, 0, 0)),
        ],
        out_shape=[
            jax.ShapeDtypeStruct((3, D, slots), jnp.bfloat16),
            jax.ShapeDtypeStruct((HEADS, 2, slots), jnp.float32),
        ],
        scratch_shapes=[pltpu.VMEM((slots, slots), jnp.float32)] * 2
        + [pltpu.VMEM((slots, GW), jnp.bfloat16)] * 2
        + [pltpu.VMEM((GW, slots), jnp.bfloat16)] * 3
        + [pltpu.VMEM((slots, slots), jnp.bfloat16)],
        compiler_params=params(),
        cost_estimate=cost(15e9, 40e6),
        name="attention_backward",
    )(grown, datt, att, v, k, q, boxes, boxes.T)


def token_backward_kernel(dqkv_ref, weight_ref, tokens_ref, dres_ref, dweight_ref, sums_ref, grad_ref, total_ref):
    step = pl.program_id(0)
    part = dqkv_ref[0]
    dweight_ref[...] = dot(part, tokens_ref[...], NN).astype(jnp.bfloat16)
    sums_ref[0] = dot(jnp.ones((8, part.shape[1]), jnp.bfloat16), part, NT)
    term = dot(part, weight_ref[...], TN)

    @pl.when(step == 0)
    def _():
        total_ref[...] = dres_ref[...] + term

    @pl.when(step > 0)
    def _():
        total_ref[...] += term

    @pl.when(step == pl.num_programs(0) - 1)
    def _():
        grad_ref[...] = total_ref[...].astype(jnp.bfloat16)


def token_backward(dqkv, weights, tokens, dres):
    slots = tokens.shape[0]
    block = pl.BlockSpec((D, D), lambda i: (i, 0))
    return pl.pallas_call(
        token_backward_kernel,
        grid=(3,),
        in_specs=[pl.BlockSpec((1, D, slots), lambda i: (i, 0, 0)), block, fixed((slots, D)), fixed((slots, D))],
        out_specs=[block, pl.BlockSpec((1, 8, D), lambda i: (i, 0, 0)), fixed((slots, D))],
        out_shape=[
            jax.ShapeDtypeStruct((3 * D, D), jnp.bfloat16),
            jax.ShapeDtypeStruct((3, 8, D), jnp.float32),
            jax.ShapeDtypeStruct((slots, D), jnp.bfloat16),
        ],
        scratch_shapes=[pltpu.VMEM((slots, D), jnp.float32)],
        compiler_params=params(),
        cost_estimate=cost(7.3e9, 20e6),
        name="token_backward",
    )(dqkv, weights, tokens, dres)


def page_step(tokens, boxes, segments, patches, cot_out, cot_pair, gathered, vectors, box_coef):
    q, k, v, grown, att, inv_sum = attention_forward(
        tokens, gathered, vectors, boxes, patches, box_coef
    )
    found = feed_forward(att, tokens, gathered, vectors, segments, cot_pair)
    mixed, pair_scores, spread, dwl, dwr = found[0], found[8], found[9], found[10], found[11]
    dwd, dwu, dbu, sums, dwo, dres, datt = feed_backward(
        patches, cot_out, segments, spread, found[:8], att, inv_sum, vectors, gathered
    )
    dqkv, dcoef = attention_backward(grown, datt, att, q, k, v, boxes)
    dwqkv, bias_sums, token_grad = token_backward(dqkv, gathered, tokens, dres)
    vector_part = jnp.concatenate(
        [sums[:2], bias_sums[0, :1], bias_sums[2, :1], sums[4:8], dbu.reshape(FF // D, D)], axis=0
    )
    coef_part = jnp.sum(dcoef, axis=2).T
    return (mixed, pair_scores, token_grad, (dwqkv, dwo, dwu, dwd, dwl, dwr), vector_part, coef_part)


def exchange_sum(values):
    for axis in ("dp", "grid"):
        size = lax.axis_size(axis)
        reach = 1
        while reach < size:
            values = values + lax.ppermute(values, axis, [(i, i ^ reach) for i in range(size)])
            reach *= 2
    return values


def momentum_step(grad, param, moment, average, rate):
    new_moment = 0.5 * moment + grad
    new_param = param - rate * (grad + 0.5 * new_moment)
    new_average = 0.5 * average + 0.5 * new_param
    return (new_moment, new_param, new_average)


def on_device(
    tokens,
    boxes,
    segments,
    patches,
    cot_out,
    cot_pair,
    weights,
    weight_momentum,
    weight_average,
    vectors,
    vector_momentum,
    vector_average,
    box_coef,
    coef_momentum,
    coef_average,
):
    axes = ("dp", "grid")
    page_count, slot_count = tokens.shape[:2]
    device_count = lax.axis_size(axes)
    gathered = lax.all_gather(weights.astype(jnp.bfloat16), axes, axis=0, tiled=True)
    pages = [
        page_step(
            tokens[p], boxes[p], segments[p : p + 1], patches[p : p + 1], cot_out[p], cot_pair[p], gathered, vectors, box_coef
        )
        for p in range(page_count)
    ]
    mixed, pair_scores, token_grad = (jnp.stack([page[i] for page in pages]) for i in range(3))
    full_grad = sum(jnp.concatenate(page[3], axis=0) for page in pages)
    small = sum(
        jnp.concatenate([page[4], jnp.pad(page[5].reshape(1, 2 * HEADS), ((0, 3), (0, D - 2 * HEADS)))], axis=0)
        for page in pages
    )
    small = exchange_sum(small)
    weight_grad = lax.psum_scatter(full_grad, axes, scatter_dimension=0, tiled=True).astype(jnp.float32)
    vector_rows = vectors.shape[0]
    vector_grad = small[:vector_rows]
    coef_grad = small[vector_rows, : 2 * HEADS].reshape(2, HEADS)
    rate_scale = (device_count * page_count * slot_count) ** (-0.5)
    new_weight_momentum, new_weights, new_weight_average = momentum_step(
        weight_grad, weights, weight_momentum, weight_average, 0.1 * rate_scale
    )
    new_vector_momentum, new_vectors, new_vector_average = momentum_step(
        vector_grad, vectors, vector_momentum, vector_average, 0.1 * rate_scale
    )
    new_coef_momentum, new_coef, new_coef_average = momentum_step(
        coef_grad, box_coef, coef_momentum, coef_average, 0.01 * rate_scale
    )
    return (
        mixed,
        pair_scores,
        token_grad,
        weight_grad,
        new_weights,
        new_weight_momentum,
        new_weight_average,
        new_weights.astype(jnp.bfloat16),
        vector_grad,
        new_vectors,
        new_vector_momentum,
        new_vector_average,
        coef_grad,
        new_coef,
        new_coef_momentum,
        new_coef_average,
    )


def solution(mesh):
    rows = P(("dp", "grid"))
    return jax.shard_map(
        on_device,
        mesh=mesh,
        in_specs=(rows,) * 9 + (P(),) * 6,
        out_specs=(rows,) * 8 + (P(),) * 8,
        check_vma=False,
    )
```

```python
import math

import jax
import jax.numpy as jnp
from jax import lax
from jax.experimental import pallas as pl
from jax.experimental.pallas import tpu as pltpu
from jax.sharding import PartitionSpec as P

D = 768
HEADS = 12
HDIM = 64
FF = 3072
TEXT = 448
SEGS = 64
GROUP = 4
GW = GROUP * HDIM
TILE = 256
VMEM_LIMIT = 60 * 1024 * 1024
NT = (((1,), (1,)), ((), ()))
NN = (((1,), (0,)), ((), ()))
TN = (((0,), (0,)), ((), ()))

def dot(a, b, dims):
    return lax.dot_general(a, b, dims, preferred_element_type=jnp.float32)


def split_dot(exact, b, dims):
    high = b.astype(jnp.bfloat16)
    rest = b - high.astype(jnp.float32)
    middle = rest.astype(jnp.bfloat16)
    last = (rest - middle.astype(jnp.float32)).astype(jnp.bfloat16)
    return dot(exact, high, dims) + dot(exact, middle, dims) + dot(exact, last, dims)


def params():
    return pltpu.CompilerParams(vmem_limit_bytes=VMEM_LIMIT)


def cost(flops, nbytes):
    return pl.CostEstimate(flops=int(flops), bytes_accessed=int(nbytes), transcendentals=0)


def tile_rows(step):
    return pl.ds(pl.multiple_of(step * TILE, TILE), TILE)


def fixed(shape):
    return pl.BlockSpec(shape, lambda *_: (0,) * len(shape))


def write_buckets(box_row_ref, box_col_ref, bucket_refs):
    def fill(step):
        rows = tile_rows(step)
        for c in range(2):
            spread = jnp.abs(box_col_ref[rows, c : c + 1] - box_row_ref[c : c + 1, :])
            bucket_refs[c][rows, :] = jnp.minimum(spread >> 5, 31).astype(jnp.float32)

    pl.loop(0, box_row_ref.shape[1] // TILE)(fill)


def attention_forward_kernel(
    coef_ref,
    patches_ref,
    tokens_ref,
    wq_ref,
    wk_ref,
    wv_ref,
    bq_ref,
    bv_ref,
    box_row_ref,
    box_col_ref,
    q_ref,
    k_ref,
    v_ref,
    grown_ref,
    att_ref,
    inv_ref,
    exact_ref,
    bucket0_ref,
    bucket1_ref,
    key_ref,
    value_ref,
):
    head = pl.program_id(0)
    slots = tokens_ref.shape[0]
    own = head % GROUP

    @pl.when(head == 0)
    def _():
        write_buckets(box_row_ref, box_col_ref, (bucket0_ref, bucket1_ref))

    @pl.when(own == 0)
    def _():
        q_ref[...] = (dot(tokens_ref[...], wq_ref[...], NT) + bq_ref[...]).astype(jnp.bfloat16)
        k_ref[...] = dot(tokens_ref[...], wk_ref[...], NT).astype(jnp.bfloat16)
        v_ref[...] = (dot(tokens_ref[...], wv_ref[...], NT) + bv_ref[...]).astype(jnp.bfloat16)

    lanes = lax.broadcasted_iota(jnp.int32, (1, GW), 1)
    mine = lanes // HDIM == own
    mask_lane = lanes == (own * HDIM + HDIM) % GW
    empty = lax.broadcasted_iota(jnp.int32, (slots, 1), 0) >= TEXT + patches_ref[0]
    empty_term = jnp.where(empty, -1e30, 0.0)
    key_ref[...] = jnp.where(
        mine, k_ref[...].astype(jnp.float32), jnp.where(mask_lane, empty_term, 0.0)
    ).astype(jnp.bfloat16)
    value_ref[...] = jnp.where(mine, v_ref[...].astype(jnp.float32), 1.0).astype(jnp.bfloat16)
    coef0 = coef_ref[0, head]
    coef1 = coef_ref[1, head]
    lead = jnp.where(mask_lane, 1.0, 0.0)
    later = own > 0

    def rows_step(step):
        rows = tile_rows(step)
        query = jnp.where(
            mine, q_ref[rows, :].astype(jnp.float32) * HDIM ** (-0.5), lead
        ).astype(jnp.bfloat16)
        score = dot(query, key_ref[...], NT)
        score = score + coef0 * bucket0_ref[rows, :] + coef1 * bucket1_ref[rows, :]
        top = jnp.max(score, axis=1, keepdims=True)
        grown = jnp.exp(score - top).astype(jnp.bfloat16)
        grown_ref[0, rows, :] = grown
        both = dot(grown, value_ref[...], NN)
        inv = 1.0 / pltpu.roll(both, HDIM, 1)
        kept = jnp.where(later, att_ref[rows, :].astype(jnp.float32), 0.0)
        exact = both * inv
        att_ref[rows, :] = jnp.where(mine, exact, kept).astype(jnp.bfloat16)
        exact_ref[rows, :] = jnp.where(mine, exact, jnp.where(later, exact_ref[rows, :], 0.0))
        inv_ref[rows, :] = jnp.where(mine, inv, jnp.where(later, inv_ref[rows, :], 0.0))

    pl.loop(0, slots // TILE, unroll=4)(rows_step)


def attention_forward(tokens, weight_qkv, vectors, boxes, patches, box_coef):
    slots = tokens.shape[0]
    blocks = D // GW
    smem = pl.BlockSpec(memory_space=pltpu.SMEM)
    lane_block = pl.BlockSpec((slots, GW), lambda h: (0, h // GROUP))
    bias = pl.BlockSpec((1, GW), lambda h: (0, h // GROUP))
    wide = jax.ShapeDtypeStruct((slots, D), jnp.bfloat16)

    def weight(at):
        return pl.BlockSpec((GW, D), lambda h: (at * blocks + h // GROUP, 0))

    return pl.pallas_call(
        attention_forward_kernel,
        grid=(HEADS,),
        in_specs=[
            smem,
            smem,
            fixed((slots, D)),
            weight(0),
            weight(1),
            weight(2),
            bias,
            bias,
            fixed((2, slots)),
            fixed((slots, 2)),
        ],
        out_specs=[lane_block] * 3
        + [pl.BlockSpec((1, slots, slots), lambda h: (h, 0, 0)), lane_block, lane_block, lane_block],
        out_shape=[wide] * 3
        + [
            jax.ShapeDtypeStruct((HEADS, slots, slots), jnp.bfloat16),
            wide,
            jax.ShapeDtypeStruct((slots, D), jnp.float32),
            jax.ShapeDtypeStruct((slots, D), jnp.float32),
        ],
        scratch_shapes=[pltpu.VMEM((slots, slots), jnp.float32)] * 2
        + [pltpu.VMEM((slots, GW), jnp.bfloat16)] * 2,
        compiler_params=params(),
        cost_estimate=cost(10e9, 40e6),
        name="attention_forward",
    )(
        box_coef,
        patches,
        tokens,
        weight_qkv,
        weight_qkv,
        weight_qkv,
        vectors[2:3],
        vectors[3:4],
        boxes,
        boxes.T,
    )


def normalize(values):
    centered = values - jnp.mean(values, axis=-1, keepdims=True)
    inv_std = lax.rsqrt(jnp.mean(centered * centered, axis=-1, keepdims=True) + 1e-05)
    return (centered * inv_std, inv_std)


def normalize_back(grad_normed, normed, inv_std):
    first_mean = jnp.mean(grad_normed, axis=-1, keepdims=True)
    second_mean = jnp.mean(grad_normed * normed, axis=-1, keepdims=True)
    return inv_std * (grad_normed - first_mean - normed * second_mean)


def gelu_pair(values):
    half = values * (0.5**0.5)
    size = jnp.abs(half)
    fraction = 1.0 / (1.0 + 0.3275911 * size)
    series = fraction * (
        0.254829592
        + fraction
        * (
            -0.284496736
            + fraction * (1.421413741 + fraction * (-1.453152027 + fraction * 1.061405429))
        )
    )
    bell = jnp.exp(-half * half)
    tail = 0.5 * series * bell
    below = jnp.where(values >= 0, 1.0 - tail, tail)
    return (values * below, below + values * bell * (0.5 / math.pi) ** 0.5)


def feed_forward_kernel(
    att_ref,
    tokens_ref,
    wo_ref,
    wu_ref,
    wd_ref,
    wl_ref,
    wr_ref,
    vectors_ref,
    segments_ref,
    cot_pair_ref,
    mixed_ref,
    normed1_ref,
    inv1_ref,
    hidden_ref,
    act_ref,
    slope_ref,
    normed2_ref,
    inv2_ref,
    pair_ref,
    spread_ref,
    dleft_ref,
    dright_ref,
    pooled_ref,
    total_ref,
):
    step = pl.program_id(0)
    tile = att_ref.shape[0]
    branch = dot(att_ref[...], wo_ref[...], NT) + vectors_ref[4:5, :]
    normed1, inv1 = normalize(tokens_ref[...].astype(jnp.float32) + branch)
    hidden = normed1 * vectors_ref[0:1, :] + vectors_ref[1:2, :]
    low = hidden.astype(jnp.bfloat16)
    normed1_ref[...] = normed1
    inv1_ref[...] = inv1
    hidden_ref[...] = low
    feed = hidden + vectors_ref[7:8, :]
    for part in range(FF // D):
        cols = slice(part * D, (part + 1) * D)
        pre = dot(low, wu_ref[cols, :], NT) + vectors_ref[8 + part : 9 + part, :]
        act, slope = gelu_pair(pre)
        act = act.astype(jnp.bfloat16)
        act_ref[:, cols] = act
        slope_ref[:, cols] = slope.astype(jnp.bfloat16)
        feed = feed + dot(act, wd_ref[cols, :], NN)
    normed2, inv2 = normalize(feed)
    output = normed2 * vectors_ref[5:6, :] + vectors_ref[6:7, :]
    normed2_ref[...] = normed2
    inv2_ref[...] = inv2
    mixed_ref[...] = output.astype(jnp.bfloat16)

    @pl.when(step == 0)
    def _():
        total_ref[...] = jnp.zeros_like(total_ref)

    slot = step * tile + lax.broadcasted_iota(jnp.int32, (1, tile), 1)
    numbers = lax.broadcasted_iota(jnp.int32, (SEGS, 1), 0)

    @pl.when(step * tile < TEXT)
    def _():
        member = (segments_ref[:, pl.ds(pl.multiple_of(step * tile, tile), tile)] == numbers) & (slot < TEXT)
        total_ref[...] += split_dot(member.astype(jnp.bfloat16), output, NN)

    @pl.when(step == pl.num_programs(0) - 1)
    def _():
        member = (segments_ref[...] == numbers) & (
            lax.broadcasted_iota(jnp.int32, (1, segments_ref.shape[1]), 1) < TEXT
        )
        counted = jnp.sum(member.astype(jnp.float32), axis=1, keepdims=True)
        pooled = (total_ref[...] / counted).astype(jnp.bfloat16)
        scale = D ** (-0.5)
        left = dot(pooled, wl_ref[...], NT).astype(jnp.bfloat16)
        right = dot(pooled, wr_ref[...], NT).astype(jnp.bfloat16)
        pair_ref[...] = dot(left, right, NT) * scale
        cot = cot_pair_ref[...]
        grad_left = (split_dot_left(cot, right, NN) * scale).astype(jnp.bfloat16)
        grad_right = (split_dot_left(cot, left, TN) * scale).astype(jnp.bfloat16)
        grad_pooled = dot(grad_left, wl_ref[...], NN) + dot(grad_right, wr_ref[...], NN)
        spread_ref[...] = grad_pooled / counted
        dleft_ref[...] = grad_left
        dright_ref[...] = grad_right
        pooled_ref[...] = pooled


def split_dot_left(a, exact, dims):
    high = a.astype(jnp.bfloat16)
    rest = a - high.astype(jnp.float32)
    middle = rest.astype(jnp.bfloat16)
    last = (rest - middle.astype(jnp.float32)).astype(jnp.bfloat16)
    return dot(high, exact, dims) + dot(middle, exact, dims) + dot(last, exact, dims)


def feed_forward(att, tokens, weights, vectors, segments, cot_pair):
    slots = att.shape[0]
    tile = pl.BlockSpec((TILE, D), lambda i: (i, 0))
    wide = pl.BlockSpec((TILE, FF), lambda i: (i, 0))
    column = pl.BlockSpec((TILE, 1), lambda i: (i, 0))

    def weight(rows, at):
        return pl.BlockSpec((rows, D), lambda i: (at // rows, 0), pipeline_mode=pl.Buffered(1))

    def shape(dims, dtype=jnp.float32):
        return jax.ShapeDtypeStruct(dims, dtype)

    return pl.pallas_call(
        feed_forward_kernel,
        grid=(slots // TILE,),
        in_specs=[
            tile,
            tile,
            weight(D, 3 * D),
            pl.BlockSpec((pl.Element(FF), pl.Element(D)), lambda i: (4 * D, 0), pipeline_mode=pl.Buffered(1)),
            pl.BlockSpec((pl.Element(FF), pl.Element(D)), lambda i: (4 * D + FF, 0), pipeline_mode=pl.Buffered(1)),
            weight(D, 4 * D + 2 * FF),
            weight(D, 5 * D + 2 * FF),
            fixed(vectors.shape),
            fixed((1, 512)),
            fixed((SEGS, SEGS)),
        ],
        out_specs=[tile, tile, column, tile, wide, wide, tile, column, fixed((SEGS, SEGS))] + [fixed((SEGS, D))] * 4,
        out_shape=[
            shape((slots, D), jnp.bfloat16),
            shape((slots, D)),
            shape((slots, 1)),
            shape((slots, D), jnp.bfloat16),
            shape((slots, FF), jnp.bfloat16),
            shape((slots, FF), jnp.bfloat16),
            shape((slots, D)),
            shape((slots, 1)),
            shape((SEGS, SEGS)),
            shape((SEGS, D)),
            shape((SEGS, D), jnp.bfloat16),
            shape((SEGS, D), jnp.bfloat16),
            shape((SEGS, D), jnp.bfloat16),
        ],
        scratch_shapes=[pltpu.VMEM((SEGS, D), jnp.float32)],
        compiler_params=params(),
        cost_estimate=cost(11e9, 50e6),
        name="feed_forward",
    )(
        att,
        tokens,
        weights,
        weights,
        weights,
        weights,
        weights,
        vectors,
        jnp.pad(segments, ((0, 0), (0, 512 - segments.shape[1])), constant_values=SEGS),
        cot_pair,
    )


def store_halves(ref, values):
    ref[0] = values[:, : D // 2].astype(jnp.bfloat16)
    ref[1] = values[:, D // 2 :].astype(jnp.bfloat16)


def second_norm_kernel(
    patches_ref,
    cot_ref,
    segments_ref,
    spread_ref,
    normed2_ref,
    inv2_ref,
    vectors_ref,
    act_ref,
    slope_ref,
    wd_ref,
    wu_ref,
    hidden_ref,
    dleft_ref,
    dright_ref,
    pooled_ref,
    late_ref,
    sums_ref,
    dbu_ref,
    low_ref,
    total_ref,
):
    step = pl.program_id(0)
    slots = cot_ref.shape[0]

    @pl.when(step == 0)
    def _():
        sums_ref[...] = jnp.zeros_like(sums_ref)
        numbers = lax.broadcasted_iota(jnp.int32, (1, SEGS), 1)

        def rows_step(at):
            rows = tile_rows(at)
            slot = at * TILE + lax.broadcasted_iota(jnp.int32, (TILE, 1), 0)
            live = (slot < TEXT + patches_ref[0]).astype(jnp.float32)
            member = (segments_ref[rows, :] == numbers) & (slot < TEXT)
            grad = cot_ref[rows, :].astype(jnp.float32) * live
            grad = grad + split_dot(member.astype(jnp.bfloat16), spread_ref[...], NN)
            normed = normed2_ref[rows, :]
            sums_ref[5:6, :] += jnp.sum(grad * normed, axis=0, keepdims=True)
            sums_ref[6:7, :] += jnp.sum(grad, axis=0, keepdims=True)
            dres = normalize_back(grad * vectors_ref[5:6, :], normed, inv2_ref[rows, :])
            low = dres.astype(jnp.bfloat16)
            sums_ref[7:8, :] += jnp.sum(low.astype(jnp.float32), axis=0, keepdims=True)
            total_ref[rows, :] = dres
            low_ref[rows, :] = low

        pl.loop(0, slots // TILE)(rows_step)
        dact = dot(low_ref[...], wd_ref[...], NT)
        dpre = (dact * slope_ref[...].astype(jnp.float32)).astype(jnp.bfloat16)
        dbu_ref[...] = jnp.sum(dpre.astype(jnp.float32), axis=0, keepdims=True)
        store_halves(late_ref, dot(dpre, hidden_ref[...], TN))
        total_ref[...] += dot(dpre, wu_ref[...], NN)

    @pl.when((step > 0) & (step <= FF // D))
    def _():
        store_halves(late_ref, dot(act_ref[...], low_ref[...], TN))

    @pl.when(step == FF // D + 1)
    def _():
        store_halves(late_ref, dot(dleft_ref[...], pooled_ref[...], TN))

    @pl.when(step == FF // D + 2)
    def _():
        store_halves(late_ref, dot(dright_ref[...], pooled_ref[...], TN))


def feed_backward_kernel(
    low_ref,
    start_ref,
    normed1_ref,
    inv1_ref,
    hidden_ref,
    att_ref,
    inv_sum_ref,
    vectors_ref,
    slope_ref,
    wd_ref,
    wu_ref,
    wo_ref,
    early_ref,
    dbu_ref,
    sums_ref,
    dres_ref,
    datt_ref,
    grad_ref,
):
    step = pl.program_id(0)
    slots = low_ref.shape[0]
    last = pl.num_programs(0) - 1

    @pl.when(step == 0)
    def _():
        dres_ref[...] = start_ref[...]

    @pl.when(step < last)
    def _():
        dact = dot(low_ref[...], wd_ref[...], NT)
        dpre = (dact * slope_ref[...].astype(jnp.float32)).astype(jnp.bfloat16)
        dbu_ref[...] = jnp.sum(dpre.astype(jnp.float32), axis=0, keepdims=True)
        store_halves(early_ref, dot(dpre, hidden_ref[...], TN))
        dres_ref[...] += dot(dpre, wu_ref[...], NN)

    @pl.when(step == last)
    def _():
        sums_ref[...] = jnp.zeros_like(sums_ref)

        def rows_step(at):
            rows = tile_rows(at)
            grad = dres_ref[rows, :]
            normed = normed1_ref[rows, :]
            sums_ref[0:1, :] += jnp.sum(grad * normed, axis=0, keepdims=True)
            sums_ref[1:2, :] += jnp.sum(grad, axis=0, keepdims=True)
            dres = normalize_back(grad * vectors_ref[0:1, :], normed, inv1_ref[rows, :])
            low = dres.astype(jnp.bfloat16)
            sums_ref[4:5, :] += jnp.sum(low.astype(jnp.float32), axis=0, keepdims=True)
            dres_ref[rows, :] = dres
            grad_ref[rows, :] = low
            datt = dot(low, wo_ref[...], NN).astype(jnp.bfloat16).astype(jnp.float32)
            datt_ref[rows, :] = (datt * inv_sum_ref[rows, :]).astype(jnp.bfloat16)

        pl.loop(0, slots // TILE)(rows_step)
        store_halves(early_ref, dot(grad_ref[...], att_ref[...], TN))


def once(shape):
    return pl.BlockSpec(shape, lambda *_: (0,) * len(shape), pipeline_mode=pl.Buffered(1))


def shape_of(dims, dtype=jnp.float32):
    return jax.ShapeDtypeStruct(dims, dtype)


HALF_BLOCK = (2, D, D // 2)
HALF_ROWS = (3 * D + D + FF + FF + 2 * D) // 2


def second_norm(patches, cot_out, segments, spread, forward, pair_factors, vectors, weights):
    _, _, _, hidden, act, slope, normed2, inv2 = forward
    slots = cot_out.shape[0]
    parts = FF // D
    full = once((slots, D))
    column = once((slots, 1))
    tail = parts - 1
    return pl.pallas_call(
        second_norm_kernel,
        grid=(parts + 3,),
        in_specs=[
            pl.BlockSpec(memory_space=pltpu.SMEM),
            full,
            column,
            once((SEGS, D)),
            full,
            column,
            once(vectors.shape),
            pl.BlockSpec((slots, D), lambda i: (0, jnp.clip(i - 1, 0, parts - 1))),
            pl.BlockSpec((slots, D), lambda i: (0, tail), pipeline_mode=pl.Buffered(1)),
            pl.BlockSpec((D, D), lambda i: (4 + parts + tail, 0), pipeline_mode=pl.Buffered(1)),
            pl.BlockSpec((D, D), lambda i: (4 + tail, 0), pipeline_mode=pl.Buffered(1)),
            full,
            once((SEGS, D)),
            once((SEGS, D)),
            once((SEGS, D)),
        ],
        out_specs=[
            pl.BlockSpec(HALF_BLOCK, lambda i: (0, i, 0)),
            fixed((8, D)),
            fixed((1, D)),
            full,
            full,
        ],
        out_shape=[
            shape_of((2, HALF_ROWS, D // 2), jnp.bfloat16),
            shape_of((8, D)),
            shape_of((1, D)),
            shape_of((slots, D), jnp.bfloat16),
            shape_of((slots, D)),
        ],
        compiler_params=params(),
        cost_estimate=cost(10e9, 30e6),
        name="second_norm_backward",
    )(
        patches,
        cot_out,
        jnp.pad(segments, ((0, 0), (0, slots - segments.shape[1])), constant_values=SEGS).reshape(slots, 1),
        spread,
        normed2,
        inv2,
        vectors,
        act,
        slope,
        weights,
        weights,
        hidden,
        *pair_factors,
    )


def feed_backward(low, start, forward, att, inv_sum, vectors, weights):
    _, normed1, inv1, hidden, _, slope, _, _ = forward
    slots = low.shape[0]
    parts = FF // D
    last = parts - 1
    full = once((slots, D))

    def at(i):
        return jnp.minimum(i, last - 1)

    return pl.pallas_call(
        feed_backward_kernel,
        grid=(parts,),
        in_specs=[
            full,
            full,
            full,
            once((slots, 1)),
            full,
            full,
            full,
            once(vectors.shape),
            pl.BlockSpec((slots, D), lambda i: (0, at(i))),
            pl.BlockSpec((D, D), lambda i: (4 + parts + at(i), 0)),
            pl.BlockSpec((D, D), lambda i: (4 + at(i), 0)),
            pl.BlockSpec((D, D), lambda i: (3, 0), pipeline_mode=pl.Buffered(1)),
        ],
        out_specs=[
            pl.BlockSpec(HALF_BLOCK, lambda i: (0, jnp.where(i == last, 3, 4 + i), 0)),
            pl.BlockSpec((1, D), lambda i: (0, at(i))),
            fixed((8, D)),
            full,
            full,
        ],
        out_shape=[
            shape_of((2, HALF_ROWS, D // 2), jnp.bfloat16),
            shape_of((1, FF - D)),
            shape_of((8, D)),
            shape_of((slots, D)),
            shape_of((slots, D), jnp.bfloat16),
        ],
        scratch_shapes=[pltpu.VMEM((slots, D), jnp.bfloat16)],
        compiler_params=params(),
        cost_estimate=cost(17e9, 40e6),
        name="feed_backward",
    )(low, start, normed1, inv1, hidden, att, inv_sum, vectors, slope, weights, weights, weights)


def attention_backward_kernel(
    grown_ref,
    datt_ref,
    exact_ref,
    v_ref,
    k_ref,
    q_ref,
    box_row_ref,
    box_col_ref,
    dqkv_ref,
    dcoef_ref,
    bucket0_ref,
    bucket1_ref,
    value_ref,
    lead_ref,
    qt_ref,
    dt_ref,
    kt_ref,
    dscore_ref,
):
    head = pl.program_id(0)
    slots = datt_ref.shape[0]
    own = head % GROUP

    @pl.when(head == 0)
    def _():
        write_buckets(box_row_ref, box_col_ref, (bucket0_ref, bucket1_ref))

    @pl.when(own == 0)
    def _():
        scale = HDIM ** (-0.5)
        qt_ref[...] = (q_ref[...].astype(jnp.float32) * scale).T.astype(jnp.bfloat16)
        kt_ref[...] = (k_ref[...].astype(jnp.float32) * scale).T.astype(jnp.bfloat16)
        dt_ref[...] = datt_ref[...].astype(jnp.float32).T.astype(jnp.bfloat16)

    lanes = lax.broadcasted_iota(jnp.int32, (1, GW), 1)
    mine = lanes // HDIM == own
    at = (own * HDIM + HDIM) % GW
    value_ref[...] = jnp.where(
        mine,
        v_ref[...].astype(jnp.float32),
        jnp.where((lanes >= at) & (lanes < at + 3), -1.0, 0.0),
    ).astype(jnp.bfloat16)
    grad = datt_ref[...].astype(jnp.float32)
    delta = jnp.sum(
        jnp.where(mine, grad * exact_ref[...], 0.0), axis=1, keepdims=True
    )
    high = delta.astype(jnp.bfloat16).astype(jnp.float32)
    middle = (delta - high).astype(jnp.bfloat16).astype(jnp.float32)
    last = delta - high - middle
    terms = jnp.where(lanes == at, high, jnp.where(lanes == at + 1, middle, last))
    terms = jnp.where((lanes >= at) & (lanes < at + 3), terms, 0.0)
    lead_ref[...] = jnp.where(mine, grad, terms).astype(jnp.bfloat16)
    dcoef_ref[...] = jnp.zeros_like(dcoef_ref)

    def rows_step(step):
        rows = tile_rows(step)
        diff = dot(lead_ref[rows, :], value_ref[...], NT)
        dscore = grown_ref[0, rows, :].astype(jnp.float32) * diff
        dscore_ref[rows, :] = dscore.astype(jnp.bfloat16)
        dcoef_ref[0, 0:1, :] += jnp.sum(dscore * bucket0_ref[rows, :], axis=0, keepdims=True)
        dcoef_ref[0, 1:2, :] += jnp.sum(dscore * bucket1_ref[rows, :], axis=0, keepdims=True)

    pl.loop(0, slots // TILE, unroll=4)(rows_step)
    head_rows = pl.ds(pl.multiple_of(own * HDIM, HDIM), HDIM)
    dqkv_ref[0] = dot(kt_ref[head_rows, :], dscore_ref[...], NT).astype(jnp.bfloat16)
    dqkv_ref[1] = dot(qt_ref[head_rows, :], dscore_ref[...], NN).astype(jnp.bfloat16)
    dqkv_ref[2] = dot(dt_ref[head_rows, :], grown_ref[0], NN).astype(jnp.bfloat16)


def attention_backward(grown, datt, exact, q, k, v, boxes):
    slots = datt.shape[0]
    lane_block = pl.BlockSpec((slots, GW), lambda h: (0, h // GROUP))
    return pl.pallas_call(
        attention_backward_kernel,
        grid=(HEADS,),
        in_specs=[pl.BlockSpec((1, slots, slots), lambda h: (h, 0, 0))]
        + [lane_block] * 5
        + [fixed((2, slots)), fixed((slots, 2))],
        out_specs=[
            pl.BlockSpec((3, HDIM, slots), lambda h: (0, h, 0)),
            pl.BlockSpec((1, 2, slots), lambda h: (h, 0, 0)),
        ],
        out_shape=[
            jax.ShapeDtypeStruct((3, D, slots), jnp.bfloat16),
            jax.ShapeDtypeStruct((HEADS, 2, slots), jnp.float32),
        ],
        scratch_shapes=[pltpu.VMEM((slots, slots), jnp.float32)] * 2
        + [pltpu.VMEM((slots, GW), jnp.bfloat16)] * 2
        + [pltpu.VMEM((GW, slots), jnp.bfloat16)] * 3
        + [pltpu.VMEM((slots, slots), jnp.bfloat16)],
        compiler_params=params(),
        cost_estimate=cost(15e9, 40e6),
        name="attention_backward",
    )(grown, datt, exact, v, k, q, boxes, boxes.T)


def token_backward_kernel(
    dqkv_ref, weight_ref, tokens_ref, dres_ref, _, early_ref, sums_ref, grad_ref, total_ref
):
    step = pl.program_id(0)
    part = dqkv_ref[0]
    store_halves(early_ref, dot(part, tokens_ref[...], NN))
    sums_ref[0] = dot(jnp.ones((8, part.shape[1]), jnp.bfloat16), part, NT)
    term = dot(part, weight_ref[...], TN)

    @pl.when(step == 0)
    def _():
        total_ref[...] = dres_ref[...] + term

    @pl.when(step > 0)
    def _():
        total_ref[...] += term

    @pl.when(step == pl.num_programs(0) - 1)
    def _():
        grad_ref[...] = total_ref[...].astype(jnp.bfloat16)


def token_backward(dqkv, weights, tokens, dres, early):
    slots = tokens.shape[0]
    return pl.pallas_call(
        token_backward_kernel,
        grid=(3,),
        in_specs=[
            pl.BlockSpec((1, D, slots), lambda i: (i, 0, 0)),
            pl.BlockSpec((D, D), lambda i: (i, 0)),
            fixed((slots, D)),
            fixed((slots, D)),
            pl.BlockSpec(memory_space=pl.ANY),
        ],
        out_specs=[
            pl.BlockSpec(HALF_BLOCK, lambda i: (0, i, 0)),
            pl.BlockSpec((1, 8, D), lambda i: (i, 0, 0)),
            fixed((slots, D)),
        ],
        out_shape=[
            shape_of(early.shape, jnp.bfloat16),
            shape_of((3, 8, D)),
            shape_of((slots, D), jnp.bfloat16),
        ],
        scratch_shapes=[pltpu.VMEM((slots, D), jnp.float32)],
        input_output_aliases={4: 0},
        compiler_params=params(),
        cost_estimate=cost(7.3e9, 20e6),
        name="token_backward",
    )(dqkv, weights, tokens, dres, early)


def page_step(tokens, boxes, segments, patches, cot_out, cot_pair, gathered, vectors, box_coef):
    q, k, v, grown, att, inv_sum, exact = attention_forward(
        tokens, gathered, vectors, boxes, patches, box_coef
    )
    found = feed_forward(att, tokens, gathered, vectors, segments, cot_pair)
    mixed, pair_scores, spread = found[0], found[8], found[9]
    late, sums2, dbu_tail, low, start = second_norm(
        patches, cot_out, segments, spread, found[:8], found[10:], vectors, gathered
    )
    early, dbu_head, sums1, dres, datt = feed_backward(
        low, start, found[:8], att, inv_sum, vectors, gathered
    )
    dqkv, dcoef = attention_backward(grown, datt, exact, q, k, v, boxes)
    dqkv, late = lax.optimization_barrier((dqkv, scatter_dp(late)))
    early, bias_sums, token_grad = token_backward(dqkv, gathered, tokens, dres, early)
    vector_part = jnp.concatenate(
        [
            sums1[:2],
            bias_sums[0, :1],
            bias_sums[2, :1],
            sums1[4:5],
            sums2[5:8],
            dbu_head.reshape(FF // D - 1, D),
            dbu_tail,
        ],
        axis=0,
    )
    coef_part = jnp.sum(dcoef, axis=2).T
    return (mixed, pair_scores, token_grad, early, late, vector_part, coef_part)


def exchange_sum(values):
    for axis in ("dp", "grid"):
        size = lax.axis_size(axis)
        reach = 1
        while reach < size:
            values = values + lax.ppermute(values, axis, [(i, i ^ reach) for i in range(size)])
            reach *= 2
    return values


def scatter_dp(halves):
    return lax.psum_scatter(
        halves.reshape(-1, D // 2), "dp", scatter_dimension=0, tiled=True
    )


def scatter_grid(rows):
    size = lax.axis_size("grid")
    place = lax.axis_index("grid")
    blocks = rows.reshape(size, -1, D // 2)

    def block(at):
        return lax.dynamic_index_in_dim(blocks, at % size, 0, keepdims=False)

    got = [
        lax.ppermute(block(place + s), "grid", [(i, (i + s) % size) for i in range(size)])
        for s in range(1, size)
    ]
    return sum((g.astype(jnp.float32) for g in got), block(place).astype(jnp.float32))


def swap_halves(first, second):
    size = lax.axis_size("dp")
    low = lax.axis_index("dp") < size // 2
    other = lax.ppermute(
        jnp.where(low, second, first).astype(jnp.bfloat16), "dp", [(i, (i + size // 2) % size) for i in range(size)]
    ).astype(jnp.float32)
    kept = jnp.where(low, first, second)
    return jnp.concatenate([jnp.where(low, kept, other), jnp.where(low, other, kept)], axis=1)


def momentum_step(grad, param, moment, average, rate):
    new_moment = 0.5 * moment + grad
    new_param = param - rate * (grad + 0.5 * new_moment)
    new_average = 0.5 * average + 0.5 * new_param
    return (new_moment, new_param, new_average)


def on_device(
    tokens,
    boxes,
    segments,
    patches,
    cot_out,
    cot_pair,
    weights,
    weight_momentum,
    weight_average,
    vectors,
    vector_momentum,
    vector_average,
    box_coef,
    coef_momentum,
    coef_average,
):
    axes = ("dp", "grid")
    page_count, slot_count = tokens.shape[:2]
    device_count = lax.axis_size(axes)
    gathered = lax.all_gather(weights.astype(jnp.bfloat16), axes, axis=0, tiled=True)
    pages = [
        page_step(
            tokens[p], boxes[p], segments[p : p + 1], patches[p : p + 1], cot_out[p], cot_pair[p], gathered, vectors, box_coef
        )
        for p in range(page_count)
    ]
    mixed, pair_scores, token_grad = (jnp.stack([page[i] for page in pages]) for i in range(3))
    early, late = (sum(page[i] for page in pages) for i in (3, 4))
    small = sum(
        jnp.concatenate([page[5], jnp.pad(page[6].reshape(1, 2 * HEADS), ((0, 3), (0, D - 2 * HEADS)))], axis=0)
        for page in pages
    )
    late_rows = scatter_grid(late)
    early_rows = scatter_grid(scatter_dp(early))
    small = exchange_sum(small)
    weight_grad = swap_halves(early_rows, late_rows)
    vector_rows = vectors.shape[0]
    vector_grad = small[:vector_rows]
    coef_grad = small[vector_rows, : 2 * HEADS].reshape(2, HEADS)
    rate_scale = (device_count * page_count * slot_count) ** (-0.5)
    new_weight_momentum, new_weights, new_weight_average = momentum_step(
        weight_grad, weights, weight_momentum, weight_average, 0.1 * rate_scale
    )
    new_vector_momentum, new_vectors, new_vector_average = momentum_step(
        vector_grad, vectors, vector_momentum, vector_average, 0.1 * rate_scale
    )
    new_coef_momentum, new_coef, new_coef_average = momentum_step(
        coef_grad, box_coef, coef_momentum, coef_average, 0.01 * rate_scale
    )
    return (
        mixed,
        pair_scores,
        token_grad,
        weight_grad,
        new_weights,
        new_weight_momentum,
        new_weight_average,
        new_weights.astype(jnp.bfloat16),
        vector_grad,
        new_vectors,
        new_vector_momentum,
        new_vector_average,
        coef_grad,
        new_coef,
        new_coef_momentum,
        new_coef_average,
    )


def solution(mesh):
    rows = P(("dp", "grid"))
    return jax.shard_map(
        on_device,
        mesh=mesh,
        in_specs=(rows,) * 9 + (P(),) * 6,
        out_specs=(rows,) * 8 + (P(),) * 8,
        check_vma=False,
    )
```

```python
import math

import jax
import jax.numpy as jnp
from jax import lax
from jax.experimental import pallas as pl
from jax.experimental.pallas import tpu as pltpu
from jax.sharding import PartitionSpec as P

D = 768
HEADS = 12
HDIM = 64
FF = 3072
TEXT = 448
SEGS = 64
PAIR = 2 * HDIM
GW = 2 * PAIR
LOG2E = math.log2(math.e)
TILE = 256
WIDE = 512
VMEM_LIMIT = 60 * 1024 * 1024
NT = (((1,), (1,)), ((), ()))
NN = (((1,), (0,)), ((), ()))
TN = (((0,), (0,)), ((), ()))

def dot(a, b, dims):
    return lax.dot_general(a, b, dims, preferred_element_type=jnp.float32)


def split_dot(exact, b, dims):
    high = b.astype(jnp.bfloat16)
    rest = b - high.astype(jnp.float32)
    middle = rest.astype(jnp.bfloat16)
    last = (rest - middle.astype(jnp.float32)).astype(jnp.bfloat16)
    return dot(exact, high, dims) + dot(exact, middle, dims) + dot(exact, last, dims)


def params():
    return pltpu.CompilerParams(vmem_limit_bytes=VMEM_LIMIT)


def cost(flops, nbytes):
    return pl.CostEstimate(flops=int(flops), bytes_accessed=int(nbytes), transcendentals=0)


def tile_rows(step):
    return pl.ds(pl.multiple_of(step * TILE, TILE), TILE)


def wide_rows(step):
    return pl.ds(pl.multiple_of(step * WIDE, WIDE), WIDE)


def fixed(shape):
    return pl.BlockSpec(shape, lambda *_: (0,) * len(shape))


def once(shape):
    return pl.BlockSpec(shape, lambda *_: (0,) * len(shape), pipeline_mode=pl.Buffered(1))


def shape_of(dims, dtype=jnp.float32):
    return jax.ShapeDtypeStruct(dims, dtype)


HALF_BLOCK = (2, D, D // 2)
HALF_ROWS = (3 * D + D + FF + FF + 2 * D) // 2


def square(at):
    return pl.BlockSpec((D, D), lambda i: (at, 0), pipeline_mode=pl.Buffered(1))


def write_buckets(box_row_ref, box_col_ref, bucket_refs, live_row=None):
    def fill(step):
        rows = tile_rows(step)
        for c in range(2):
            spread = jnp.abs(box_col_ref[rows, c : c + 1] - box_row_ref[c : c + 1, :])
            bucket = jnp.minimum(spread >> 5, 31).astype(jnp.float32)
            bucket_refs[c][rows, :] = bucket if live_row is None else jnp.where(live_row, bucket, 0.0)

    pl.loop(0, box_row_ref.shape[1] // TILE)(fill)


def attention_forward_kernel(
    coef_ref,
    patches_ref,
    tokens_ref,
    wq_ref,
    wk_ref,
    wv_ref,
    vectors_ref,
    box_row_ref,
    box_col_ref,
    q_ref,
    k_ref,
    v_ref,
    grown_ref,
    att_ref,
    inv_ref,
    exact_ref,
    bucket0_ref,
    bucket1_ref,
    live_ref,
    value_ref,
    size_ref,
):
    pair = pl.program_id(0)
    slots = tokens_ref.shape[0]
    side = pl.ds(pl.multiple_of(pair % 2 * PAIR, PAIR), PAIR)
    low = jnp.bfloat16

    @pl.when(pair == 0)
    def _():
        write_buckets(box_row_ref, box_col_ref, (bucket0_ref, bucket1_ref))
        slot = lax.broadcasted_iota(jnp.int32, (slots, PAIR), 0)
        live_ref[...] = (slot < TEXT + patches_ref[0]).astype(jnp.float32).astype(low)

    @pl.when(pair % 2 == 0)
    def _():
        query = (dot(tokens_ref[...], wq_ref[...], NT) + vectors_ref[2:3, :]) * (
            LOG2E * HDIM ** (-0.5)
        )
        key = dot(tokens_ref[...], wk_ref[...], NT)
        q_ref[...] = query.astype(low)
        k_ref[...] = key.astype(low)
        v_ref[...] = (dot(tokens_ref[...], wv_ref[...], NT) + vectors_ref[3:4, :]).astype(low)
        of_head = lax.broadcasted_iota(jnp.int32, (GW, PAIR), 0) // HDIM
        ones = (of_head == lax.broadcasted_iota(jnp.int32, (GW, PAIR), 1)).astype(low)
        query_size = jnp.max(dot((query * query).astype(low), ones, NN), axis=0, keepdims=True)
        key_size = jnp.max(dot((key * key).astype(low), ones, NN), axis=0, keepdims=True)
        size_ref[0] = jnp.max(query_size * key_size)

    second = lax.broadcasted_iota(jnp.int32, (1, PAIR), 1) >= HDIM
    masks = [jnp.where(second, 0.0, 1.0), jnp.where(second, 1.0, 0.0)]
    masks = [mask.astype(low) for mask in masks]
    value = v_ref[:, side] * live_ref[...]
    for j in range(2):
        value_ref[j] = value * masks[j] + live_ref[...] * masks[1 - j]
    coefs = [[coef_ref[c, 2 * pair + j] * LOG2E for c in range(2)] for j in range(2)]
    spread = [31.0 * (jnp.abs(c[0]) + jnp.abs(c[1])) for c in coefs]
    room = 57.0 - jnp.maximum(spread[0], spread[1])
    small = (room > 0) & (1.03 * size_ref[0] <= room * room)

    def rows_step(step, shifted):
        rows = tile_rows(step)
        query = q_ref[rows, side]
        bucket0 = bucket0_ref[rows, :]
        bucket1 = bucket1_ref[rows, :]
        found = []
        for j in range(2):
            score = dot(query * masks[j], k_ref[:, side], NT)
            score = score + coefs[j][0] * bucket0 + coefs[j][1] * bucket1
            if shifted:
                slot = lax.broadcasted_iota(jnp.int32, (1, slots), 1)
                score = jnp.where(slot < TEXT + patches_ref[0], score, -1e30)
                score = score - jnp.max(score, axis=1, keepdims=True)
            grown = jnp.exp2(score).astype(low)
            grown_ref[j, rows, :] = grown
            found.append(dot(grown, value_ref[j], NN))
        total = jnp.where(second, found[0], found[1])
        inv = 1.0 / pltpu.roll(total, HDIM, 1)
        exact = jnp.where(second, found[1], found[0]) * inv
        exact_ref[rows, :] = exact
        att_ref[rows, :] = exact.astype(low)
        inv_ref[rows, :] = inv

    @pl.when(small)
    def _():
        pl.loop(0, slots // TILE, unroll=4)(lambda step: rows_step(step, False))

    @pl.when(jnp.logical_not(small))
    def _():
        pl.loop(0, slots // TILE)(lambda step: rows_step(step, True))


def attention_forward(tokens, weights, vectors, boxes, boxes_t, patches, box_coef):
    slots = tokens.shape[0]
    blocks = D // GW
    smem = pl.BlockSpec(memory_space=pltpu.SMEM)
    lane_block = pl.BlockSpec((slots, GW), lambda h: (0, h // 2))
    pair_block = pl.BlockSpec((slots, PAIR), lambda h: (0, h))
    low = shape_of((slots, D), jnp.bfloat16)
    wide = shape_of((slots, D))

    def weight(at):
        return pl.BlockSpec((GW, D), lambda h: (at * blocks + h // 2, 0))

    return pl.pallas_call(
        attention_forward_kernel,
        grid=(HEADS // 2,),
        in_specs=[
            smem,
            smem,
            fixed((slots, D)),
            weight(0),
            weight(1),
            weight(2),
            pl.BlockSpec((vectors.shape[0], GW), lambda h: (0, h // 2)),
            fixed((2, slots)),
            fixed((slots, 2)),
        ],
        out_specs=[lane_block] * 3
        + [pl.BlockSpec((2, slots, slots), lambda h: (h, 0, 0))]
        + [pair_block] * 3,
        out_shape=[low] * 3 + [shape_of((HEADS, slots, slots), jnp.bfloat16), low, wide, wide],
        scratch_shapes=[pltpu.VMEM((slots, slots), jnp.float32)] * 2
        + [
            pltpu.VMEM((slots, PAIR), jnp.bfloat16),
            pltpu.VMEM((2, slots, PAIR), jnp.bfloat16),
            pltpu.SMEM((1,), jnp.float32),
        ],
        compiler_params=params(),
        cost_estimate=cost(10e9, 40e6),
        name="attention_forward",
    )(
        box_coef,
        patches,
        tokens,
        weights,
        weights,
        weights,
        vectors,
        boxes,
        boxes_t,
    )


def normalize(values):
    centered = values - jnp.mean(values, axis=-1, keepdims=True)
    inv_std = lax.rsqrt(jnp.mean(centered * centered, axis=-1, keepdims=True) + 1e-05)
    return (centered * inv_std, inv_std)


def normalize_back(grad_normed, normed, inv_std):
    first_mean = jnp.mean(grad_normed, axis=-1, keepdims=True)
    second_mean = jnp.mean(grad_normed * normed, axis=-1, keepdims=True)
    return inv_std * (grad_normed - first_mean - normed * second_mean)


def gelu_pair(values):
    below = 0.5 + 0.5 * lax.erf(values * (0.5**0.5))
    bell = jnp.exp(values * values * -0.5) * (0.5 / math.pi) ** 0.5
    return (values * below, below + values * bell)


def split_dot_left(a, exact, dims):
    high = a.astype(jnp.bfloat16)
    rest = a - high.astype(jnp.float32)
    middle = rest.astype(jnp.bfloat16)
    last = (rest - middle.astype(jnp.float32)).astype(jnp.bfloat16)
    return dot(high, exact, dims) + dot(middle, exact, dims) + dot(last, exact, dims)


def store_halves(ref, values):
    ref[0] = values[:, : D // 2].astype(jnp.bfloat16)
    ref[1] = values[:, D // 2 :].astype(jnp.bfloat16)


PARTS = FF // D
NORM_STEP = PARTS + 1
TAIL_STEP = PARTS + 2
PAIR_STEP = TAIL_STEP + PARTS + 1


def middle_kernel(
    patches_ref,
    att_ref,
    tokens_ref,
    wo_ref,
    wu_ref,
    wd_ref,
    wl_ref,
    wr_ref,
    vectors_ref,
    segment_row_ref,
    segment_col_ref,
    cot_pair_ref,
    cot_ref,
    slope_ref,
    late_ref,
    pair_ref,
    sums_ref,
    dbu_ref,
    inv1_ref,
    mixed_out,
    normed1_out,
    hidden_out,
    low_out,
    dres_out,
    act_ref,
    tail_ref,
    mixed_ref,
    normed1_ref,
    hidden_ref,
    low_ref,
    total_ref,
    normed2_ref,
    inv2_ref,
    pool_ref,
    pooled_ref,
    dpair_ref,
    sems,
):
    step = pl.program_id(0)
    slots = att_ref.shape[0]
    tiles = slots // TILE
    outs = (
        (normed1_ref, normed1_out),
        (hidden_ref, hidden_out),
        (mixed_ref, mixed_out),
        (low_ref, low_out),
        (total_ref, dres_out),
    )
    sends = [pltpu.make_async_copy(src, dst, sems.at[i]) for i, (src, dst) in enumerate(outs)]

    @pl.when(step == 0)
    def _():

        @pl.loop(0, tiles)
        def _(at):
            rows = tile_rows(at)
            branch = dot(att_ref[rows, :], wo_ref[...], NT) + vectors_ref[4:5, :]
            normed, inv = normalize(tokens_ref[rows, :].astype(jnp.float32) + branch)
            hidden = normed * vectors_ref[0:1, :] + vectors_ref[1:2, :]
            normed1_ref[rows, :] = normed
            inv1_ref[rows, :] = inv
            hidden_ref[rows, :] = hidden.astype(jnp.bfloat16)
            total_ref[rows, :] = hidden + vectors_ref[7:8, :]

        sends[0].start()
        sends[1].start()

    @pl.when((step > 0) & (step <= PARTS))
    def _():
        bias = vectors_ref[pl.ds(7 + step, 1), :]

        for at in range(tiles):
            rows = slice(at * TILE, (at + 1) * TILE)
            act, slope = gelu_pair(dot(hidden_ref[rows, :], wu_ref[...], NT) + bias)
            act = act.astype(jnp.bfloat16)
            act_ref[step - 1, rows, :] = act
            slope_ref[rows, :] = slope.astype(jnp.bfloat16)
            total_ref[rows, :] += dot(act, wd_ref[...], NN)

    @pl.when(step == NORM_STEP)
    def _():
        numbers = lax.broadcasted_iota(jnp.int32, (SEGS, 1), 0)
        slot_row = lax.broadcasted_iota(jnp.int32, (1, slots), 1)
        member = (segment_row_ref[...] == numbers) & (slot_row < TEXT)
        counted = jnp.sum(member.astype(jnp.float32), axis=1, keepdims=True)
        pool_ref[...] = jnp.zeros_like(pool_ref)

        @pl.loop(0, tiles)
        def _(at):
            rows = tile_rows(at)
            normed, inv = normalize(total_ref[rows, :])
            inv2_ref[rows, :] = inv
            output = normed * vectors_ref[5:6, :] + vectors_ref[6:7, :]
            normed2_ref[rows, :] = normed
            mixed_ref[rows, :] = output.astype(jnp.bfloat16)

            @pl.when(at * TILE < TEXT)
            def _():
                slot = at * TILE + lax.broadcasted_iota(jnp.int32, (1, TILE), 1)
                belongs = (segment_row_ref[:, rows] == numbers) & (slot < TEXT)
                pool_ref[...] += split_dot(belongs.astype(jnp.bfloat16), output, NN)

        sends[2].start()
        pooled = (pool_ref[...] / counted).astype(jnp.bfloat16)
        left_weight = wl_ref[...]
        right_weight = wr_ref[...]
        scale = D ** (-0.5)
        left = dot(pooled, left_weight, NT).astype(jnp.bfloat16)
        right = dot(pooled, right_weight, NT).astype(jnp.bfloat16)
        pair_ref[...] = dot(left, right, NT) * scale
        cot = cot_pair_ref[...]
        grad_left = (split_dot_left(cot, right, NN) * scale).astype(jnp.bfloat16)
        grad_right = (split_dot_left(cot, left, TN) * scale).astype(jnp.bfloat16)
        grad_pooled = dot(grad_left, left_weight, NN) + dot(grad_right, right_weight, NN)
        spread = grad_pooled / counted
        pooled_ref[...] = pooled
        dpair_ref[0] = grad_left
        dpair_ref[1] = grad_right
        columns = lax.broadcasted_iota(jnp.int32, (1, SEGS), 1)
        pool_ref[...] = spread
        sums_ref[...] = jnp.zeros_like(sums_ref)

        @pl.loop(0, tiles)
        def _(at):
            rows = tile_rows(at)
            slot = at * TILE + lax.broadcasted_iota(jnp.int32, (TILE, 1), 0)
            live = (slot < TEXT + patches_ref[0]).astype(jnp.float32)
            belongs = (segment_col_ref[rows, :] == columns) & (slot < TEXT)
            grad = cot_ref[rows, :].astype(jnp.float32) * live
            grad = grad + split_dot(belongs.astype(jnp.bfloat16), pool_ref[...], NN)
            normed = normed2_ref[rows, :]
            sums_ref[0:1, :] += jnp.sum(grad * normed, axis=0, keepdims=True)
            sums_ref[1:2, :] += jnp.sum(grad, axis=0, keepdims=True)
            dres = normalize_back(grad * vectors_ref[5:6, :], normed, inv2_ref[rows, :])
            low = dres.astype(jnp.bfloat16)
            sums_ref[2:3, :] += jnp.sum(low.astype(jnp.float32), axis=0, keepdims=True)
            total_ref[rows, :] = dres
            low_ref[rows, :] = low

        sends[3].start()

    @pl.when(step == TAIL_STEP)
    def _():
        dbu_ref[...] = jnp.zeros_like(dbu_ref)

        @pl.loop(0, slots // WIDE)
        def _(at):
            rows = wide_rows(at)
            dact = dot(low_ref[rows, :], wd_ref[...], NT)
            dpre = (dact * slope_ref[rows, :].astype(jnp.float32)).astype(jnp.bfloat16)
            dbu_ref[...] += jnp.sum(dpre.astype(jnp.float32), axis=0, keepdims=True)
            tail_ref[rows, :] = dpre
            total_ref[rows, :] += dot(dpre, wu_ref[...], NN)

        sends[4].start()
        store_halves(late_ref, dot(tail_ref[...], hidden_ref[...], TN))

    @pl.when((step > TAIL_STEP) & (step < PAIR_STEP))
    def _():
        store_halves(late_ref, dot(act_ref[step - TAIL_STEP - 1], low_ref[...], TN))

    @pl.when(step >= PAIR_STEP)
    def _():
        store_halves(late_ref, dot(dpair_ref[step - PAIR_STEP], pooled_ref[...], TN))

    @pl.when(step == PAIR_STEP + 1)
    def _():
        for send in sends:
            send.wait()


def middle(att, tokens, weights, vectors, segments, segments_t, cot_pair, cot_out, patches):
    slots = att.shape[0]
    full = once((slots, D))
    anywhere = pl.BlockSpec(memory_space=pl.ANY)
    low = jnp.bfloat16

    def part(step):
        return jnp.clip(step - 1, 0, PARTS - 1)

    def half_row(step):
        return jnp.clip(step - TAIL_STEP, 0, PARTS + 2)

    return pl.pallas_call(
        middle_kernel,
        grid=(PAIR_STEP + 2,),
        in_specs=[
            pl.BlockSpec(memory_space=pltpu.SMEM),
            full,
            full,
            square(3),
            pl.BlockSpec((D, D), lambda i: (4 + part(i), 0)),
            pl.BlockSpec((D, D), lambda i: (4 + PARTS + part(i), 0)),
            square(4 + 2 * PARTS),
            square(5 + 2 * PARTS),
            once(vectors.shape),
            once((1, slots)),
            once((slots, 1)),
            once((SEGS, SEGS)),
            full,
        ],
        out_specs=[
            pl.BlockSpec((slots, D), lambda i: (0, part(i))),
            pl.BlockSpec(HALF_BLOCK, lambda i: (0, half_row(i), 0)),
            fixed((SEGS, SEGS)),
            fixed((8, D)),
            fixed((1, D)),
            fixed((slots, 1)),
        ]
        + [anywhere] * 5,
        out_shape=[
            shape_of((slots, FF), low),
            shape_of((2, HALF_ROWS, D // 2), low),
            shape_of((SEGS, SEGS)),
            shape_of((8, D)),
            shape_of((1, D)),
            shape_of((slots, 1)),
            shape_of((slots, D), low),
            shape_of((slots, D)),
            shape_of((slots, D), low),
            shape_of((slots, D), low),
            shape_of((slots, D)),
        ],
        scratch_shapes=[
            pltpu.VMEM((PARTS, slots, D), low),
            pltpu.VMEM((slots, D), low),
            pltpu.VMEM((slots, D), low),
            pltpu.VMEM((slots, D), jnp.float32),
            pltpu.VMEM((slots, D), low),
            pltpu.VMEM((slots, D), low),
            pltpu.VMEM((slots, D), jnp.float32),
            pltpu.VMEM((slots, D), jnp.float32),
            pltpu.VMEM((slots, 1), jnp.float32),
            pltpu.VMEM((SEGS, D), jnp.float32),
            pltpu.VMEM((SEGS, D), low),
            pltpu.VMEM((2, SEGS, D), low),
            pltpu.SemaphoreType.DMA((5,)),
        ],
        compiler_params=params(),
        cost_estimate=cost(20e9, 40e6),
        name="middle",
    )(
        patches,
        att,
        tokens,
        *[weights] * 5,
        vectors,
        segments,
        segments_t,
        cot_pair,
        cot_out,
    )


def head_sums(values):
    rows = lax.broadcasted_iota(jnp.int32, (GW, GW), 0)
    cols = lax.broadcasted_iota(jnp.int32, (GW, GW), 1)
    takes = (rows // PAIR == cols // PAIR) & (rows // HDIM != cols // HDIM)
    takes = takes.astype(jnp.float32).astype(jnp.bfloat16)
    sums = jnp.concatenate(
        [split_dot_left(values[:, at : at + GW], takes, NN) for at in range(0, D, GW)], axis=1
    )
    high = sums.astype(jnp.bfloat16).astype(jnp.float32)
    middle = (sums - high).astype(jnp.bfloat16).astype(jnp.float32)
    place = lax.broadcasted_iota(jnp.int32, (1, D), 1) % HDIM
    terms = jnp.where(place == 0, high, jnp.where(place == 1, middle, sums - high - middle))
    return jnp.where(place < 3, terms, 0.0).astype(jnp.bfloat16)


def feed_backward_kernel(
    low_ref,
    hidden_ref,
    inv1_ref,
    vectors_ref,
    slope_ref,
    wd_ref,
    wu_ref,
    wo_ref,
    start_in,
    normed1_in,
    att_in,
    inv_sum_in,
    exact_in,
    early_ref,
    dbu_ref,
    sums_ref,
    dres_out,
    datt_out,
    terms_out,
    total_ref,
    normed1_ref,
    att_ref,
    inv_sum_ref,
    exact_ref,
    grad_ref,
    datt_ref,
    terms_ref,
    sems,
):
    step = pl.program_id(0)
    slots = low_ref.shape[0]
    last = pl.num_programs(0) - 1
    loads = [
        pltpu.make_async_copy(src, dst, sems.at[i])
        for i, (src, dst) in enumerate(
            (
                (start_in, total_ref),
                (normed1_in, normed1_ref),
                (att_in, att_ref),
                (inv_sum_in, inv_sum_ref),
                (exact_in, exact_ref),
            )
        )
    ]

    @pl.when(step == 0)
    def _():
        for load in loads:
            load.start()

    @pl.when(step < last)
    def _():
        dact = dot(low_ref[...], wd_ref[...], NT)
        dpre = (dact * slope_ref[...].astype(jnp.float32)).astype(jnp.bfloat16)
        dbu_ref[...] = jnp.sum(dpre.astype(jnp.float32), axis=0, keepdims=True)
        store_halves(early_ref, dot(dpre, hidden_ref[...], TN))
        pl.when(step == 0)(loads[0].wait)
        total_ref[...] += dot(dpre, wu_ref[...], NN)

    @pl.when(step == last)
    def _():
        sums_ref[...] = jnp.zeros_like(sums_ref)
        for load in loads[1:]:
            load.wait()

        def rows_step(at):
            rows = tile_rows(at)
            grad = total_ref[rows, :]
            normed = normed1_ref[rows, :]
            sums_ref[0:1, :] += jnp.sum(grad * normed, axis=0, keepdims=True)
            sums_ref[1:2, :] += jnp.sum(grad, axis=0, keepdims=True)
            dres = normalize_back(grad * vectors_ref[0:1, :], normed, inv1_ref[rows, :])
            low = dres.astype(jnp.bfloat16)
            sums_ref[4:5, :] += jnp.sum(low.astype(jnp.float32), axis=0, keepdims=True)
            total_ref[rows, :] = dres
            grad_ref[rows, :] = low
            datt = dot(low, wo_ref[...], NN).astype(jnp.bfloat16).astype(jnp.float32)
            datt = (datt * inv_sum_ref[rows, :]).astype(jnp.bfloat16)
            datt_ref[rows, :] = datt
            terms_ref[rows, :] = head_sums(datt.astype(jnp.float32) * exact_ref[rows, :])

        pl.loop(0, slots // TILE)(rows_step)
        sends = [
            pltpu.make_async_copy(src, dst, sems.at[5 + i])
            for i, (src, dst) in enumerate(
                ((total_ref, dres_out), (datt_ref, datt_out), (terms_ref, terms_out))
            )
        ]
        for send in sends:
            send.start()
        store_halves(early_ref, dot(grad_ref[...], att_ref[...], TN))
        for send in sends:
            send.wait()


def feed_backward(low, start, normed1, inv1, hidden, slope, att, inv_sum, exact, vectors, weights):
    slots = low.shape[0]
    last = PARTS - 1
    full = once((slots, D))
    anywhere = pl.BlockSpec(memory_space=pl.ANY)

    def at(i):
        return jnp.minimum(i, last - 1)

    return pl.pallas_call(
        feed_backward_kernel,
        grid=(PARTS,),
        in_specs=[
            full,
            full,
            once((slots, 1)),
            once(vectors.shape),
            pl.BlockSpec((slots, D), lambda i: (0, at(i))),
            pl.BlockSpec((D, D), lambda i: (4 + PARTS + at(i), 0)),
            pl.BlockSpec((D, D), lambda i: (4 + at(i), 0)),
            square(3),
        ]
        + [anywhere] * 5,
        out_specs=[
            pl.BlockSpec(HALF_BLOCK, lambda i: (0, jnp.where(i == last, 3, 4 + i), 0)),
            pl.BlockSpec((1, D), lambda i: (0, at(i))),
            fixed((8, D)),
        ]
        + [anywhere] * 3,
        out_shape=[
            shape_of((2, HALF_ROWS, D // 2), jnp.bfloat16),
            shape_of((1, FF - D)),
            shape_of((8, D)),
            shape_of((slots, D)),
            shape_of((slots, D), jnp.bfloat16),
            shape_of((slots, D), jnp.bfloat16),
        ],
        scratch_shapes=[
            pltpu.VMEM((slots, D), jnp.float32),
            pltpu.VMEM((slots, D), jnp.float32),
            pltpu.VMEM((slots, D), jnp.bfloat16),
            pltpu.VMEM((slots, D), jnp.float32),
            pltpu.VMEM((slots, D), jnp.float32),
            pltpu.VMEM((slots, D), jnp.bfloat16),
            pltpu.VMEM((slots, D), jnp.bfloat16),
            pltpu.VMEM((slots, D), jnp.bfloat16),
            pltpu.SemaphoreType.DMA((8,)),
        ],
        compiler_params=params(),
        cost_estimate=cost(17e9, 40e6),
        name="feed_backward",
    )(low, hidden, inv1, vectors, slope, weights, weights, weights, start, normed1, att, inv_sum, exact)


def attention_backward_kernel(
    patches_ref,
    grown_ref,
    datt_ref,
    terms_ref,
    v_ref,
    k_ref,
    q_ref,
    box_row_ref,
    box_col_ref,
    dqkv_ref,
    dcoef_ref,
    bucket0_ref,
    bucket1_ref,
    dscore_ref,
):
    pair = pl.program_id(0)
    slots = datt_ref.shape[0]
    low = jnp.bfloat16
    live_row = lax.broadcasted_iota(jnp.int32, (1, slots), 1) < TEXT + patches_ref[0]

    @pl.when(pair == 0)
    def _():
        write_buckets(box_row_ref, box_col_ref, (bucket0_ref, bucket1_ref), live_row)

    query_t = q_ref[...].astype(jnp.float32).T.astype(low)
    key_t = (k_ref[...].astype(jnp.float32) * HDIM ** (-0.5)).T
    key_t = jnp.where(live_row, key_t, 0.0).astype(low)
    datt_t = datt_ref[...].astype(jnp.float32).T.astype(low)
    lanes = lax.broadcasted_iota(jnp.int32, (1, PAIR), 1)
    second = lanes >= HDIM
    masks = [jnp.where(second, 0.0, 1.0), jnp.where(second, 1.0, 0.0)]
    masks = [mask.astype(low) for mask in masks]
    dcoef_ref[...] = jnp.zeros_like(dcoef_ref)
    leads = []
    values = []
    for j in range(2):
        at = HDIM * (1 - j)
        minus = jnp.where((lanes >= at) & (lanes < at + 3), -1.0, 0.0).astype(low)
        leads.append(datt_ref[...] * masks[j] + terms_ref[...] * masks[1 - j])
        values.append(v_ref[...] * masks[j] + minus)

    for j in range(2):
        head_rows = slice(j * HDIM, (j + 1) * HDIM)
        for step in range(slots // TILE):
            rows = slice(step * TILE, (step + 1) * TILE)
            diff = dot(leads[j][rows], values[j], NT)
            dscore = grown_ref[j, rows, :].astype(jnp.float32) * diff
            dscore_ref[j, rows, :] = dscore.astype(low)
            dcoef_ref[j, 0:1, :] += jnp.sum(dscore * bucket0_ref[rows, :], axis=0, keepdims=True)
            dcoef_ref[j, 1:2, :] += jnp.sum(dscore * bucket1_ref[rows, :], axis=0, keepdims=True)
        dqkv_ref[0, head_rows] = dot(key_t[head_rows], dscore_ref[j], NT).astype(low)
        dkey = dot(query_t[head_rows], dscore_ref[j], NN) * (1.0 / LOG2E)
        dqkv_ref[1, head_rows] = jnp.where(live_row, dkey, 0.0).astype(low)
        dvalue = dot(datt_t[head_rows], grown_ref[j], NN)
        dqkv_ref[2, head_rows] = jnp.where(live_row, dvalue, 0.0).astype(low)


def attention_backward(grown, datt, terms, q, k, v, boxes, boxes_t, patches):
    slots = datt.shape[0]
    pair_block = pl.BlockSpec((slots, PAIR), lambda h: (0, h))
    return pl.pallas_call(
        attention_backward_kernel,
        grid=(HEADS // 2,),
        in_specs=[
            pl.BlockSpec(memory_space=pltpu.SMEM),
            pl.BlockSpec((2, slots, slots), lambda h: (h, 0, 0)),
        ]
        + [pair_block] * 5
        + [fixed((2, slots)), fixed((slots, 2))],
        out_specs=[
            pl.BlockSpec((3, PAIR, slots), lambda h: (0, h, 0)),
            pl.BlockSpec((2, 2, slots), lambda h: (h, 0, 0)),
        ],
        out_shape=[
            shape_of((3, D, slots), jnp.bfloat16),
            shape_of((HEADS, 2, slots)),
        ],
        scratch_shapes=[pltpu.VMEM((slots, slots), jnp.float32)] * 2
        + [pltpu.VMEM((2, slots, slots), jnp.bfloat16)],
        compiler_params=params(),
        cost_estimate=cost(15e9, 40e6),
        name="attention_backward",
    )(patches, grown, datt, terms, v, k, q, boxes, boxes_t)


def qkv_weights_kernel(dqkv_ref, tokens_ref, _, early_ref, sums_ref):
    part = dqkv_ref[0]
    store_halves(early_ref, dot(part, tokens_ref[...], NN))
    sums_ref[0] = dot(jnp.ones((8, part.shape[1]), jnp.bfloat16), part, NT)


def qkv_weights(dqkv, tokens, early):
    slots = tokens.shape[0]
    return pl.pallas_call(
        qkv_weights_kernel,
        grid=(3,),
        in_specs=[
            pl.BlockSpec((1, D, slots), lambda i: (i, 0, 0)),
            fixed((slots, D)),
            pl.BlockSpec(memory_space=pl.ANY),
        ],
        out_specs=[
            pl.BlockSpec(HALF_BLOCK, lambda i: (0, i, 0)),
            pl.BlockSpec((1, 8, D), lambda i: (i, 0, 0)),
        ],
        out_shape=[shape_of(early.shape, jnp.bfloat16), shape_of((3, 8, D))],
        input_output_aliases={2: 0},
        compiler_params=params(),
        cost_estimate=cost(3.6e9, 10e6),
        name="qkv_weights",
    )(dqkv, tokens, early)


def token_gradient_kernel(dqkv_ref, weight_ref, dres_ref, grad_ref):
    total = dres_ref[...]
    for part in range(3):
        total = total + dot(dqkv_ref[part], weight_ref[part * D : (part + 1) * D, :], TN)
    grad_ref[...] = total.astype(jnp.bfloat16)


def token_gradient(dqkv, weights, dres):
    slots = dres.shape[0]
    tile = pl.BlockSpec((TILE, D), lambda i: (i, 0))
    return pl.pallas_call(
        token_gradient_kernel,
        grid=(slots // TILE,),
        in_specs=[
            pl.BlockSpec((3, D, TILE), lambda i: (0, 0, i)),
            pl.BlockSpec((3 * D, D), lambda i: (0, 0), pipeline_mode=pl.Buffered(1)),
            tile,
        ],
        out_specs=tile,
        out_shape=shape_of((slots, D), jnp.bfloat16),
        compiler_params=params(),
        cost_estimate=cost(3.6e9, 12e6),
        name="token_gradient",
    )(dqkv, weights, dres)


def page_step(
    tokens, boxes, boxes_t, segments, segments_t, patches, cot_out, cot_pair, weights, vectors, box_coef
):
    q, k, v, grown, att, inv_sum, exact = attention_forward(
        tokens, weights, vectors, boxes, boxes_t, patches, box_coef
    )
    slope, late, pair_scores, sums2, dbu_tail, inv1, mixed, normed1, hidden, low, start = middle(
        att, tokens, weights, vectors, segments, segments_t, cot_pair, cot_out, patches
    )
    early, dbu_head, sums1, dres, datt, terms = feed_backward(
        low, start, normed1, inv1, hidden, slope, att, inv_sum, exact, vectors, weights
    )
    dqkv, dcoef = attention_backward(grown, datt, terms, q, k, v, boxes, boxes_t, patches)
    early, bias_sums = qkv_weights(dqkv, tokens, early)
    early, late = lax.optimization_barrier((early, scatter_dp(late)))
    early = scatter_dp(early)
    token_grad = token_gradient(dqkv, weights, dres)
    vector_part = jnp.concatenate(
        [
            sums1[:2],
            bias_sums[0, :1],
            bias_sums[2, :1],
            sums1[4:5],
            sums2[:3],
            dbu_head.reshape(FF // D - 1, D),
            dbu_tail,
        ],
        axis=0,
    )
    coef_part = jnp.sum(dcoef, axis=2).T
    return (mixed, pair_scores, token_grad, early, late, vector_part, coef_part)


def exchange_sum(values):
    for axis in ("dp", "grid"):
        size = lax.axis_size(axis)
        reach = 1
        while reach < size:
            values = values + lax.ppermute(values, axis, [(i, i ^ reach) for i in range(size)])
            reach *= 2
    return values


def scatter_dp(halves):
    return lax.psum_scatter(
        halves.reshape(-1, D // 2), "dp", scatter_dimension=0, tiled=True
    )


def scatter_grid(rows):
    size = lax.axis_size("grid")
    place = lax.axis_index("grid")
    blocks = rows.reshape(size, -1, D // 2)

    def block(at):
        return lax.dynamic_index_in_dim(blocks, at % size, 0, keepdims=False)

    got = [
        lax.ppermute(block(place + s), "grid", [(i, (i + s) % size) for i in range(size)])
        for s in range(1, size)
    ]
    return sum((g.astype(jnp.float32) for g in got), block(place).astype(jnp.float32))


def swap_halves(first, second):
    size = lax.axis_size("dp")
    low = lax.axis_index("dp") < size // 2
    other = lax.ppermute(
        jnp.where(low, second, first).astype(jnp.bfloat16), "dp", [(i, (i + size // 2) % size) for i in range(size)]
    ).astype(jnp.float32)
    kept = jnp.where(low, first, second)
    return jnp.concatenate([jnp.where(low, kept, other), jnp.where(low, other, kept)], axis=1)


def momentum_step(grad, param, moment, average, rate):
    new_moment = 0.5 * moment + grad
    new_param = param - rate * (grad + 0.5 * new_moment)
    new_average = 0.5 * average + 0.5 * new_param
    return (new_moment, new_param, new_average)


def on_device(
    tokens,
    boxes,
    segments,
    patches,
    cot_out,
    cot_pair,
    weights,
    weight_momentum,
    weight_average,
    vectors,
    vector_momentum,
    vector_average,
    box_coef,
    coef_momentum,
    coef_average,
):
    axes = ("dp", "grid")
    page_count, slot_count = tokens.shape[:2]
    device_count = lax.axis_size(axes)
    gathered = lax.all_gather(weights.astype(jnp.bfloat16), axes, axis=0, tiled=True)
    boxes_t = boxes.transpose(0, 2, 1)
    segments = jnp.pad(segments, ((0, 0), (0, slot_count - segments.shape[1])), constant_values=SEGS)
    segments_t = segments.reshape(page_count, slot_count, 1)
    pages = [
        page_step(
            tokens[p],
            boxes[p],
            boxes_t[p],
            segments[p : p + 1],
            segments_t[p],
            patches[p : p + 1],
            cot_out[p],
            cot_pair[p],
            gathered,
            vectors,
            box_coef,
        )
        for p in range(page_count)
    ]
    mixed, pair_scores, token_grad = (jnp.stack([page[i] for page in pages]) for i in range(3))
    early, late = (sum(page[i] for page in pages) for i in (3, 4))
    small = sum(
        jnp.concatenate([page[5], jnp.pad(page[6].reshape(1, 2 * HEADS), ((0, 3), (0, D - 2 * HEADS)))], axis=0)
        for page in pages
    )
    late_rows = scatter_grid(late)
    early_rows = scatter_grid(early)
    small = exchange_sum(small)
    weight_grad = swap_halves(early_rows, late_rows)
    vector_rows = vectors.shape[0]
    vector_grad = small[:vector_rows]
    coef_grad = small[vector_rows, : 2 * HEADS].reshape(2, HEADS)
    rate_scale = (device_count * page_count * slot_count) ** (-0.5)
    new_weight_momentum, new_weights, new_weight_average = momentum_step(
        weight_grad, weights, weight_momentum, weight_average, 0.1 * rate_scale
    )
    new_vector_momentum, new_vectors, new_vector_average = momentum_step(
        vector_grad, vectors, vector_momentum, vector_average, 0.1 * rate_scale
    )
    new_coef_momentum, new_coef, new_coef_average = momentum_step(
        coef_grad, box_coef, coef_momentum, coef_average, 0.01 * rate_scale
    )
    return (
        mixed,
        pair_scores,
        token_grad,
        weight_grad,
        new_weights,
        new_weight_momentum,
        new_weight_average,
        new_weights.astype(jnp.bfloat16),
        vector_grad,
        new_vectors,
        new_vector_momentum,
        new_vector_average,
        coef_grad,
        new_coef,
        new_coef_momentum,
        new_coef_average,
    )


def solution(mesh):
    rows = P(("dp", "grid"))
    return jax.shard_map(
        on_device,
        mesh=mesh,
        in_specs=(rows,) * 9 + (P(),) * 6,
        out_specs=(rows,) * 8 + (P(),) * 8,
        check_vma=False,
    )
```

```python
import functools
import math

import jax
import jax.numpy as jnp
from jax import lax
from jax.experimental import pallas as pl
from jax.experimental.pallas import tpu as pltpu
from jax.sharding import PartitionSpec as P

D = 768
HEADS = 12
HDIM = 64
FF = 3072
TEXT = 448
SEGS = 64
PAIR = 2 * HDIM
GW = 2 * PAIR
LOG2E = math.log2(math.e)
TILE = 256
WIDE = 512
VMEM_LIMIT = 60 * 1024 * 1024
NT = (((1,), (1,)), ((), ()))
NN = (((1,), (0,)), ((), ()))
TN = (((0,), (0,)), ((), ()))

def dot(a, b, dims):
    return lax.dot_general(a, b, dims, preferred_element_type=jnp.float32)


def split_dot(exact, b, dims):
    high = b.astype(jnp.bfloat16)
    rest = b - high.astype(jnp.float32)
    middle = rest.astype(jnp.bfloat16)
    last = (rest - middle.astype(jnp.float32)).astype(jnp.bfloat16)
    return dot(exact, high, dims) + dot(exact, middle, dims) + dot(exact, last, dims)


def params():
    return pltpu.CompilerParams(vmem_limit_bytes=VMEM_LIMIT)


def cost(flops, nbytes):
    return pl.CostEstimate(flops=int(flops), bytes_accessed=int(nbytes), transcendentals=0)


def tile_rows(step):
    return pl.ds(pl.multiple_of(step * TILE, TILE), TILE)


def wide_rows(step):
    return pl.ds(pl.multiple_of(step * WIDE, WIDE), WIDE)


def fixed(shape):
    return pl.BlockSpec(shape, lambda *_: (0,) * len(shape))


def once(shape):
    return pl.BlockSpec(shape, lambda *_: (0,) * len(shape), pipeline_mode=pl.Buffered(1))


def shape_of(dims, dtype=jnp.float32):
    return jax.ShapeDtypeStruct(dims, dtype)


HALF_BLOCK = (2, D, D // 2)
HALF_ROWS = (3 * D + D + FF + FF + 2 * D) // 2


def square(at):
    return pl.BlockSpec((D, D), lambda i: (at, 0), pipeline_mode=pl.Buffered(1))


def write_buckets(box_row_ref, box_col_ref, bucket_refs, live_row=None):
    box_col_ref[...] = jnp.tile(box_row_ref[...].astype(jnp.float32), (4, 1)).T.astype(jnp.int32)

    def fill(step):
        rows = tile_rows(step)
        for c in range(2):
            spread = jnp.abs(box_col_ref[rows, c : c + 1] - box_row_ref[c : c + 1, :])
            bucket = jnp.minimum(spread >> 5, 31).astype(jnp.float32)
            bucket_refs[c][rows, :] = bucket if live_row is None else jnp.where(live_row, bucket, 0.0)

    pl.loop(0, box_row_ref.shape[1] // TILE)(fill)


def place_weights(layout, piece_refs, weight_ref, out_ref, sems, meanwhile):
    step = pl.program_id(0)
    place = lax.axis_index("grid")
    mine = lax.axis_index("dp")
    depth = lax.axis_size("grid")
    shard = weight_ref.shape[0] // (lax.axis_size("dp") * depth)
    by_owner = {}
    count = 0
    for ref, (start, entries) in zip(piece_refs, layout):
        rows = ref.shape[1]
        if entries is None:
            every = [(owner, "far") for owner in range(ref.shape[0])]
        else:
            every = [
                ((mine ^ over) * depth + lax.rem(place + depth - back, depth), over)
                for over, back in entries
            ]
        for at, (owner, over) in enumerate(every):
            if over == "far" and owner * shard < 3 * D:
                over = "near"
            target = weight_ref.at[pl.ds(pl.multiple_of(owner * shard + start, 16), rows)]
            by_owner.setdefault(over, []).append(pltpu.make_async_copy(ref.at[at], target, sems.at[count]))
            count += 1
    out = pltpu.make_async_copy(weight_ref, out_ref, sems.at[count])
    needed = -(-3 * D // (shard * depth))

    def each(first, action):
        for over, copies in by_owner.items():
            if over in ("near", "far"):
                if first == (over == "near"):
                    for copy in copies:
                        action(copy)
                continue
            chosen = (mine ^ over) < needed

            @pl.when(chosen if first else jnp.logical_not(chosen))
            def _():
                for copy in copies:
                    action(copy)

    @pl.when(step == 0)
    def _():
        each(True, lambda copy: copy.start())
        meanwhile()
        each(True, lambda copy: copy.wait())
        each(False, lambda copy: copy.start())

    @pl.when(step == 1)
    def _():
        each(False, lambda copy: copy.wait())
        out.start()

    @pl.when(step == pl.num_programs(0) - 1)
    def _():
        out.wait()


def attention_forward_kernel(
    layout,
    pieces,
    coef_ref,
    patches_ref,
    tokens_ref,
    vectors_ref,
    box_row_ref,
    *refs,
):
    piece_refs, refs = refs[:pieces], refs[pieces:]
    q_ref, k_ref, v_ref, grown_ref, att_ref, inv_ref, exact_ref = refs[:7]
    box_col_ref, bucket0_ref, bucket1_ref, live_ref, value_ref, size_ref, weight_ref, sems = refs[-8:]
    pair = pl.program_id(0)
    slots = tokens_ref.shape[0]
    side = pl.ds(pl.multiple_of(pair % 2 * PAIR, PAIR), PAIR)
    low = jnp.bfloat16

    def prepare():
        write_buckets(box_row_ref, box_col_ref, (bucket0_ref, bucket1_ref))
        slot = lax.broadcasted_iota(jnp.int32, (slots, PAIR), 0)
        live_ref[...] = (slot < TEXT + patches_ref[0]).astype(jnp.float32).astype(low)

    if layout is None:

        @pl.when(pair == 0)
        def _():
            load = pltpu.make_async_copy(piece_refs[0].at[pl.ds(0, 3 * D)], weight_ref, sems.at[0])
            load.start()
            prepare()
            load.wait()

    else:
        place_weights(layout, piece_refs, weight_ref, refs[7], sems, prepare)

    @pl.when(pair % 2 == 0)
    def _():
        def weight(at):
            return weight_ref[pl.ds(pl.multiple_of(at * D + pair // 2 * GW, GW), GW), :]

        query = (dot(tokens_ref[...], weight(0), NT) + vectors_ref[2:3, :]) * (
            LOG2E * HDIM ** (-0.5)
        )
        key = dot(tokens_ref[...], weight(1), NT)
        q_ref[...] = query.astype(low)
        k_ref[...] = key.astype(low)
        v_ref[...] = (dot(tokens_ref[...], weight(2), NT) + vectors_ref[3:4, :]).astype(low)
        of_head = lax.broadcasted_iota(jnp.int32, (GW, PAIR), 0) // HDIM
        ones = (of_head == lax.broadcasted_iota(jnp.int32, (GW, PAIR), 1)).astype(low)
        query_size = jnp.max(dot((query * query).astype(low), ones, NN), axis=0, keepdims=True)
        key_size = jnp.max(dot((key * key).astype(low), ones, NN), axis=0, keepdims=True)
        size_ref[0] = jnp.max(query_size * key_size)

    second = lax.broadcasted_iota(jnp.int32, (1, PAIR), 1) >= HDIM
    masks = [jnp.where(second, 0.0, 1.0), jnp.where(second, 1.0, 0.0)]
    masks = [mask.astype(low) for mask in masks]
    value = v_ref[:, side] * live_ref[...]
    for j in range(2):
        value_ref[j] = value * masks[j] + live_ref[...] * masks[1 - j]
    coefs = [[coef_ref[c, 2 * pair + j] * LOG2E for c in range(2)] for j in range(2)]
    spread = [31.0 * (jnp.abs(c[0]) + jnp.abs(c[1])) for c in coefs]
    room = 57.0 - jnp.maximum(spread[0], spread[1])
    small = (room > 0) & (1.03 * size_ref[0] <= room * room)

    def rows_step(step, shifted):
        rows = tile_rows(step)
        query = q_ref[rows, side]
        bucket0 = bucket0_ref[rows, :]
        bucket1 = bucket1_ref[rows, :]
        found = []
        for j in range(2):
            score = dot(query * masks[j], k_ref[:, side], NT)
            score = score + coefs[j][0] * bucket0 + coefs[j][1] * bucket1
            if shifted:
                slot = lax.broadcasted_iota(jnp.int32, (1, slots), 1)
                score = jnp.where(slot < TEXT + patches_ref[0], score, -1e30)
                score = score - jnp.max(score, axis=1, keepdims=True)
            grown = jnp.exp2(score).astype(low)
            grown_ref[j, rows, :] = grown
            found.append(dot(grown, value_ref[j], NN))
        total = jnp.where(second, found[0], found[1])
        inv = 1.0 / pltpu.roll(total, HDIM, 1)
        exact = jnp.where(second, found[1], found[0]) * inv
        exact_ref[rows, :] = exact
        att_ref[rows, :] = exact.astype(low)
        inv_ref[rows, :] = inv

    @pl.when(small)
    def _():
        pl.loop(0, slots // TILE, unroll=4)(lambda step: rows_step(step, False))

    @pl.when(jnp.logical_not(small))
    def _():
        pl.loop(0, slots // TILE)(lambda step: rows_step(step, True))


def attention_forward(tokens, pieces, layout, vectors, boxes, patches, box_coef):
    slots = tokens.shape[0]
    smem = pl.BlockSpec(memory_space=pltpu.SMEM)
    anywhere = pl.BlockSpec(memory_space=pl.ANY)
    lane_block = pl.BlockSpec((slots, GW), lambda h: (0, h // 2))
    pair_block = pl.BlockSpec((slots, PAIR), lambda h: (0, h))
    low = shape_of((slots, D), jnp.bfloat16)
    wide = shape_of((slots, D))
    weights = shape_of((2 * HALF_ROWS, D), jnp.bfloat16)
    copies = 0 if layout is None else sum(
        piece.shape[0] if entries is None else len(entries) for piece, (_, entries) in zip(pieces, layout)
    )
    out = pl.pallas_call(
        functools.partial(attention_forward_kernel, layout, len(pieces)),
        grid=(HEADS // 2,),
        in_specs=[
            smem,
            smem,
            fixed((slots, D)),
            pl.BlockSpec((vectors.shape[0], GW), lambda h: (0, h // 2)),
            fixed((2, slots)),
        ]
        + [anywhere] * len(pieces),
        out_specs=[lane_block] * 3
        + [pl.BlockSpec((2, slots, slots), lambda h: (h, 0, 0))]
        + [pair_block] * 3
        + [anywhere] * bool(copies),
        out_shape=[low] * 3
        + [shape_of((HEADS, slots, slots), jnp.bfloat16), low, wide, wide]
        + [weights] * bool(copies),
        scratch_shapes=[pltpu.VMEM((slots, 8), jnp.int32)]
        + [pltpu.VMEM((slots, slots), jnp.float32)] * 2
        + [
            pltpu.VMEM((slots, PAIR), jnp.bfloat16),
            pltpu.VMEM((2, slots, PAIR), jnp.bfloat16),
            pltpu.SMEM((1,), jnp.float32),
            pltpu.VMEM(weights.shape if copies else (3 * D, D), jnp.bfloat16),
            pltpu.SemaphoreType.DMA((copies + 1,)),
        ],
        compiler_params=params(),
        cost_estimate=cost(10e9, 40e6),
        name="attention_forward",
    )(box_coef, patches, tokens, vectors, boxes, *pieces)
    return out[:7], out[7] if copies else pieces[0]


def normalize(values):
    centered = values - jnp.mean(values, axis=-1, keepdims=True)
    inv_std = lax.rsqrt(jnp.mean(centered * centered, axis=-1, keepdims=True) + 1e-05)
    return (centered * inv_std, inv_std)


def normalize_back(grad_normed, normed, inv_std):
    first_mean = jnp.mean(grad_normed, axis=-1, keepdims=True)
    second_mean = jnp.mean(grad_normed * normed, axis=-1, keepdims=True)
    return inv_std * (grad_normed - first_mean - normed * second_mean)


def gelu_pair(values):
    below = 0.5 + 0.5 * lax.erf(values * (0.5**0.5))
    bell = jnp.exp(values * values * -0.5) * (0.5 / math.pi) ** 0.5
    return (values * below, below + values * bell)


def split_dot_left(a, exact, dims):
    high = a.astype(jnp.bfloat16)
    rest = a - high.astype(jnp.float32)
    middle = rest.astype(jnp.bfloat16)
    last = (rest - middle.astype(jnp.float32)).astype(jnp.bfloat16)
    return dot(high, exact, dims) + dot(middle, exact, dims) + dot(last, exact, dims)


def store_halves(ref, values):
    ref[0] = values[:, : D // 2].astype(jnp.bfloat16)
    ref[1] = values[:, D // 2 :].astype(jnp.bfloat16)


PARTS = FF // D
NORM_STEP = PARTS + 1
TAIL_STEP = PARTS + 2
PAIR_STEP = TAIL_STEP + PARTS + 1


def middle_kernel(
    patches_ref,
    att_ref,
    tokens_ref,
    wo_ref,
    wu_ref,
    wd_ref,
    wl_ref,
    wr_ref,
    vectors_ref,
    segment_row_ref,
    cot_pair_ref,
    cot_ref,
    slope_ref,
    late_ref,
    pair_ref,
    sums_ref,
    dbu_ref,
    inv1_ref,
    mixed_out,
    normed1_out,
    hidden_out,
    low_out,
    dres_out,
    act_ref,
    tail_ref,
    mixed_ref,
    normed1_ref,
    hidden_ref,
    low_ref,
    total_ref,
    normed2_ref,
    inv2_ref,
    pool_ref,
    pooled_ref,
    dpair_ref,
    sems,
):
    step = pl.program_id(0)
    slots = att_ref.shape[0]
    tiles = slots // TILE
    outs = (
        (normed1_ref, normed1_out),
        (hidden_ref, hidden_out),
        (mixed_ref, mixed_out),
        (low_ref, low_out),
        (total_ref, dres_out),
    )
    sends = [pltpu.make_async_copy(src, dst, sems.at[i]) for i, (src, dst) in enumerate(outs)]

    @pl.when(step == 0)
    def _():

        @pl.loop(0, tiles)
        def _(at):
            rows = tile_rows(at)
            branch = dot(att_ref[rows, :], wo_ref[...], NT) + vectors_ref[4:5, :]
            normed, inv = normalize(tokens_ref[rows, :].astype(jnp.float32) + branch)
            hidden = normed * vectors_ref[0:1, :] + vectors_ref[1:2, :]
            normed1_ref[rows, :] = normed
            inv1_ref[rows, :] = inv
            hidden_ref[rows, :] = hidden.astype(jnp.bfloat16)
            total_ref[rows, :] = hidden + vectors_ref[7:8, :]

        sends[0].start()
        sends[1].start()

    @pl.when((step > 0) & (step <= PARTS))
    def _():
        bias = vectors_ref[pl.ds(7 + step, 1), :]

        for at in range(tiles):
            rows = slice(at * TILE, (at + 1) * TILE)
            act, slope = gelu_pair(dot(hidden_ref[rows, :], wu_ref[...], NT) + bias)
            act = act.astype(jnp.bfloat16)
            act_ref[step - 1, rows, :] = act
            slope_ref[rows, :] = slope.astype(jnp.bfloat16)
            total_ref[rows, :] += dot(act, wd_ref[...], NN)

    @pl.when(step == NORM_STEP)
    def _():
        numbers = lax.broadcasted_iota(jnp.int32, (SEGS, 1), 0)
        slot_row = lax.broadcasted_iota(jnp.int32, (1, slots), 1)
        member = (segment_row_ref[...] == numbers) & (slot_row < TEXT)
        counted = jnp.sum(member.astype(jnp.float32), axis=1, keepdims=True)
        pool_ref[...] = jnp.zeros_like(pool_ref)

        @pl.loop(0, tiles)
        def _(at):
            rows = tile_rows(at)
            normed, inv = normalize(total_ref[rows, :])
            inv2_ref[rows, :] = inv
            output = normed * vectors_ref[5:6, :] + vectors_ref[6:7, :]
            normed2_ref[rows, :] = normed
            mixed_ref[rows, :] = output.astype(jnp.bfloat16)

            @pl.when(at * TILE < TEXT)
            def _():
                slot = at * TILE + lax.broadcasted_iota(jnp.int32, (1, TILE), 1)
                belongs = (segment_row_ref[:, rows] == numbers) & (slot < TEXT)
                pool_ref[...] += split_dot(belongs.astype(jnp.bfloat16), output, NN)

        sends[2].start()
        pooled = (pool_ref[...] / counted).astype(jnp.bfloat16)
        left_weight = wl_ref[...]
        right_weight = wr_ref[...]
        scale = D ** (-0.5)
        left = dot(pooled, left_weight, NT).astype(jnp.bfloat16)
        right = dot(pooled, right_weight, NT).astype(jnp.bfloat16)
        pair_ref[...] = dot(left, right, NT) * scale
        cot = cot_pair_ref[...]
        grad_left = (split_dot_left(cot, right, NN) * scale).astype(jnp.bfloat16)
        grad_right = (split_dot_left(cot, left, TN) * scale).astype(jnp.bfloat16)
        grad_pooled = dot(grad_left, left_weight, NN) + dot(grad_right, right_weight, NN)
        spread = grad_pooled / counted
        pooled_ref[...] = pooled
        dpair_ref[0] = grad_left
        dpair_ref[1] = grad_right
        pool_ref[...] = spread
        sums_ref[...] = jnp.zeros_like(sums_ref)

        @pl.loop(0, tiles)
        def _(at):
            rows = tile_rows(at)
            slot = at * TILE + lax.broadcasted_iota(jnp.int32, (TILE, 1), 0)
            live = (slot < TEXT + patches_ref[0]).astype(jnp.float32)
            slot_of = at * TILE + lax.broadcasted_iota(jnp.int32, (1, TILE), 1)
            belongs = (segment_row_ref[:, rows] == numbers) & (slot_of < TEXT)
            grad = cot_ref[rows, :].astype(jnp.float32) * live
            grad = grad + split_dot(belongs.astype(jnp.bfloat16), pool_ref[...], TN)
            normed = normed2_ref[rows, :]
            sums_ref[0:1, :] += jnp.sum(grad * normed, axis=0, keepdims=True)
            sums_ref[1:2, :] += jnp.sum(grad, axis=0, keepdims=True)
            dres = normalize_back(grad * vectors_ref[5:6, :], normed, inv2_ref[rows, :])
            low = dres.astype(jnp.bfloat16)
            sums_ref[2:3, :] += jnp.sum(low.astype(jnp.float32), axis=0, keepdims=True)
            total_ref[rows, :] = dres
            low_ref[rows, :] = low

        sends[3].start()

    @pl.when(step == TAIL_STEP)
    def _():
        dbu_ref[...] = jnp.zeros_like(dbu_ref)

        @pl.loop(0, slots // WIDE)
        def _(at):
            rows = wide_rows(at)
            dact = dot(low_ref[rows, :], wd_ref[...], NT)
            dpre = (dact * slope_ref[rows, :].astype(jnp.float32)).astype(jnp.bfloat16)
            dbu_ref[...] += jnp.sum(dpre.astype(jnp.float32), axis=0, keepdims=True)
            tail_ref[rows, :] = dpre
            total_ref[rows, :] += dot(dpre, wu_ref[...], NN)

        sends[4].start()
        store_halves(late_ref, dot(tail_ref[...], hidden_ref[...], TN))

    @pl.when((step > TAIL_STEP) & (step < PAIR_STEP))
    def _():
        store_halves(late_ref, dot(act_ref[step - TAIL_STEP - 1], low_ref[...], TN))

    @pl.when(step >= PAIR_STEP)
    def _():
        store_halves(late_ref, dot(dpair_ref[step - PAIR_STEP], pooled_ref[...], TN))

    @pl.when(step == PAIR_STEP + 1)
    def _():
        for send in sends:
            send.wait()


def middle(att, tokens, weights, vectors, segments, cot_pair, cot_out, patches):
    slots = att.shape[0]
    full = once((slots, D))
    anywhere = pl.BlockSpec(memory_space=pl.ANY)
    low = jnp.bfloat16

    def part(step):
        return jnp.clip(step - 1, 0, PARTS - 1)

    def half_row(step):
        return jnp.clip(step - TAIL_STEP, 0, PARTS + 2)

    return pl.pallas_call(
        middle_kernel,
        grid=(PAIR_STEP + 2,),
        in_specs=[
            pl.BlockSpec(memory_space=pltpu.SMEM),
            full,
            full,
            square(3),
            pl.BlockSpec((D, D), lambda i: (4 + part(i), 0)),
            pl.BlockSpec((D, D), lambda i: (4 + PARTS + part(i), 0)),
            square(4 + 2 * PARTS),
            square(5 + 2 * PARTS),
            once(vectors.shape),
            once((1, slots)),
            once((SEGS, SEGS)),
            full,
        ],
        out_specs=[
            pl.BlockSpec((slots, D), lambda i: (0, part(i))),
            pl.BlockSpec(HALF_BLOCK, lambda i: (0, half_row(i), 0)),
            fixed((SEGS, SEGS)),
            fixed((8, D)),
            fixed((1, D)),
            fixed((slots, 1)),
        ]
        + [anywhere] * 5,
        out_shape=[
            shape_of((slots, FF), low),
            shape_of((2, HALF_ROWS, D // 2), low),
            shape_of((SEGS, SEGS)),
            shape_of((8, D)),
            shape_of((1, D)),
            shape_of((slots, 1)),
            shape_of((slots, D), low),
            shape_of((slots, D)),
            shape_of((slots, D), low),
            shape_of((slots, D), low),
            shape_of((slots, D)),
        ],
        scratch_shapes=[
            pltpu.VMEM((PARTS, slots, D), low),
            pltpu.VMEM((slots, D), low),
            pltpu.VMEM((slots, D), low),
            pltpu.VMEM((slots, D), jnp.float32),
            pltpu.VMEM((slots, D), low),
            pltpu.VMEM((slots, D), low),
            pltpu.VMEM((slots, D), jnp.float32),
            pltpu.VMEM((slots, D), jnp.float32),
            pltpu.VMEM((slots, 1), jnp.float32),
            pltpu.VMEM((SEGS, D), jnp.float32),
            pltpu.VMEM((SEGS, D), low),
            pltpu.VMEM((2, SEGS, D), low),
            pltpu.SemaphoreType.DMA((5,)),
        ],
        compiler_params=params(),
        cost_estimate=cost(20e9, 40e6),
        name="middle",
    )(
        patches,
        att,
        tokens,
        *[weights] * 5,
        vectors,
        segments,
        cot_pair,
        cot_out,
    )


def head_sums(values):
    rows = lax.broadcasted_iota(jnp.int32, (GW, GW), 0)
    cols = lax.broadcasted_iota(jnp.int32, (GW, GW), 1)
    takes = (rows // PAIR == cols // PAIR) & (rows // HDIM != cols // HDIM)
    takes = takes.astype(jnp.float32).astype(jnp.bfloat16)
    sums = jnp.concatenate(
        [split_dot_left(values[:, at : at + GW], takes, NN) for at in range(0, D, GW)], axis=1
    )
    high = sums.astype(jnp.bfloat16).astype(jnp.float32)
    middle = (sums - high).astype(jnp.bfloat16).astype(jnp.float32)
    place = lax.broadcasted_iota(jnp.int32, (1, D), 1) % HDIM
    terms = jnp.where(place == 0, high, jnp.where(place == 1, middle, sums - high - middle))
    return jnp.where(place < 3, terms, 0.0).astype(jnp.bfloat16)


def feed_backward_kernel(
    low_ref,
    hidden_ref,
    inv1_ref,
    vectors_ref,
    slope_ref,
    wd_ref,
    wu_ref,
    wo_ref,
    start_in,
    normed1_in,
    att_in,
    inv_sum_in,
    exact_in,
    early_ref,
    dbu_ref,
    sums_ref,
    dres_out,
    datt_out,
    terms_out,
    total_ref,
    normed1_ref,
    att_ref,
    inv_sum_ref,
    exact_ref,
    grad_ref,
    datt_ref,
    terms_ref,
    sems,
):
    step = pl.program_id(0)
    slots = low_ref.shape[0]
    last = pl.num_programs(0) - 1
    loads = [
        pltpu.make_async_copy(src, dst, sems.at[i])
        for i, (src, dst) in enumerate(
            (
                (start_in, total_ref),
                (normed1_in, normed1_ref),
                (att_in, att_ref),
                (inv_sum_in, inv_sum_ref),
                (exact_in, exact_ref),
            )
        )
    ]

    @pl.when(step == 0)
    def _():
        for load in loads:
            load.start()

    @pl.when(step < last)
    def _():
        dact = dot(low_ref[...], wd_ref[...], NT)
        dpre = (dact * slope_ref[...].astype(jnp.float32)).astype(jnp.bfloat16)
        dbu_ref[...] = jnp.sum(dpre.astype(jnp.float32), axis=0, keepdims=True)
        store_halves(early_ref, dot(dpre, hidden_ref[...], TN))
        pl.when(step == 0)(loads[0].wait)
        total_ref[...] += dot(dpre, wu_ref[...], NN)

    @pl.when(step == last)
    def _():
        sums_ref[...] = jnp.zeros_like(sums_ref)
        for load in loads[1:]:
            load.wait()

        def rows_step(at):
            rows = tile_rows(at)
            grad = total_ref[rows, :]
            normed = normed1_ref[rows, :]
            sums_ref[0:1, :] += jnp.sum(grad * normed, axis=0, keepdims=True)
            sums_ref[1:2, :] += jnp.sum(grad, axis=0, keepdims=True)
            dres = normalize_back(grad * vectors_ref[0:1, :], normed, inv1_ref[rows, :])
            low = dres.astype(jnp.bfloat16)
            sums_ref[4:5, :] += jnp.sum(low.astype(jnp.float32), axis=0, keepdims=True)
            total_ref[rows, :] = dres
            grad_ref[rows, :] = low
            datt = dot(low, wo_ref[...], NN).astype(jnp.bfloat16).astype(jnp.float32)
            datt = (datt * inv_sum_ref[rows, :]).astype(jnp.bfloat16)
            datt_ref[rows, :] = datt
            terms_ref[rows, :] = head_sums(datt.astype(jnp.float32) * exact_ref[rows, :])

        pl.loop(0, slots // TILE)(rows_step)
        sends = [
            pltpu.make_async_copy(src, dst, sems.at[5 + i])
            for i, (src, dst) in enumerate(
                ((total_ref, dres_out), (datt_ref, datt_out), (terms_ref, terms_out))
            )
        ]
        for send in sends:
            send.start()
        store_halves(early_ref, dot(grad_ref[...], att_ref[...], TN))
        for send in sends:
            send.wait()


def feed_backward(low, start, normed1, inv1, hidden, slope, att, inv_sum, exact, vectors, weights):
    slots = low.shape[0]
    last = PARTS - 1
    full = once((slots, D))
    anywhere = pl.BlockSpec(memory_space=pl.ANY)

    def at(i):
        return jnp.minimum(i, last - 1)

    return pl.pallas_call(
        feed_backward_kernel,
        grid=(PARTS,),
        in_specs=[
            full,
            full,
            once((slots, 1)),
            once(vectors.shape),
            pl.BlockSpec((slots, D), lambda i: (0, at(i))),
            pl.BlockSpec((D, D), lambda i: (4 + PARTS + at(i), 0)),
            pl.BlockSpec((D, D), lambda i: (4 + at(i), 0)),
            square(3),
        ]
        + [anywhere] * 5,
        out_specs=[
            pl.BlockSpec(HALF_BLOCK, lambda i: (0, jnp.where(i == last, 3, 4 + i), 0)),
            pl.BlockSpec((1, D), lambda i: (0, at(i))),
            fixed((8, D)),
        ]
        + [anywhere] * 3,
        out_shape=[
            shape_of((2, HALF_ROWS, D // 2), jnp.bfloat16),
            shape_of((1, FF - D)),
            shape_of((8, D)),
            shape_of((slots, D)),
            shape_of((slots, D), jnp.bfloat16),
            shape_of((slots, D), jnp.bfloat16),
        ],
        scratch_shapes=[
            pltpu.VMEM((slots, D), jnp.float32),
            pltpu.VMEM((slots, D), jnp.float32),
            pltpu.VMEM((slots, D), jnp.bfloat16),
            pltpu.VMEM((slots, D), jnp.float32),
            pltpu.VMEM((slots, D), jnp.float32),
            pltpu.VMEM((slots, D), jnp.bfloat16),
            pltpu.VMEM((slots, D), jnp.bfloat16),
            pltpu.VMEM((slots, D), jnp.bfloat16),
            pltpu.SemaphoreType.DMA((8,)),
        ],
        compiler_params=params(),
        cost_estimate=cost(17e9, 40e6),
        name="feed_backward",
    )(low, hidden, inv1, vectors, slope, weights, weights, weights, start, normed1, att, inv_sum, exact)


def attention_backward_kernel(
    patches_ref,
    grown_ref,
    datt_ref,
    terms_ref,
    v_ref,
    k_ref,
    q_ref,
    box_row_ref,
    dqkv_ref,
    dcoef_ref,
    box_col_ref,
    bucket0_ref,
    bucket1_ref,
    dscore_ref,
):
    pair = pl.program_id(0)
    slots = datt_ref.shape[0]
    low = jnp.bfloat16
    live_row = lax.broadcasted_iota(jnp.int32, (1, slots), 1) < TEXT + patches_ref[0]

    @pl.when(pair == 0)
    def _():
        write_buckets(box_row_ref, box_col_ref, (bucket0_ref, bucket1_ref), live_row)

    query_t = q_ref[...].astype(jnp.float32).T.astype(low)
    key_t = (k_ref[...].astype(jnp.float32) * HDIM ** (-0.5)).T
    key_t = jnp.where(live_row, key_t, 0.0).astype(low)
    datt_t = datt_ref[...].astype(jnp.float32).T.astype(low)
    lanes = lax.broadcasted_iota(jnp.int32, (1, PAIR), 1)
    second = lanes >= HDIM
    masks = [jnp.where(second, 0.0, 1.0), jnp.where(second, 1.0, 0.0)]
    masks = [mask.astype(low) for mask in masks]
    dcoef_ref[...] = jnp.zeros_like(dcoef_ref)
    leads = []
    values = []
    for j in range(2):
        at = HDIM * (1 - j)
        minus = jnp.where((lanes >= at) & (lanes < at + 3), -1.0, 0.0).astype(low)
        leads.append(datt_ref[...] * masks[j] + terms_ref[...] * masks[1 - j])
        values.append(v_ref[...] * masks[j] + minus)

    for j in range(2):
        head_rows = slice(j * HDIM, (j + 1) * HDIM)
        for step in range(slots // TILE):
            rows = slice(step * TILE, (step + 1) * TILE)
            diff = dot(leads[j][rows], values[j], NT)
            dscore = grown_ref[j, rows, :].astype(jnp.float32) * diff
            dscore_ref[j, rows, :] = dscore.astype(low)
            dcoef_ref[j, 0:1, :] += jnp.sum(dscore * bucket0_ref[rows, :], axis=0, keepdims=True)
            dcoef_ref[j, 1:2, :] += jnp.sum(dscore * bucket1_ref[rows, :], axis=0, keepdims=True)
        dqkv_ref[0, head_rows] = dot(key_t[head_rows], dscore_ref[j], NT).astype(low)
        dkey = dot(query_t[head_rows], dscore_ref[j], NN) * (1.0 / LOG2E)
        dqkv_ref[1, head_rows] = jnp.where(live_row, dkey, 0.0).astype(low)
        dvalue = dot(datt_t[head_rows], grown_ref[j], NN)
        dqkv_ref[2, head_rows] = jnp.where(live_row, dvalue, 0.0).astype(low)


def attention_backward(grown, datt, terms, q, k, v, boxes, patches):
    slots = datt.shape[0]
    pair_block = pl.BlockSpec((slots, PAIR), lambda h: (0, h))
    return pl.pallas_call(
        attention_backward_kernel,
        grid=(HEADS // 2,),
        in_specs=[
            pl.BlockSpec(memory_space=pltpu.SMEM),
            pl.BlockSpec((2, slots, slots), lambda h: (h, 0, 0)),
        ]
        + [pair_block] * 5
        + [fixed((2, slots))],
        out_specs=[
            pl.BlockSpec((3, PAIR, slots), lambda h: (0, h, 0)),
            pl.BlockSpec((2, 2, slots), lambda h: (h, 0, 0)),
        ],
        out_shape=[
            shape_of((3, D, slots), jnp.bfloat16),
            shape_of((HEADS, 2, slots)),
        ],
        scratch_shapes=[pltpu.VMEM((slots, 8), jnp.int32)]
        + [pltpu.VMEM((slots, slots), jnp.float32)] * 2
        + [pltpu.VMEM((2, slots, slots), jnp.bfloat16)],
        compiler_params=params(),
        cost_estimate=cost(15e9, 40e6),
        name="attention_backward",
    )(patches, grown, datt, terms, v, k, q, boxes)


def qkv_weights_kernel(dqkv_ref, tokens_ref, _, early_ref, sums_ref):
    part = dqkv_ref[0]
    store_halves(early_ref, dot(part, tokens_ref[...], NN))
    sums_ref[0] = dot(jnp.ones((8, part.shape[1]), jnp.bfloat16), part, NT)


def qkv_weights(dqkv, tokens, early):
    slots = tokens.shape[0]
    return pl.pallas_call(
        qkv_weights_kernel,
        grid=(3,),
        in_specs=[
            pl.BlockSpec((1, D, slots), lambda i: (i, 0, 0)),
            fixed((slots, D)),
            pl.BlockSpec(memory_space=pl.ANY),
        ],
        out_specs=[
            pl.BlockSpec(HALF_BLOCK, lambda i: (0, i, 0)),
            pl.BlockSpec((1, 8, D), lambda i: (i, 0, 0)),
        ],
        out_shape=[shape_of(early.shape, jnp.bfloat16), shape_of((3, 8, D))],
        input_output_aliases={2: 0},
        compiler_params=params(),
        cost_estimate=cost(3.6e9, 10e6),
        name="qkv_weights",
    )(dqkv, tokens, early)


def token_gradient_kernel(dqkv_ref, weight_ref, dres_ref, grad_ref):
    total = dres_ref[...]
    for part in range(3):
        total = total + dot(dqkv_ref[part], weight_ref[part * D : (part + 1) * D, :], TN)
    grad_ref[...] = total.astype(jnp.bfloat16)


def token_gradient(dqkv, weights, dres):
    slots = dres.shape[0]
    tile = pl.BlockSpec((TILE, D), lambda i: (i, 0))
    return pl.pallas_call(
        token_gradient_kernel,
        grid=(slots // TILE,),
        in_specs=[
            pl.BlockSpec((3, D, TILE), lambda i: (0, 0, i)),
            pl.BlockSpec((3 * D, D), lambda i: (0, 0), pipeline_mode=pl.Buffered(1)),
            tile,
        ],
        out_specs=tile,
        out_shape=shape_of((slots, D), jnp.bfloat16),
        compiler_params=params(),
        cost_estimate=cost(3.6e9, 12e6),
        name="token_gradient",
    )(dqkv, weights, dres)


def page_step(
    tokens, boxes, segments, patches, cot_out, cot_pair, pieces, layout, vectors, box_coef
):
    (q, k, v, grown, att, inv_sum, exact), weights = attention_forward(
        tokens, pieces, layout, vectors, boxes, patches, box_coef
    )
    slope, late, pair_scores, sums2, dbu_tail, inv1, mixed, normed1, hidden, low, start = middle(
        att, tokens, weights, vectors, segments, cot_pair, cot_out, patches
    )
    early, dbu_head, sums1, dres, datt, terms = feed_backward(
        low, start, normed1, inv1, hidden, slope, att, inv_sum, exact, vectors, weights
    )
    dqkv, dcoef = attention_backward(grown, datt, terms, q, k, v, boxes, patches)
    early, bias_sums = qkv_weights(dqkv, tokens, early)
    early, late = lax.optimization_barrier((early, scatter_dp(late)))
    early = scatter_dp(early)
    token_grad = token_gradient(dqkv, weights, dres)
    vector_part = jnp.concatenate(
        [
            sums1[:2],
            bias_sums[0, :1],
            bias_sums[2, :1],
            sums1[4:5],
            sums2[:3],
            dbu_head.reshape(FF // D - 1, D),
            dbu_tail,
        ],
        axis=0,
    )
    coef_part = jnp.sum(dcoef, axis=2).T
    return (mixed, pair_scores, token_grad, early, late, vector_part, coef_part)


def exchange_sum(values):
    for axis in ("dp", "grid"):
        size = lax.axis_size(axis)
        reach = 1
        while reach < size:
            values = values + lax.ppermute(values, axis, [(i, i ^ reach) for i in range(size)])
            reach *= 2
    return values


def scatter_dp(halves):
    return lax.psum_scatter(
        halves.reshape(-1, D // 2), "dp", scatter_dimension=0, tiled=True
    )


def scatter_grid(rows):
    size = lax.axis_size("grid")
    place = lax.axis_index("grid")
    blocks = rows.reshape(size, -1, D // 2)

    def block(at):
        return lax.dynamic_index_in_dim(blocks, at % size, 0, keepdims=False)

    got = [
        lax.ppermute(block(place + s), "grid", [(i, (i + s) % size) for i in range(size)])
        for s in range(1, size)
    ]
    return sum((g.astype(jnp.float32) for g in got), block(place).astype(jnp.float32))


def swap_halves(first, second):
    size = lax.axis_size("dp")
    low = lax.axis_index("dp") < size // 2
    other = lax.ppermute(
        jnp.where(low, second, first).astype(jnp.bfloat16), "dp", [(i, (i + size // 2) % size) for i in range(size)]
    ).astype(jnp.float32)
    kept = jnp.where(low, first, second)
    return jnp.concatenate([jnp.where(low, kept, other), jnp.where(low, other, kept)], axis=1)


def gather_weights(shard, ready):
    dp_size, grid_size = lax.axis_size("dp"), lax.axis_size("grid")
    rows = shard.shape[0]
    if (dp_size, grid_size) != (8, 4) or rows != 336:
        return [lax.all_gather(shard, ("dp", "grid"), axis=0, tiled=True)], None
    barrier = lax.optimization_barrier

    def over(values, reach):
        return lax.ppermute(values, "dp", [(i, i ^ reach) for i in range(dp_size)])

    def up(values, reach):
        return lax.ppermute(values, "grid", [(i, (i + reach) % grid_size) for i in range(grid_size)])

    cuts = (0, *CUTS)
    one, two = (shard[a:b] for a, b in zip(cuts, cuts[1:]))
    rest = lax.all_gather(shard[cuts[-1] :], ("dp", "grid"), axis=0)
    hops = (1, 2, 3)
    one_grid = jnp.stack([one] + [up(one, s) for s in hops])
    one_grid, two, *_ = barrier((one_grid, two, *ready))
    one_x, one_y = over(one_grid, 2), over(one_grid, 4)
    two_grid = jnp.stack([two] + [up(two, s) for s in hops])
    one_x, one_y, two_grid = barrier((one_x, one_y, two_grid))
    two_x, two_y = over(two_grid, 2), over(two_grid, 4)
    two_x, two_y = barrier((two_x, two_y))
    xy = over(jnp.concatenate([one_y[:2], two_y[:2]], axis=1), 2)
    yx = over(jnp.concatenate([one_x[2:], two_x[2:]], axis=1), 4)
    own = [one_grid, one_x, one_y, two_grid, two_x, two_y, xy, yx]
    every = tuple(range(grid_size))
    layout = [(cuts[part], [(r, s) for s in every]) for part in (0, 1) for r in (0, 2, 4)]
    layout += [(0, [(6, s) for s in (0, 1)]), (0, [(6, s) for s in (2, 3)])]
    layout += [(start, [(r ^ 1, s) for r, s in entries]) for start, entries in layout]
    pieces = own + [over(piece, 1) for piece in own]
    return pieces + [rest], layout + [(cuts[-1], None)]


CUTS = (96, 208)


def momentum_step(grad, param, moment, average, rate):
    new_moment = 0.5 * moment + grad
    new_param = param - rate * (grad + 0.5 * new_moment)
    new_average = 0.5 * average + 0.5 * new_param
    return (new_moment, new_param, new_average)


def on_device(
    tokens,
    boxes,
    segments,
    patches,
    cot_out,
    cot_pair,
    weights,
    weight_momentum,
    weight_average,
    vectors,
    vector_momentum,
    vector_average,
    box_coef,
    coef_momentum,
    coef_average,
):
    axes = ("dp", "grid")
    page_count, slot_count = tokens.shape[:2]
    device_count = lax.axis_size(axes)
    segments = jnp.pad(segments, ((0, 0), (0, slot_count - segments.shape[1])), constant_values=SEGS)
    pieces, layout = gather_weights(weights.astype(jnp.bfloat16), (segments,))
    pages = [
        page_step(
            tokens[p],
            boxes[p],
            segments[p : p + 1],
            patches[p : p + 1],
            cot_out[p],
            cot_pair[p],
            pieces,
            layout,
            vectors,
            box_coef,
        )
        for p in range(page_count)
    ]
    mixed, pair_scores, token_grad = (jnp.stack([page[i] for page in pages]) for i in range(3))
    early, late = (sum(page[i] for page in pages) for i in (3, 4))
    small = sum(
        jnp.concatenate([page[5], jnp.pad(page[6].reshape(1, 2 * HEADS), ((0, 3), (0, D - 2 * HEADS)))], axis=0)
        for page in pages
    )
    late_rows = scatter_grid(late)
    early_rows = scatter_grid(early)
    small = exchange_sum(small)
    weight_grad = swap_halves(early_rows, late_rows)
    vector_rows = vectors.shape[0]
    vector_grad = small[:vector_rows]
    coef_grad = small[vector_rows, : 2 * HEADS].reshape(2, HEADS)
    rate_scale = (device_count * page_count * slot_count) ** (-0.5)
    new_weight_momentum, new_weights, new_weight_average = momentum_step(
        weight_grad, weights, weight_momentum, weight_average, 0.1 * rate_scale
    )
    new_vector_momentum, new_vectors, new_vector_average = momentum_step(
        vector_grad, vectors, vector_momentum, vector_average, 0.1 * rate_scale
    )
    new_coef_momentum, new_coef, new_coef_average = momentum_step(
        coef_grad, box_coef, coef_momentum, coef_average, 0.01 * rate_scale
    )
    return (
        mixed,
        pair_scores,
        token_grad,
        weight_grad,
        new_weights,
        new_weight_momentum,
        new_weight_average,
        new_weights.astype(jnp.bfloat16),
        vector_grad,
        new_vectors,
        new_vector_momentum,
        new_vector_average,
        coef_grad,
        new_coef,
        new_coef_momentum,
        new_coef_average,
    )


def solution(mesh):
    rows = P(("dp", "grid"))
    return jax.shard_map(
        on_device,
        mesh=mesh,
        in_specs=(rows,) * 9 + (P(),) * 6,
        out_specs=(rows,) * 8 + (P(),) * 8,
        check_vma=False,
    )
```

```python
import functools
import math

import jax
import jax.numpy as jnp
from jax import lax
from jax.experimental import pallas as pl
from jax.experimental.pallas import tpu as pltpu
from jax.sharding import PartitionSpec as P

D = 768
HEADS = 12
HDIM = 64
FF = 3072
TEXT = 448
SEGS = 64
PAIR = 2 * HDIM
GW = 2 * PAIR
LOG2E = math.log2(math.e)
TILE = 256
WIDE = 512
VMEM_LIMIT = 60 * 1024 * 1024
NT = (((1,), (1,)), ((), ()))
NN = (((1,), (0,)), ((), ()))
TN = (((0,), (0,)), ((), ()))

def dot(a, b, dims):
    return lax.dot_general(a, b, dims, preferred_element_type=jnp.float32)


def split_dot(exact, b, dims):
    high = b.astype(jnp.bfloat16)
    rest = b - high.astype(jnp.float32)
    middle = rest.astype(jnp.bfloat16)
    last = (rest - middle.astype(jnp.float32)).astype(jnp.bfloat16)
    return dot(exact, high, dims) + dot(exact, middle, dims) + dot(exact, last, dims)


def params():
    return pltpu.CompilerParams(vmem_limit_bytes=VMEM_LIMIT)


def cost(flops, nbytes):
    return pl.CostEstimate(flops=int(flops), bytes_accessed=int(nbytes), transcendentals=0)


def tile_rows(step):
    return pl.ds(pl.multiple_of(step * TILE, TILE), TILE)


def wide_rows(step):
    return pl.ds(pl.multiple_of(step * WIDE, WIDE), WIDE)


def fixed(shape):
    return pl.BlockSpec(shape, lambda *_: (0,) * len(shape))


def once(shape):
    return pl.BlockSpec(shape, lambda *_: (0,) * len(shape), pipeline_mode=pl.Buffered(1))


def shape_of(dims, dtype=jnp.float32):
    return jax.ShapeDtypeStruct(dims, dtype)


HALF_BLOCK = (2, D, D // 2)
HALF_ROWS = (3 * D + D + FF + FF + 2 * D) // 2


def square(at):
    return pl.BlockSpec((D, D), lambda i: (at, 0), pipeline_mode=pl.Buffered(1))


def write_buckets(box_row_ref, box_col_ref, bucket_refs, live_row=None):
    box_col_ref[...] = jnp.tile(box_row_ref[...].astype(jnp.float32), (4, 1)).T.astype(jnp.int32)

    def fill(step):
        rows = tile_rows(step)
        for c in range(2):
            spread = jnp.abs(box_col_ref[rows, c : c + 1] - box_row_ref[c : c + 1, :])
            bucket = jnp.minimum(spread >> 5, 31).astype(jnp.float32)
            bucket_refs[c][rows, :] = bucket if live_row is None else jnp.where(live_row, bucket, 0.0)

    pl.loop(0, box_row_ref.shape[1] // TILE)(fill)


def place_weights(layout, piece_refs, weight_ref, out_ref, sems, meanwhile):
    step = pl.program_id(0)
    place = lax.axis_index("grid")
    mine = lax.axis_index("dp")
    depth = lax.axis_size("grid")
    shard = weight_ref.shape[0] // (lax.axis_size("dp") * depth)
    by_owner = {}
    count = 0
    for ref, (start, entries) in zip(piece_refs, layout):
        rows = ref.shape[1]
        if entries is None:
            every = [(owner, "far") for owner in range(ref.shape[0])]
        else:
            every = [
                ((mine ^ over) * depth + lax.rem(place + depth - back, depth), over)
                for over, back in entries
            ]
        for at, (owner, over) in enumerate(every):
            if over == "far" and owner * shard < 3 * D:
                over = "near"
            target = weight_ref.at[pl.ds(pl.multiple_of(owner * shard + start, 16), rows)]
            by_owner.setdefault(over, []).append(pltpu.make_async_copy(ref.at[at], target, sems.at[count]))
            count += 1
    out = pltpu.make_async_copy(weight_ref, out_ref, sems.at[count])
    needed = -(-3 * D // (shard * depth))

    def each(first, action):
        for over, copies in by_owner.items():
            if over in ("near", "far"):
                if first == (over == "near"):
                    for copy in copies:
                        action(copy)
                continue
            chosen = (mine ^ over) < needed

            @pl.when(chosen if first else jnp.logical_not(chosen))
            def _():
                for copy in copies:
                    action(copy)

    @pl.when(step == 0)
    def _():
        each(True, lambda copy: copy.start())
        meanwhile()
        each(True, lambda copy: copy.wait())
        each(False, lambda copy: copy.start())

    @pl.when(step == 1)
    def _():
        each(False, lambda copy: copy.wait())
        out.start()

    @pl.when(step == pl.num_programs(0) - 1)
    def _():
        out.wait()


def attention_forward_kernel(
    layout,
    pieces,
    coef_ref,
    patches_ref,
    tokens_ref,
    vectors_ref,
    box_row_ref,
    *refs,
):
    piece_refs, refs = refs[:pieces], refs[pieces:]
    q_ref, k_ref, v_ref, grown_ref, att_ref, inv_ref, exact_ref = refs[:7]
    box_col_ref, bucket0_ref, bucket1_ref, live_ref, value_ref, size_ref, weight_ref, sems = refs[-8:]
    pair = pl.program_id(0)
    slots = tokens_ref.shape[0]
    side = pl.ds(pl.multiple_of(pair % 2 * PAIR, PAIR), PAIR)
    low = jnp.bfloat16

    def prepare():
        write_buckets(box_row_ref, box_col_ref, (bucket0_ref, bucket1_ref))
        slot = lax.broadcasted_iota(jnp.int32, (slots, PAIR), 0)
        live_ref[...] = (slot < TEXT + patches_ref[0]).astype(jnp.float32).astype(low)

    if layout is None:

        @pl.when(pair == 0)
        def _():
            load = pltpu.make_async_copy(piece_refs[0].at[pl.ds(0, 3 * D)], weight_ref, sems.at[0])
            load.start()
            prepare()
            load.wait()

    else:
        place_weights(layout, piece_refs, weight_ref, refs[7], sems, prepare)

    @pl.when(pair % 2 == 0)
    def _():
        def weight(at):
            return weight_ref[pl.ds(pl.multiple_of(at * D + pair // 2 * GW, GW), GW), :]

        query = (dot(tokens_ref[...], weight(0), NT) + vectors_ref[2:3, :]) * (
            LOG2E * HDIM ** (-0.5)
        )
        key = dot(tokens_ref[...], weight(1), NT)
        q_ref[...] = query.astype(low)
        k_ref[...] = key.astype(low)
        v_ref[...] = (dot(tokens_ref[...], weight(2), NT) + vectors_ref[3:4, :]).astype(low)
        of_head = lax.broadcasted_iota(jnp.int32, (GW, PAIR), 0) // HDIM
        ones = (of_head == lax.broadcasted_iota(jnp.int32, (GW, PAIR), 1)).astype(low)
        query_size = jnp.max(dot((query * query).astype(low), ones, NN), axis=0, keepdims=True)
        key_size = jnp.max(dot((key * key).astype(low), ones, NN), axis=0, keepdims=True)
        size_ref[0] = jnp.max(query_size * key_size)

    second = lax.broadcasted_iota(jnp.int32, (1, PAIR), 1) >= HDIM
    masks = [jnp.where(second, 0.0, 1.0), jnp.where(second, 1.0, 0.0)]
    masks = [mask.astype(low) for mask in masks]
    value = v_ref[:, side] * live_ref[...]
    for j in range(2):
        value_ref[j] = value * masks[j] + live_ref[...] * masks[1 - j]
    coefs = [[coef_ref[c, 2 * pair + j] * LOG2E for c in range(2)] for j in range(2)]
    spread = [31.0 * (jnp.abs(c[0]) + jnp.abs(c[1])) for c in coefs]
    room = 57.0 - jnp.maximum(spread[0], spread[1])
    small = (room > 0) & (1.03 * size_ref[0] <= room * room)

    def rows_step(step, shifted):
        rows = tile_rows(step)
        query = q_ref[rows, side]
        bucket0 = bucket0_ref[rows, :]
        bucket1 = bucket1_ref[rows, :]
        found = []
        for j in range(2):
            score = dot(query * masks[j], k_ref[:, side], NT)
            score = score + coefs[j][0] * bucket0 + coefs[j][1] * bucket1
            if shifted:
                slot = lax.broadcasted_iota(jnp.int32, (1, slots), 1)
                score = jnp.where(slot < TEXT + patches_ref[0], score, -1e30)
                score = score - jnp.max(score, axis=1, keepdims=True)
            grown = jnp.exp2(score).astype(low)
            grown_ref[j, rows, :] = grown
            found.append(dot(grown, value_ref[j], NN))
        total = jnp.where(second, found[0], found[1])
        inv = 1.0 / pltpu.roll(total, HDIM, 1)
        exact = jnp.where(second, found[1], found[0]) * inv
        exact_ref[rows, :] = exact
        att_ref[rows, :] = exact.astype(low)
        inv_ref[rows, :] = inv

    @pl.when(small)
    def _():
        pl.loop(0, slots // TILE, unroll=4)(lambda step: rows_step(step, False))

    @pl.when(jnp.logical_not(small))
    def _():
        pl.loop(0, slots // TILE)(lambda step: rows_step(step, True))


def attention_forward(tokens, pieces, layout, vectors, boxes, patches, box_coef):
    slots = tokens.shape[0]
    smem = pl.BlockSpec(memory_space=pltpu.SMEM)
    anywhere = pl.BlockSpec(memory_space=pl.ANY)
    lane_block = pl.BlockSpec((slots, GW), lambda h: (0, h // 2))
    pair_block = pl.BlockSpec((slots, PAIR), lambda h: (0, h))
    low = shape_of((slots, D), jnp.bfloat16)
    wide = shape_of((slots, D))
    weights = shape_of((2 * HALF_ROWS, D), jnp.bfloat16)
    copies = 0 if layout is None else sum(
        piece.shape[0] if entries is None else len(entries) for piece, (_, entries) in zip(pieces, layout)
    )
    out = pl.pallas_call(
        functools.partial(attention_forward_kernel, layout, len(pieces)),
        grid=(HEADS // 2,),
        in_specs=[
            smem,
            smem,
            fixed((slots, D)),
            pl.BlockSpec((vectors.shape[0], GW), lambda h: (0, h // 2)),
            fixed((2, slots)),
        ]
        + [anywhere] * len(pieces),
        out_specs=[lane_block] * 3
        + [pl.BlockSpec((2, slots, slots), lambda h: (h, 0, 0))]
        + [pair_block] * 3
        + [anywhere] * bool(copies),
        out_shape=[low] * 3
        + [shape_of((HEADS, slots, slots), jnp.bfloat16), low, wide, wide]
        + [weights] * bool(copies),
        scratch_shapes=[pltpu.VMEM((slots, 8), jnp.int32)]
        + [pltpu.VMEM((slots, slots), jnp.float32)] * 2
        + [
            pltpu.VMEM((slots, PAIR), jnp.bfloat16),
            pltpu.VMEM((2, slots, PAIR), jnp.bfloat16),
            pltpu.SMEM((1,), jnp.float32),
            pltpu.VMEM(weights.shape if copies else (3 * D, D), jnp.bfloat16),
            pltpu.SemaphoreType.DMA((copies + 1,)),
        ],
        compiler_params=params(),
        cost_estimate=cost(10e9, 40e6),
        name="attention_forward",
    )(box_coef, patches, tokens, vectors, boxes, *pieces)
    return out[:7], out[7] if copies else pieces[0]


def normalize(values):
    centered = values - jnp.mean(values, axis=-1, keepdims=True)
    inv_std = lax.rsqrt(jnp.mean(centered * centered, axis=-1, keepdims=True) + 1e-05)
    return (centered * inv_std, inv_std)


def normalize_back(grad_normed, normed, inv_std):
    first_mean = jnp.mean(grad_normed, axis=-1, keepdims=True)
    second_mean = jnp.mean(grad_normed * normed, axis=-1, keepdims=True)
    return inv_std * (grad_normed - first_mean - normed * second_mean)


def gelu_pair(values):
    below = 0.5 + 0.5 * lax.erf(values * (0.5**0.5))
    bell = jnp.exp(values * values * -0.5) * (0.5 / math.pi) ** 0.5
    return (values * below, below + values * bell)


def split_dot_left(a, exact, dims):
    high = a.astype(jnp.bfloat16)
    rest = a - high.astype(jnp.float32)
    middle = rest.astype(jnp.bfloat16)
    last = (rest - middle.astype(jnp.float32)).astype(jnp.bfloat16)
    return dot(high, exact, dims) + dot(middle, exact, dims) + dot(last, exact, dims)


def store_halves(ref, values):
    ref[0] = values[:, : D // 2].astype(jnp.bfloat16)
    ref[1] = values[:, D // 2 :].astype(jnp.bfloat16)


PARTS = FF // D
NORM_STEP = PARTS + 1
TAIL_STEP = PARTS + 2
PAIR_STEP = TAIL_STEP + PARTS + 1


def middle_kernel(
    patches_ref,
    att_ref,
    tokens_ref,
    wo_ref,
    wu_ref,
    wd_ref,
    wl_ref,
    wr_ref,
    vectors_ref,
    segment_row_ref,
    cot_pair_ref,
    cot_ref,
    slope_ref,
    late_ref,
    pair_ref,
    sums_ref,
    dbu_ref,
    inv1_ref,
    mixed_out,
    normed1_out,
    hidden_out,
    low_out,
    dres_out,
    act_ref,
    tail_ref,
    mixed_ref,
    normed1_ref,
    hidden_ref,
    low_ref,
    total_ref,
    normed2_ref,
    inv2_ref,
    pool_ref,
    pooled_ref,
    dpair_ref,
    sems,
):
    step = pl.program_id(0)
    slots = att_ref.shape[0]
    tiles = slots // TILE
    outs = (
        (normed1_ref, normed1_out),
        (hidden_ref, hidden_out),
        (mixed_ref, mixed_out),
        (low_ref, low_out),
        (total_ref, dres_out),
    )
    sends = [pltpu.make_async_copy(src, dst, sems.at[i]) for i, (src, dst) in enumerate(outs)]

    @pl.when(step == 0)
    def _():

        @pl.loop(0, tiles)
        def _(at):
            rows = tile_rows(at)
            branch = dot(att_ref[rows, :], wo_ref[...], NT) + vectors_ref[4:5, :]
            normed, inv = normalize(tokens_ref[rows, :].astype(jnp.float32) + branch)
            hidden = normed * vectors_ref[0:1, :] + vectors_ref[1:2, :]
            normed1_ref[rows, :] = normed
            inv1_ref[rows, :] = inv
            hidden_ref[rows, :] = hidden.astype(jnp.bfloat16)
            total_ref[rows, :] = hidden + vectors_ref[7:8, :]

        sends[0].start()
        sends[1].start()

    @pl.when((step > 0) & (step <= PARTS))
    def _():
        bias = vectors_ref[pl.ds(7 + step, 1), :]

        for at in range(tiles):
            rows = slice(at * TILE, (at + 1) * TILE)
            act, slope = gelu_pair(dot(hidden_ref[rows, :], wu_ref[...], NT) + bias)
            act = act.astype(jnp.bfloat16)
            act_ref[step - 1, rows, :] = act
            slope_ref[rows, :] = slope.astype(jnp.bfloat16)
            total_ref[rows, :] += dot(act, wd_ref[...], NN)

    @pl.when(step == NORM_STEP)
    def _():
        numbers = lax.broadcasted_iota(jnp.int32, (SEGS, 1), 0)
        slot_row = lax.broadcasted_iota(jnp.int32, (1, slots), 1)
        member = (segment_row_ref[...] == numbers) & (slot_row < TEXT)
        counted = jnp.sum(member.astype(jnp.float32), axis=1, keepdims=True)
        pool_ref[...] = jnp.zeros_like(pool_ref)

        @pl.loop(0, tiles)
        def _(at):
            rows = tile_rows(at)
            normed, inv = normalize(total_ref[rows, :])
            inv2_ref[rows, :] = inv
            output = normed * vectors_ref[5:6, :] + vectors_ref[6:7, :]
            normed2_ref[rows, :] = normed
            mixed_ref[rows, :] = output.astype(jnp.bfloat16)

            @pl.when(at * TILE < TEXT)
            def _():
                slot = at * TILE + lax.broadcasted_iota(jnp.int32, (1, TILE), 1)
                belongs = (segment_row_ref[:, rows] == numbers) & (slot < TEXT)
                pool_ref[...] += split_dot(belongs.astype(jnp.bfloat16), output, NN)

        sends[2].start()
        pooled = (pool_ref[...] / counted).astype(jnp.bfloat16)
        left_weight = wl_ref[...]
        right_weight = wr_ref[...]
        scale = D ** (-0.5)
        left = dot(pooled, left_weight, NT).astype(jnp.bfloat16)
        right = dot(pooled, right_weight, NT).astype(jnp.bfloat16)
        pair_ref[...] = dot(left, right, NT) * scale
        cot = cot_pair_ref[...]
        grad_left = (split_dot_left(cot, right, NN) * scale).astype(jnp.bfloat16)
        grad_right = (split_dot_left(cot, left, TN) * scale).astype(jnp.bfloat16)
        grad_pooled = dot(grad_left, left_weight, NN) + dot(grad_right, right_weight, NN)
        spread = grad_pooled / counted
        pooled_ref[...] = pooled
        dpair_ref[0] = grad_left
        dpair_ref[1] = grad_right
        pool_ref[...] = spread
        sums_ref[...] = jnp.zeros_like(sums_ref)

        @pl.loop(0, tiles)
        def _(at):
            rows = tile_rows(at)
            slot = at * TILE + lax.broadcasted_iota(jnp.int32, (TILE, 1), 0)
            live = (slot < TEXT + patches_ref[0]).astype(jnp.float32)
            slot_of = at * TILE + lax.broadcasted_iota(jnp.int32, (1, TILE), 1)
            belongs = (segment_row_ref[:, rows] == numbers) & (slot_of < TEXT)
            grad = cot_ref[rows, :].astype(jnp.float32) * live
            grad = grad + split_dot(belongs.astype(jnp.bfloat16), pool_ref[...], TN)
            normed = normed2_ref[rows, :]
            sums_ref[0:1, :] += jnp.sum(grad * normed, axis=0, keepdims=True)
            sums_ref[1:2, :] += jnp.sum(grad, axis=0, keepdims=True)
            dres = normalize_back(grad * vectors_ref[5:6, :], normed, inv2_ref[rows, :])
            low = dres.astype(jnp.bfloat16)
            sums_ref[2:3, :] += jnp.sum(low.astype(jnp.float32), axis=0, keepdims=True)
            total_ref[rows, :] = dres
            low_ref[rows, :] = low

        sends[3].start()

    @pl.when(step == TAIL_STEP)
    def _():
        dbu_ref[...] = jnp.zeros_like(dbu_ref)

        @pl.loop(0, slots // WIDE)
        def _(at):
            rows = wide_rows(at)
            dact = dot(low_ref[rows, :], wd_ref[...], NT)
            dpre = (dact * slope_ref[rows, :].astype(jnp.float32)).astype(jnp.bfloat16)
            dbu_ref[...] += jnp.sum(dpre.astype(jnp.float32), axis=0, keepdims=True)
            tail_ref[rows, :] = dpre
            total_ref[rows, :] += dot(dpre, wu_ref[...], NN)

        sends[4].start()
        store_halves(late_ref, dot(tail_ref[...], hidden_ref[...], TN))

    @pl.when((step > TAIL_STEP) & (step < PAIR_STEP))
    def _():
        store_halves(late_ref, dot(act_ref[step - TAIL_STEP - 1], low_ref[...], TN))

    @pl.when(step >= PAIR_STEP)
    def _():
        store_halves(late_ref, dot(dpair_ref[step - PAIR_STEP], pooled_ref[...], TN))

    @pl.when(step == PAIR_STEP + 1)
    def _():
        for send in sends:
            send.wait()


def middle(att, tokens, weights, vectors, segments, cot_pair, cot_out, patches):
    slots = att.shape[0]
    full = once((slots, D))
    anywhere = pl.BlockSpec(memory_space=pl.ANY)
    low = jnp.bfloat16

    def part(step):
        return jnp.clip(step - 1, 0, PARTS - 1)

    def half_row(step):
        return jnp.clip(step - TAIL_STEP, 0, PARTS + 2)

    return pl.pallas_call(
        middle_kernel,
        grid=(PAIR_STEP + 2,),
        in_specs=[
            pl.BlockSpec(memory_space=pltpu.SMEM),
            full,
            full,
            square(3),
            pl.BlockSpec((D, D), lambda i: (4 + part(i), 0)),
            pl.BlockSpec((D, D), lambda i: (4 + PARTS + part(i), 0)),
            square(4 + 2 * PARTS),
            square(5 + 2 * PARTS),
            once(vectors.shape),
            once((1, slots)),
            once((SEGS, SEGS)),
            full,
        ],
        out_specs=[
            pl.BlockSpec((slots, D), lambda i: (0, part(i))),
            pl.BlockSpec(HALF_BLOCK, lambda i: (0, half_row(i), 0)),
            fixed((SEGS, SEGS)),
            fixed((8, D)),
            fixed((1, D)),
            fixed((slots, 1)),
        ]
        + [anywhere] * 5,
        out_shape=[
            shape_of((slots, FF), low),
            shape_of((2, HALF_ROWS, D // 2), low),
            shape_of((SEGS, SEGS)),
            shape_of((8, D)),
            shape_of((1, D)),
            shape_of((slots, 1)),
            shape_of((slots, D), low),
            shape_of((slots, D)),
            shape_of((slots, D), low),
            shape_of((slots, D), low),
            shape_of((slots, D)),
        ],
        scratch_shapes=[
            pltpu.VMEM((PARTS, slots, D), low),
            pltpu.VMEM((slots, D), low),
            pltpu.VMEM((slots, D), low),
            pltpu.VMEM((slots, D), jnp.float32),
            pltpu.VMEM((slots, D), low),
            pltpu.VMEM((slots, D), low),
            pltpu.VMEM((slots, D), jnp.float32),
            pltpu.VMEM((slots, D), jnp.float32),
            pltpu.VMEM((slots, 1), jnp.float32),
            pltpu.VMEM((SEGS, D), jnp.float32),
            pltpu.VMEM((SEGS, D), low),
            pltpu.VMEM((2, SEGS, D), low),
            pltpu.SemaphoreType.DMA((5,)),
        ],
        compiler_params=params(),
        cost_estimate=cost(20e9, 40e6),
        name="middle",
    )(
        patches,
        att,
        tokens,
        *[weights] * 5,
        vectors,
        segments,
        cot_pair,
        cot_out,
    )


def head_sums(values):
    rows = lax.broadcasted_iota(jnp.int32, (GW, GW), 0)
    cols = lax.broadcasted_iota(jnp.int32, (GW, GW), 1)
    takes = (rows // PAIR == cols // PAIR) & (rows // HDIM != cols // HDIM)
    takes = takes.astype(jnp.float32).astype(jnp.bfloat16)
    sums = jnp.concatenate(
        [split_dot_left(values[:, at : at + GW], takes, NN) for at in range(0, D, GW)], axis=1
    )
    high = sums.astype(jnp.bfloat16).astype(jnp.float32)
    middle = (sums - high).astype(jnp.bfloat16).astype(jnp.float32)
    place = lax.broadcasted_iota(jnp.int32, (1, D), 1) % HDIM
    terms = jnp.where(place == 0, high, jnp.where(place == 1, middle, sums - high - middle))
    return jnp.where(place < 3, terms, 0.0).astype(jnp.bfloat16)


def feed_backward_kernel(
    low_ref,
    hidden_ref,
    inv1_ref,
    vectors_ref,
    slope_ref,
    wd_ref,
    wu_ref,
    wo_ref,
    start_in,
    normed1_in,
    att_in,
    inv_sum_in,
    exact_in,
    early_ref,
    dbu_ref,
    sums_ref,
    dres_out,
    datt_out,
    terms_out,
    total_ref,
    normed1_ref,
    att_ref,
    inv_sum_ref,
    exact_ref,
    grad_ref,
    datt_ref,
    terms_ref,
    sems,
):
    step = pl.program_id(0)
    slots = low_ref.shape[0]
    last = pl.num_programs(0) - 1
    loads = [
        pltpu.make_async_copy(src, dst, sems.at[i])
        for i, (src, dst) in enumerate(
            (
                (start_in, total_ref),
                (normed1_in, normed1_ref),
                (att_in, att_ref),
                (inv_sum_in, inv_sum_ref),
                (exact_in, exact_ref),
            )
        )
    ]

    @pl.when(step == 0)
    def _():
        for load in loads:
            load.start()

    @pl.when(step < last)
    def _():
        dact = dot(low_ref[...], wd_ref[...], NT)
        dpre = (dact * slope_ref[...].astype(jnp.float32)).astype(jnp.bfloat16)
        dbu_ref[...] = jnp.sum(dpre.astype(jnp.float32), axis=0, keepdims=True)
        store_halves(early_ref, dot(dpre, hidden_ref[...], TN))
        pl.when(step == 0)(loads[0].wait)
        total_ref[...] += dot(dpre, wu_ref[...], NN)

    @pl.when(step == last)
    def _():
        sums_ref[...] = jnp.zeros_like(sums_ref)
        for load in loads[1:]:
            load.wait()

        def rows_step(at):
            rows = tile_rows(at)
            grad = total_ref[rows, :]
            normed = normed1_ref[rows, :]
            sums_ref[0:1, :] += jnp.sum(grad * normed, axis=0, keepdims=True)
            sums_ref[1:2, :] += jnp.sum(grad, axis=0, keepdims=True)
            dres = normalize_back(grad * vectors_ref[0:1, :], normed, inv1_ref[rows, :])
            low = dres.astype(jnp.bfloat16)
            sums_ref[4:5, :] += jnp.sum(low.astype(jnp.float32), axis=0, keepdims=True)
            total_ref[rows, :] = dres
            grad_ref[rows, :] = low
            datt = dot(low, wo_ref[...], NN).astype(jnp.bfloat16).astype(jnp.float32)
            datt = (datt * inv_sum_ref[rows, :]).astype(jnp.bfloat16)
            datt_ref[rows, :] = datt
            terms_ref[rows, :] = head_sums(datt.astype(jnp.float32) * exact_ref[rows, :])

        pl.loop(0, slots // TILE)(rows_step)
        sends = [
            pltpu.make_async_copy(src, dst, sems.at[5 + i])
            for i, (src, dst) in enumerate(
                ((total_ref, dres_out), (datt_ref, datt_out), (terms_ref, terms_out))
            )
        ]
        for send in sends:
            send.start()
        store_halves(early_ref, dot(grad_ref[...], att_ref[...], TN))
        for send in sends:
            send.wait()


def feed_backward(low, start, normed1, inv1, hidden, slope, att, inv_sum, exact, vectors, weights):
    slots = low.shape[0]
    last = PARTS - 1
    full = once((slots, D))
    anywhere = pl.BlockSpec(memory_space=pl.ANY)

    def at(i):
        return jnp.minimum(i, last - 1)

    return pl.pallas_call(
        feed_backward_kernel,
        grid=(PARTS,),
        in_specs=[
            full,
            full,
            once((slots, 1)),
            once(vectors.shape),
            pl.BlockSpec((slots, D), lambda i: (0, at(i))),
            pl.BlockSpec((D, D), lambda i: (4 + PARTS + at(i), 0)),
            pl.BlockSpec((D, D), lambda i: (4 + at(i), 0)),
            square(3),
        ]
        + [anywhere] * 5,
        out_specs=[
            pl.BlockSpec(HALF_BLOCK, lambda i: (0, jnp.where(i == last, 0, 1 + i), 0)),
            pl.BlockSpec((1, D), lambda i: (0, at(i))),
            fixed((8, D)),
        ]
        + [anywhere] * 3,
        out_shape=[
            shape_of((2, FF, D // 2), jnp.bfloat16),
            shape_of((1, FF - D)),
            shape_of((8, D)),
            shape_of((slots, D)),
            shape_of((slots, D), jnp.bfloat16),
            shape_of((slots, D), jnp.bfloat16),
        ],
        scratch_shapes=[
            pltpu.VMEM((slots, D), jnp.float32),
            pltpu.VMEM((slots, D), jnp.float32),
            pltpu.VMEM((slots, D), jnp.bfloat16),
            pltpu.VMEM((slots, D), jnp.float32),
            pltpu.VMEM((slots, D), jnp.float32),
            pltpu.VMEM((slots, D), jnp.bfloat16),
            pltpu.VMEM((slots, D), jnp.bfloat16),
            pltpu.VMEM((slots, D), jnp.bfloat16),
            pltpu.SemaphoreType.DMA((8,)),
        ],
        compiler_params=params(),
        cost_estimate=cost(17e9, 40e6),
        name="feed_backward",
    )(low, hidden, inv1, vectors, slope, weights, weights, weights, start, normed1, att, inv_sum, exact)


def attention_backward_kernel(
    patches_ref,
    grown_ref,
    datt_ref,
    terms_ref,
    v_ref,
    k_ref,
    q_ref,
    box_row_ref,
    dqkv_ref,
    dcoef_ref,
    box_col_ref,
    bucket0_ref,
    bucket1_ref,
    dscore_ref,
):
    pair = pl.program_id(0)
    slots = datt_ref.shape[0]
    low = jnp.bfloat16
    live_row = lax.broadcasted_iota(jnp.int32, (1, slots), 1) < TEXT + patches_ref[0]

    @pl.when(pair == 0)
    def _():
        write_buckets(box_row_ref, box_col_ref, (bucket0_ref, bucket1_ref), live_row)

    query_t = q_ref[...].astype(jnp.float32).T.astype(low)
    key_t = (k_ref[...].astype(jnp.float32) * HDIM ** (-0.5)).T
    key_t = jnp.where(live_row, key_t, 0.0).astype(low)
    datt_t = datt_ref[...].astype(jnp.float32).T.astype(low)
    lanes = lax.broadcasted_iota(jnp.int32, (1, PAIR), 1)
    second = lanes >= HDIM
    masks = [jnp.where(second, 0.0, 1.0), jnp.where(second, 1.0, 0.0)]
    masks = [mask.astype(low) for mask in masks]
    dcoef_ref[...] = jnp.zeros_like(dcoef_ref)
    leads = []
    values = []
    for j in range(2):
        at = HDIM * (1 - j)
        minus = jnp.where((lanes >= at) & (lanes < at + 3), -1.0, 0.0).astype(low)
        leads.append(datt_ref[...] * masks[j] + terms_ref[...] * masks[1 - j])
        values.append(v_ref[...] * masks[j] + minus)

    for j in range(2):
        head_rows = slice(j * HDIM, (j + 1) * HDIM)
        for step in range(slots // TILE):
            rows = slice(step * TILE, (step + 1) * TILE)
            diff = dot(leads[j][rows], values[j], NT)
            dscore = grown_ref[j, rows, :].astype(jnp.float32) * diff
            dscore_ref[j, rows, :] = dscore.astype(low)
            dcoef_ref[j, 0:1, :] += jnp.sum(dscore * bucket0_ref[rows, :], axis=0, keepdims=True)
            dcoef_ref[j, 1:2, :] += jnp.sum(dscore * bucket1_ref[rows, :], axis=0, keepdims=True)
        dqkv_ref[0, head_rows] = dot(key_t[head_rows], dscore_ref[j], NT).astype(low)
        dkey = dot(query_t[head_rows], dscore_ref[j], NN) * (1.0 / LOG2E)
        dqkv_ref[1, head_rows] = jnp.where(live_row, dkey, 0.0).astype(low)
        dvalue = dot(datt_t[head_rows], grown_ref[j], NN)
        dqkv_ref[2, head_rows] = jnp.where(live_row, dvalue, 0.0).astype(low)


def attention_backward(grown, datt, terms, q, k, v, boxes, patches):
    slots = datt.shape[0]
    pair_block = pl.BlockSpec((slots, PAIR), lambda h: (0, h))
    return pl.pallas_call(
        attention_backward_kernel,
        grid=(HEADS // 2,),
        in_specs=[
            pl.BlockSpec(memory_space=pltpu.SMEM),
            pl.BlockSpec((2, slots, slots), lambda h: (h, 0, 0)),
        ]
        + [pair_block] * 5
        + [fixed((2, slots))],
        out_specs=[
            pl.BlockSpec((3, PAIR, slots), lambda h: (0, h, 0)),
            pl.BlockSpec((2, 2, slots), lambda h: (h, 0, 0)),
        ],
        out_shape=[
            shape_of((3, D, slots), jnp.bfloat16),
            shape_of((HEADS, 2, slots)),
        ],
        scratch_shapes=[pltpu.VMEM((slots, 8), jnp.int32)]
        + [pltpu.VMEM((slots, slots), jnp.float32)] * 2
        + [pltpu.VMEM((2, slots, slots), jnp.bfloat16)],
        compiler_params=params(),
        cost_estimate=cost(15e9, 40e6),
        name="attention_backward",
    )(patches, grown, datt, terms, v, k, q, boxes)


def qkv_weights_kernel(dqkv_ref, tokens_ref, early_ref, sums_ref):
    part = dqkv_ref[0]
    store_halves(early_ref, dot(part, tokens_ref[...], NN))
    sums_ref[0] = dot(jnp.ones((8, part.shape[1]), jnp.bfloat16), part, NT)


def qkv_weights(dqkv, tokens):
    slots = tokens.shape[0]
    return pl.pallas_call(
        qkv_weights_kernel,
        grid=(3,),
        in_specs=[
            pl.BlockSpec((1, D, slots), lambda i: (i, 0, 0)),
            fixed((slots, D)),
        ],
        out_specs=[
            pl.BlockSpec(HALF_BLOCK, lambda i: (0, i, 0)),
            pl.BlockSpec((1, 8, D), lambda i: (i, 0, 0)),
        ],
        out_shape=[shape_of((2, 3 * D, D // 2), jnp.bfloat16), shape_of((3, 8, D))],
        compiler_params=params(),
        cost_estimate=cost(3.6e9, 10e6),
        name="qkv_weights",
    )(dqkv, tokens)


def token_gradient_kernel(dqkv_ref, weight_ref, dres_ref, grad_ref):
    total = dres_ref[...]
    for part in range(3):
        total = total + dot(dqkv_ref[part], weight_ref[part * D : (part + 1) * D, :], TN)
    grad_ref[...] = total.astype(jnp.bfloat16)


def token_gradient(dqkv, weights, dres):
    slots = dres.shape[0]
    tile = pl.BlockSpec((TILE, D), lambda i: (i, 0))
    return pl.pallas_call(
        token_gradient_kernel,
        grid=(slots // TILE,),
        in_specs=[
            pl.BlockSpec((3, D, TILE), lambda i: (0, 0, i)),
            pl.BlockSpec((3 * D, D), lambda i: (0, 0), pipeline_mode=pl.Buffered(1)),
            tile,
        ],
        out_specs=tile,
        out_shape=shape_of((slots, D), jnp.bfloat16),
        compiler_params=params(),
        cost_estimate=cost(3.6e9, 12e6),
        name="token_gradient",
    )(dqkv, weights, dres)


def page_step(
    tokens, boxes, segments, patches, cot_out, cot_pair, pieces, layout, vectors, box_coef
):
    (q, k, v, grown, att, inv_sum, exact), weights = attention_forward(
        tokens, pieces, layout, vectors, boxes, patches, box_coef
    )
    slope, late, pair_scores, sums2, dbu_tail, inv1, mixed, normed1, hidden, low, start = middle(
        att, tokens, weights, vectors, segments, cot_pair, cot_out, patches
    )
    early, dbu_head, sums1, dres, datt, terms = feed_backward(
        low, start, normed1, inv1, hidden, slope, att, inv_sum, exact, vectors, weights
    )
    dqkv, dcoef = attention_backward(grown, datt, terms, q, k, v, boxes, patches)
    dqkv, middle_rows = lax.optimization_barrier((dqkv, core_sum(early)))
    first_rows, bias_sums = qkv_weights(dqkv, tokens)
    first_rows, late = lax.optimization_barrier((first_rows, scatter_dp(late)))
    token_grad = token_gradient(dqkv, weights, dres)
    early, late, token_grad = scatter_first(first_rows, early, middle_rows, scatter_grid(late), token_grad)
    vector_part = jnp.concatenate(
        [
            sums1[:2],
            bias_sums[0, :1],
            bias_sums[2, :1],
            sums1[4:5],
            sums2[:3],
            dbu_head.reshape(FF // D - 1, D),
            dbu_tail,
        ],
        axis=0,
    )
    coef_part = jnp.sum(dcoef, axis=2).T
    return (mixed, pair_scores, token_grad, early, late, vector_part, coef_part)


def exchange_sum(values):
    steps = [(axis, 1 << bit) for axis in ("grid", "dp") for bit in range(lax.axis_size(axis).bit_length() - 1)]
    steps.sort(key=lambda step: step != ("dp", 1))
    for axis, reach in steps:
        values = values + lax.ppermute(values, axis, [(i, i ^ reach) for i in range(lax.axis_size(axis))])
    return values


def scatter_dp(halves):
    return lax.psum_scatter(
        halves.reshape(-1, D // 2), "dp", scatter_dimension=0, tiled=True
    )


SPLIT_AT = 2 * HALF_ROWS // 4 - 3 * D


def by_links():
    return (lax.axis_size("dp"), lax.axis_size("grid")) == (8, 4)


def exchange(values, reach):
    return lax.ppermute(values, "dp", [(i, i ^ reach) for i in range(lax.axis_size("dp"))])


def add_low(a, b):
    return (a.astype(jnp.float32) + b.astype(jnp.float32)).astype(jnp.bfloat16)


def core_rows(take):
    core = lax.axis_index("dp") % 2
    rows = add_low(take(core), exchange(take(1 - core), 1))
    return rows.reshape(2, lax.axis_size("grid"), -1, D // 2)


def core_sum(rest):
    if not by_links():
        return rest
    count = HALF_ROWS // 4
    return core_rows(lambda core: lax.dynamic_slice_in_dim(rest, SPLIT_AT + core * count, count, 1))


def scatter_first(first_rows, rest, summed, late, token_grad):
    if not by_links():
        return scatter_dp(jnp.concatenate([first_rows, rest], axis=1)), late, token_grad
    count = HALF_ROWS // 4
    ends = jnp.concatenate([first_rows[:, count:], rest[:, :SPLIT_AT]], axis=1)
    zero = core_rows(lambda core: jnp.where(core == 0, first_rows[:, :count], ends))
    place = lax.axis_index("dp")
    x, y = place // 2 % 2, place // 4
    both = jnp.stack([zero, summed])
    half = zero.shape[1] // 2

    def pick(values, at, axis=0):
        return lax.dynamic_index_in_dim(values, at, axis, keepdims=False)

    by_x, by_y = both[:, :, :half], both[:, :, half:]
    sent_x = exchange(pick(by_x, 1 - x), 2)
    sent_y = exchange(pick(by_y, 1 - y, 1), 4)
    sent_x, sent_y, late, token_grad = lax.optimization_barrier((sent_x, sent_y, late, token_grad))
    by_x = add_low(pick(by_x, x), sent_x)
    by_y = add_low(pick(by_y, y, 1), sent_y)
    sent_x = exchange(pick(by_y, 1 - x), 2)
    sent_y = exchange(pick(by_x, 1 - y), 4)
    by_x = add_low(pick(by_x, y), sent_y)
    by_y = add_low(pick(by_y, x), sent_x)
    return jnp.concatenate([by_x, by_y]).reshape(-1, D // 2), late, token_grad


def scatter_grid(rows):
    size = lax.axis_size("grid")
    place = lax.axis_index("grid")
    blocks = rows.reshape(size, -1, D // 2)

    def block(at):
        return lax.dynamic_index_in_dim(blocks, at % size, 0, keepdims=False)

    got = [
        lax.ppermute(block(place + s), "grid", [(i, (i + s) % size) for i in range(size)])
        for s in range(1, size)
    ]
    return sum((g.astype(jnp.float32) for g in got), block(place).astype(jnp.float32))


def swap_halves(first, second):
    size = lax.axis_size("dp")
    low = lax.axis_index("dp") < size // 2
    other = lax.ppermute(
        jnp.where(low, second, first).astype(jnp.bfloat16), "dp", [(i, (i + size // 2) % size) for i in range(size)]
    ).astype(jnp.float32)
    kept = jnp.where(low, first, second)
    return jnp.concatenate([jnp.where(low, kept, other), jnp.where(low, other, kept)], axis=1)


def gather_weights(shard, ready):
    dp_size, grid_size = lax.axis_size("dp"), lax.axis_size("grid")
    rows = shard.shape[0]
    if (dp_size, grid_size) != (8, 4) or rows != 336:
        return [lax.all_gather(shard, ("dp", "grid"), axis=0, tiled=True)], None
    barrier = lax.optimization_barrier

    def over(values, reach):
        return lax.ppermute(values, "dp", [(i, i ^ reach) for i in range(dp_size)])

    def up(values, reach):
        return lax.ppermute(values, "grid", [(i, (i + reach) % grid_size) for i in range(grid_size)])

    cuts = (0, *CUTS)
    one, two = (shard[a:b] for a, b in zip(cuts, cuts[1:]))
    rest = lax.all_gather(shard[cuts[-1] :], ("dp", "grid"), axis=0)
    hops = (1, 2, 3)
    one_grid = jnp.stack([one] + [up(one, s) for s in hops])
    one_grid, two, *_ = barrier((one_grid, two, *ready))
    one_x, one_y = over(one_grid, 2), over(one_grid, 4)
    two_grid = jnp.stack([two] + [up(two, s) for s in hops])
    one_x, one_y, two_grid = barrier((one_x, one_y, two_grid))
    two_x, two_y = over(two_grid, 2), over(two_grid, 4)
    two_x, two_y = barrier((two_x, two_y))
    xy = over(jnp.concatenate([one_y[:2], two_y[:2]], axis=1), 2)
    yx = over(jnp.concatenate([one_x[2:], two_x[2:]], axis=1), 4)
    own = [one_grid, one_x, one_y, two_grid, two_x, two_y, xy, yx]
    every = tuple(range(grid_size))
    layout = [(cuts[part], [(r, s) for s in every]) for part in (0, 1) for r in (0, 2, 4)]
    layout += [(0, [(6, s) for s in (0, 1)]), (0, [(6, s) for s in (2, 3)])]
    layout += [(start, [(r ^ 1, s) for r, s in entries]) for start, entries in layout]
    pieces = own + [over(piece, 1) for piece in own]
    return pieces + [rest], layout + [(cuts[-1], None)]


CUTS = (96, 208)


def momentum_step(grad, param, moment, average, rate):
    new_moment = 0.5 * moment + grad
    new_param = param - rate * (grad + 0.5 * new_moment)
    new_average = 0.5 * average + 0.5 * new_param
    return (new_moment, new_param, new_average)


def on_device(
    tokens,
    boxes,
    segments,
    patches,
    cot_out,
    cot_pair,
    weights,
    weight_momentum,
    weight_average,
    vectors,
    vector_momentum,
    vector_average,
    box_coef,
    coef_momentum,
    coef_average,
):
    axes = ("dp", "grid")
    page_count, slot_count = tokens.shape[:2]
    device_count = lax.axis_size(axes)
    segments = jnp.pad(segments, ((0, 0), (0, slot_count - segments.shape[1])), constant_values=SEGS)
    pieces, layout = gather_weights(weights.astype(jnp.bfloat16), (segments,))
    pages = [
        page_step(
            tokens[p],
            boxes[p],
            segments[p : p + 1],
            patches[p : p + 1],
            cot_out[p],
            cot_pair[p],
            pieces,
            layout,
            vectors,
            box_coef,
        )
        for p in range(page_count)
    ]
    mixed, pair_scores, token_grad = (jnp.stack([page[i] for page in pages]) for i in range(3))
    early, late = (sum(page[i] for page in pages) for i in (3, 4))
    small = sum(
        jnp.concatenate([page[5], jnp.pad(page[6].reshape(1, 2 * HEADS), ((0, 3), (0, D - 2 * HEADS)))], axis=0)
        for page in pages
    )
    late_rows = late
    early_rows = scatter_grid(early)
    small = exchange_sum(small)
    weight_grad = swap_halves(early_rows, late_rows)
    vector_rows = vectors.shape[0]
    vector_grad = small[:vector_rows]
    coef_grad = small[vector_rows, : 2 * HEADS].reshape(2, HEADS)
    rate_scale = (device_count * page_count * slot_count) ** (-0.5)
    new_weight_momentum, new_weights, new_weight_average = momentum_step(
        weight_grad, weights, weight_momentum, weight_average, 0.1 * rate_scale
    )
    new_vector_momentum, new_vectors, new_vector_average = momentum_step(
        vector_grad, vectors, vector_momentum, vector_average, 0.1 * rate_scale
    )
    new_coef_momentum, new_coef, new_coef_average = momentum_step(
        coef_grad, box_coef, coef_momentum, coef_average, 0.01 * rate_scale
    )
    return (
        mixed,
        pair_scores,
        token_grad,
        weight_grad,
        new_weights,
        new_weight_momentum,
        new_weight_average,
        new_weights.astype(jnp.bfloat16),
        vector_grad,
        new_vectors,
        new_vector_momentum,
        new_vector_average,
        coef_grad,
        new_coef,
        new_coef_momentum,
        new_coef_average,
    )


def solution(mesh):
    rows = P(("dp", "grid"))
    return jax.shard_map(
        on_device,
        mesh=mesh,
        in_specs=(rows,) * 9 + (P(),) * 6,
        out_specs=(rows,) * 8 + (P(),) * 8,
        check_vma=False,
    )
```

```python
import functools
import math

import jax
import jax.numpy as jnp
from jax import lax
from jax.experimental import pallas as pl
from jax.experimental.pallas import tpu as pltpu
from jax.sharding import PartitionSpec as P

D = 768
HEADS = 12
HDIM = 64
FF = 3072
TEXT = 448
SEGS = 64
PAIR = 2 * HDIM
GW = 2 * PAIR
LOG2E = math.log2(math.e)
TILE = 256
WIDE = 512
VMEM_LIMIT = 60 * 1024 * 1024
NT = (((1,), (1,)), ((), ()))
NN = (((1,), (0,)), ((), ()))
TN = (((0,), (0,)), ((), ()))

def dot(a, b, dims):
    return lax.dot_general(a, b, dims, preferred_element_type=jnp.float32)


def split_dot(exact, b, dims):
    high = b.astype(jnp.bfloat16)
    rest = b - high.astype(jnp.float32)
    middle = rest.astype(jnp.bfloat16)
    last = (rest - middle.astype(jnp.float32)).astype(jnp.bfloat16)
    return dot(exact, high, dims) + dot(exact, middle, dims) + dot(exact, last, dims)


def params():
    return pltpu.CompilerParams(vmem_limit_bytes=VMEM_LIMIT)


def cost(flops, nbytes):
    return pl.CostEstimate(flops=int(flops), bytes_accessed=int(nbytes), transcendentals=0)


def tile_rows(step):
    return pl.ds(pl.multiple_of(step * TILE, TILE), TILE)


def wide_rows(step):
    return pl.ds(pl.multiple_of(step * WIDE, WIDE), WIDE)


def fixed(shape):
    return pl.BlockSpec(shape, lambda *_: (0,) * len(shape))


def once(shape):
    return pl.BlockSpec(shape, lambda *_: (0,) * len(shape), pipeline_mode=pl.Buffered(1))


def shape_of(dims, dtype=jnp.float32):
    return jax.ShapeDtypeStruct(dims, dtype)


HALF_BLOCK = (2, D, D // 2)
HALF_ROWS = (3 * D + D + FF + FF + 2 * D) // 2


def square(at):
    return pl.BlockSpec((D, D), lambda i: (at, 0), pipeline_mode=pl.Buffered(1))


def write_buckets(box_row_ref, box_col_ref, bucket_refs, live_row=None):
    box_col_ref[...] = jnp.tile(box_row_ref[...].astype(jnp.float32), (4, 1)).T.astype(jnp.int32)

    def fill(step):
        rows = tile_rows(step)
        for c in range(2):
            spread = jnp.abs(box_col_ref[rows, c : c + 1] - box_row_ref[c : c + 1, :])
            bucket = jnp.minimum(spread >> 5, 31).astype(jnp.float32)
            bucket_refs[c][rows, :] = bucket if live_row is None else jnp.where(live_row, bucket, 0.0)

    pl.loop(0, box_row_ref.shape[1] // TILE)(fill)


def place_weights(layout, piece_refs, weight_ref, out_ref, sems, meanwhile):
    step = pl.program_id(0)
    place = lax.axis_index("grid")
    mine = lax.axis_index("dp")
    depth = lax.axis_size("grid")
    shard = weight_ref.shape[0] // (lax.axis_size("dp") * depth)
    by_owner = {}
    count = 0
    for ref, (start, entries) in zip(piece_refs, layout):
        rows = ref.shape[1]
        if entries is None:
            every = [(owner, "far") for owner in range(ref.shape[0])]
        else:
            every = [
                ((mine ^ over) * depth + lax.rem(place + depth - back, depth), over)
                for over, back in entries
            ]
        for at, (owner, over) in enumerate(every):
            if over == "far" and owner * shard < 3 * D:
                over = "near"
            target = weight_ref.at[pl.ds(pl.multiple_of(owner * shard + start, 16), rows)]
            by_owner.setdefault(over, []).append(pltpu.make_async_copy(ref.at[at], target, sems.at[count]))
            count += 1
    out = pltpu.make_async_copy(weight_ref, out_ref, sems.at[count])
    needed = -(-3 * D // (shard * depth))

    def each(first, action):
        for over, copies in by_owner.items():
            if over in ("near", "far"):
                if first == (over == "near"):
                    for copy in copies:
                        action(copy)
                continue
            chosen = (mine ^ over) < needed

            @pl.when(chosen if first else jnp.logical_not(chosen))
            def _():
                for copy in copies:
                    action(copy)

    @pl.when(step == 0)
    def _():
        each(True, lambda copy: copy.start())
        meanwhile()
        each(True, lambda copy: copy.wait())
        each(False, lambda copy: copy.start())

    @pl.when(step == 1)
    def _():
        each(False, lambda copy: copy.wait())
        out.start()

    @pl.when(step == pl.num_programs(0) - 1)
    def _():
        out.wait()


def attention_forward_kernel(
    layout,
    pieces,
    coef_ref,
    patches_ref,
    tokens_ref,
    vectors_ref,
    box_row_ref,
    *refs,
):
    piece_refs, refs = refs[:pieces], refs[pieces:]
    q_ref, k_ref, v_ref, grown_ref, att_ref, inv_ref, exact_ref = refs[:7]
    box_col_ref, bucket0_ref, bucket1_ref, live_ref, value_ref, size_ref, weight_ref, sems = refs[-8:]
    pair = pl.program_id(0)
    slots = tokens_ref.shape[0]
    side = pl.ds(pl.multiple_of(pair % 2 * PAIR, PAIR), PAIR)
    low = jnp.bfloat16

    def prepare():
        write_buckets(box_row_ref, box_col_ref, (bucket0_ref, bucket1_ref))
        slot = lax.broadcasted_iota(jnp.int32, (slots, PAIR), 0)
        live_ref[...] = (slot < TEXT + patches_ref[0]).astype(jnp.float32).astype(low)

    if layout is None:

        @pl.when(pair == 0)
        def _():
            load = pltpu.make_async_copy(piece_refs[0].at[pl.ds(0, 3 * D)], weight_ref, sems.at[0])
            load.start()
            prepare()
            load.wait()

    else:
        place_weights(layout, piece_refs, weight_ref, refs[7], sems, prepare)

    @pl.when(pair % 2 == 0)
    def _():
        def weight(at):
            return weight_ref[pl.ds(pl.multiple_of(at * D + pair // 2 * GW, GW), GW), :]

        query = (dot(tokens_ref[...], weight(0), NT) + vectors_ref[2:3, :]) * (
            LOG2E * HDIM ** (-0.5)
        )
        key = dot(tokens_ref[...], weight(1), NT)
        q_ref[...] = query.astype(low)
        k_ref[...] = key.astype(low)
        v_ref[...] = (dot(tokens_ref[...], weight(2), NT) + vectors_ref[3:4, :]).astype(low)
        of_head = lax.broadcasted_iota(jnp.int32, (GW, PAIR), 0) // HDIM
        ones = (of_head == lax.broadcasted_iota(jnp.int32, (GW, PAIR), 1)).astype(low)
        query_size = jnp.max(dot((query * query).astype(low), ones, NN), axis=0, keepdims=True)
        key_size = jnp.max(dot((key * key).astype(low), ones, NN), axis=0, keepdims=True)
        size_ref[0] = jnp.max(query_size * key_size)

    second = lax.broadcasted_iota(jnp.int32, (1, PAIR), 1) >= HDIM
    masks = [jnp.where(second, 0.0, 1.0), jnp.where(second, 1.0, 0.0)]
    masks = [mask.astype(low) for mask in masks]
    value = v_ref[:, side] * live_ref[...]
    for j in range(2):
        value_ref[j] = value * masks[j] + live_ref[...] * masks[1 - j]
    coefs = [[coef_ref[c, 2 * pair + j] * LOG2E for c in range(2)] for j in range(2)]
    spread = [31.0 * (jnp.abs(c[0]) + jnp.abs(c[1])) for c in coefs]
    room = 57.0 - jnp.maximum(spread[0], spread[1])
    small = (room > 0) & (1.03 * size_ref[0] <= room * room)

    def rows_step(step, shifted):
        rows = tile_rows(step)
        query = q_ref[rows, side]
        bucket0 = bucket0_ref[rows, :]
        bucket1 = bucket1_ref[rows, :]
        found = []
        for j in range(2):
            score = dot(query * masks[j], k_ref[:, side], NT)
            score = score + coefs[j][0] * bucket0 + coefs[j][1] * bucket1
            if shifted:
                slot = lax.broadcasted_iota(jnp.int32, (1, slots), 1)
                score = jnp.where(slot < TEXT + patches_ref[0], score, -1e30)
                score = score - jnp.max(score, axis=1, keepdims=True)
            grown = jnp.exp2(score).astype(low)
            grown_ref[j, rows, :] = grown
            found.append(dot(grown, value_ref[j], NN))
        total = jnp.where(second, found[0], found[1])
        inv = 1.0 / pltpu.roll(total, HDIM, 1)
        exact = jnp.where(second, found[1], found[0]) * inv
        exact_ref[rows, :] = exact
        att_ref[rows, :] = exact.astype(low)
        inv_ref[rows, :] = inv

    @pl.when(small)
    def _():
        pl.loop(0, slots // TILE, unroll=4)(lambda step: rows_step(step, False))

    @pl.when(jnp.logical_not(small))
    def _():
        pl.loop(0, slots // TILE)(lambda step: rows_step(step, True))


def attention_forward(tokens, pieces, layout, vectors, boxes, patches, box_coef):
    slots = tokens.shape[0]
    smem = pl.BlockSpec(memory_space=pltpu.SMEM)
    anywhere = pl.BlockSpec(memory_space=pl.ANY)
    lane_block = pl.BlockSpec((slots, GW), lambda h: (0, h // 2))
    pair_block = pl.BlockSpec((slots, PAIR), lambda h: (0, h))
    low = shape_of((slots, D), jnp.bfloat16)
    wide = shape_of((slots, D))
    weights = shape_of((2 * HALF_ROWS, D), jnp.bfloat16)
    copies = 0 if layout is None else sum(
        piece.shape[0] if entries is None else len(entries) for piece, (_, entries) in zip(pieces, layout)
    )
    out = pl.pallas_call(
        functools.partial(attention_forward_kernel, layout, len(pieces)),
        grid=(HEADS // 2,),
        in_specs=[
            smem,
            smem,
            fixed((slots, D)),
            pl.BlockSpec((vectors.shape[0], GW), lambda h: (0, h // 2)),
            fixed((2, slots)),
        ]
        + [anywhere] * len(pieces),
        out_specs=[lane_block] * 3
        + [pl.BlockSpec((2, slots, slots), lambda h: (h, 0, 0))]
        + [pair_block] * 3
        + [anywhere] * bool(copies),
        out_shape=[low] * 3
        + [shape_of((HEADS, slots, slots), jnp.bfloat16), low, wide, wide]
        + [weights] * bool(copies),
        scratch_shapes=[pltpu.VMEM((slots, 8), jnp.int32)]
        + [pltpu.VMEM((slots, slots), jnp.float32)] * 2
        + [
            pltpu.VMEM((slots, PAIR), jnp.bfloat16),
            pltpu.VMEM((2, slots, PAIR), jnp.bfloat16),
            pltpu.SMEM((1,), jnp.float32),
            pltpu.VMEM(weights.shape if copies else (3 * D, D), jnp.bfloat16),
            pltpu.SemaphoreType.DMA((copies + 1,)),
        ],
        compiler_params=params(),
        cost_estimate=cost(10e9, 40e6),
        name="attention_forward",
    )(box_coef, patches, tokens, vectors, boxes, *pieces)
    return out[:7], out[7] if copies else pieces[0]


def normalize(values):
    centered = values - jnp.mean(values, axis=-1, keepdims=True)
    inv_std = lax.rsqrt(jnp.mean(centered * centered, axis=-1, keepdims=True) + 1e-05)
    return (centered * inv_std, inv_std)


def normalize_back(grad_normed, normed, inv_std):
    first_mean = jnp.mean(grad_normed, axis=-1, keepdims=True)
    second_mean = jnp.mean(grad_normed * normed, axis=-1, keepdims=True)
    return inv_std * (grad_normed - first_mean - normed * second_mean)


def gelu_pair(values):
    below = 0.5 + 0.5 * lax.erf(values * (0.5**0.5))
    bell = jnp.exp(values * values * -0.5) * (0.5 / math.pi) ** 0.5
    return (values * below, below + values * bell)


def split_dot_left(a, exact, dims):
    high = a.astype(jnp.bfloat16)
    rest = a - high.astype(jnp.float32)
    middle = rest.astype(jnp.bfloat16)
    last = (rest - middle.astype(jnp.float32)).astype(jnp.bfloat16)
    return dot(high, exact, dims) + dot(middle, exact, dims) + dot(last, exact, dims)


def store_halves(ref, values):
    ref[0] = values[:, : D // 2].astype(jnp.bfloat16)
    ref[1] = values[:, D // 2 :].astype(jnp.bfloat16)


PARTS = FF // D
NORM_STEP = PARTS + 1
TAIL_STEP = PARTS + 2
PAIR_STEP = TAIL_STEP + PARTS + 1


def middle_kernel(
    patches_ref,
    att_ref,
    tokens_ref,
    wo_ref,
    wu_ref,
    wd_ref,
    wl_ref,
    wr_ref,
    vectors_ref,
    segment_row_ref,
    cot_pair_ref,
    cot_ref,
    slope_ref,
    late_ref,
    pair_ref,
    sums_ref,
    dbu_ref,
    inv1_ref,
    mixed_out,
    normed1_out,
    hidden_out,
    low_out,
    dres_out,
    act_ref,
    tail_ref,
    mixed_ref,
    normed1_ref,
    hidden_ref,
    low_ref,
    total_ref,
    normed2_ref,
    inv2_ref,
    pool_ref,
    pooled_ref,
    dpair_ref,
    sems,
):
    step = pl.program_id(0)
    slots = att_ref.shape[0]
    tiles = slots // TILE
    outs = (
        (normed1_ref, normed1_out),
        (hidden_ref, hidden_out),
        (mixed_ref, mixed_out),
        (low_ref, low_out),
        (total_ref, dres_out),
    )
    sends = [pltpu.make_async_copy(src, dst, sems.at[i]) for i, (src, dst) in enumerate(outs)]

    @pl.when(step == 0)
    def _():

        @pl.loop(0, tiles)
        def _(at):
            rows = tile_rows(at)
            branch = dot(att_ref[rows, :], wo_ref[...], NT) + vectors_ref[4:5, :]
            normed, inv = normalize(tokens_ref[rows, :].astype(jnp.float32) + branch)
            hidden = normed * vectors_ref[0:1, :] + vectors_ref[1:2, :]
            normed1_ref[rows, :] = normed
            inv1_ref[rows, :] = inv
            hidden_ref[rows, :] = hidden.astype(jnp.bfloat16)
            total_ref[rows, :] = hidden + vectors_ref[7:8, :]

        sends[0].start()
        sends[1].start()

    @pl.when((step > 0) & (step <= PARTS))
    def _():
        bias = vectors_ref[pl.ds(7 + step, 1), :]

        for at in range(tiles):
            rows = slice(at * TILE, (at + 1) * TILE)
            act, slope = gelu_pair(dot(hidden_ref[rows, :], wu_ref[...], NT) + bias)
            act = act.astype(jnp.bfloat16)
            act_ref[step - 1, rows, :] = act
            slope_ref[rows, :] = slope.astype(jnp.bfloat16)
            total_ref[rows, :] += dot(act, wd_ref[...], NN)

    @pl.when(step == NORM_STEP)
    def _():
        numbers = lax.broadcasted_iota(jnp.int32, (SEGS, 1), 0)
        slot_row = lax.broadcasted_iota(jnp.int32, (1, slots), 1)
        member = (segment_row_ref[...] == numbers) & (slot_row < TEXT)
        counted = jnp.sum(member.astype(jnp.float32), axis=1, keepdims=True)
        pool_ref[...] = jnp.zeros_like(pool_ref)

        @pl.loop(0, tiles)
        def _(at):
            rows = tile_rows(at)
            normed, inv = normalize(total_ref[rows, :])
            inv2_ref[rows, :] = inv
            output = normed * vectors_ref[5:6, :] + vectors_ref[6:7, :]
            normed2_ref[rows, :] = normed
            mixed_ref[rows, :] = output.astype(jnp.bfloat16)

            @pl.when(at * TILE < TEXT)
            def _():
                slot = at * TILE + lax.broadcasted_iota(jnp.int32, (1, TILE), 1)
                belongs = (segment_row_ref[:, rows] == numbers) & (slot < TEXT)
                pool_ref[...] += split_dot(belongs.astype(jnp.bfloat16), output, NN)

        sends[2].start()
        pooled = (pool_ref[...] / counted).astype(jnp.bfloat16)
        left_weight = wl_ref[...]
        right_weight = wr_ref[...]
        scale = D ** (-0.5)
        left = dot(pooled, left_weight, NT).astype(jnp.bfloat16)
        right = dot(pooled, right_weight, NT).astype(jnp.bfloat16)
        pair_ref[...] = dot(left, right, NT) * scale
        cot = cot_pair_ref[...]
        grad_left = (split_dot_left(cot, right, NN) * scale).astype(jnp.bfloat16)
        grad_right = (split_dot_left(cot, left, TN) * scale).astype(jnp.bfloat16)
        grad_pooled = dot(grad_left, left_weight, NN) + dot(grad_right, right_weight, NN)
        spread = grad_pooled / counted
        pooled_ref[...] = pooled
        dpair_ref[0] = grad_left
        dpair_ref[1] = grad_right
        pool_ref[...] = spread
        sums_ref[...] = jnp.zeros_like(sums_ref)

        @pl.loop(0, tiles)
        def _(at):
            rows = tile_rows(at)
            slot = at * TILE + lax.broadcasted_iota(jnp.int32, (TILE, 1), 0)
            live = (slot < TEXT + patches_ref[0]).astype(jnp.float32)
            slot_of = at * TILE + lax.broadcasted_iota(jnp.int32, (1, TILE), 1)
            belongs = (segment_row_ref[:, rows] == numbers) & (slot_of < TEXT)
            grad = cot_ref[rows, :].astype(jnp.float32) * live
            grad = grad + split_dot(belongs.astype(jnp.bfloat16), pool_ref[...], TN)
            normed = normed2_ref[rows, :]
            sums_ref[0:1, :] += jnp.sum(grad * normed, axis=0, keepdims=True)
            sums_ref[1:2, :] += jnp.sum(grad, axis=0, keepdims=True)
            dres = normalize_back(grad * vectors_ref[5:6, :], normed, inv2_ref[rows, :])
            low = dres.astype(jnp.bfloat16)
            sums_ref[2:3, :] += jnp.sum(low.astype(jnp.float32), axis=0, keepdims=True)
            total_ref[rows, :] = dres
            low_ref[rows, :] = low

        sends[3].start()

    @pl.when(step == TAIL_STEP)
    def _():
        dbu_ref[...] = jnp.zeros_like(dbu_ref)

        @pl.loop(0, slots // WIDE)
        def _(at):
            rows = wide_rows(at)
            dact = dot(low_ref[rows, :], wd_ref[...], NT)
            dpre = (dact * slope_ref[rows, :].astype(jnp.float32)).astype(jnp.bfloat16)
            dbu_ref[...] += jnp.sum(dpre.astype(jnp.float32), axis=0, keepdims=True)
            tail_ref[rows, :] = dpre
            total_ref[rows, :] += dot(dpre, wu_ref[...], NN)

        sends[4].start()
        store_halves(late_ref, dot(tail_ref[...], hidden_ref[...], TN))

    @pl.when((step > TAIL_STEP) & (step < PAIR_STEP))
    def _():
        store_halves(late_ref, dot(act_ref[step - TAIL_STEP - 1], low_ref[...], TN))

    @pl.when(step >= PAIR_STEP)
    def _():
        store_halves(late_ref, dot(dpair_ref[step - PAIR_STEP], pooled_ref[...], TN))

    @pl.when(step == PAIR_STEP + 1)
    def _():
        for send in sends:
            send.wait()


def middle(att, tokens, weights, vectors, segments, cot_pair, cot_out, patches):
    slots = att.shape[0]
    full = once((slots, D))
    anywhere = pl.BlockSpec(memory_space=pl.ANY)
    low = jnp.bfloat16

    def part(step):
        return jnp.clip(step - 1, 0, PARTS - 1)

    def half_row(step):
        return jnp.clip(step - TAIL_STEP, 0, PARTS + 2)

    return pl.pallas_call(
        middle_kernel,
        grid=(PAIR_STEP + 2,),
        in_specs=[
            pl.BlockSpec(memory_space=pltpu.SMEM),
            full,
            full,
            square(3),
            pl.BlockSpec((D, D), lambda i: (4 + part(i), 0)),
            pl.BlockSpec((D, D), lambda i: (4 + PARTS + part(i), 0)),
            square(4 + 2 * PARTS),
            square(5 + 2 * PARTS),
            once(vectors.shape),
            once((1, slots)),
            once((SEGS, SEGS)),
            full,
        ],
        out_specs=[
            pl.BlockSpec((slots, D), lambda i: (0, part(i))),
            pl.BlockSpec(HALF_BLOCK, lambda i: (0, half_row(i), 0)),
            fixed((SEGS, SEGS)),
            fixed((8, D)),
            fixed((1, D)),
            fixed((slots, 1)),
        ]
        + [anywhere] * 5,
        out_shape=[
            shape_of((slots, FF), low),
            shape_of((2, HALF_ROWS, D // 2), low),
            shape_of((SEGS, SEGS)),
            shape_of((8, D)),
            shape_of((1, D)),
            shape_of((slots, 1)),
            shape_of((slots, D), low),
            shape_of((slots, D)),
            shape_of((slots, D), low),
            shape_of((slots, D), low),
            shape_of((slots, D)),
        ],
        scratch_shapes=[
            pltpu.VMEM((PARTS, slots, D), low),
            pltpu.VMEM((slots, D), low),
            pltpu.VMEM((slots, D), low),
            pltpu.VMEM((slots, D), jnp.float32),
            pltpu.VMEM((slots, D), low),
            pltpu.VMEM((slots, D), low),
            pltpu.VMEM((slots, D), jnp.float32),
            pltpu.VMEM((slots, D), jnp.float32),
            pltpu.VMEM((slots, 1), jnp.float32),
            pltpu.VMEM((SEGS, D), jnp.float32),
            pltpu.VMEM((SEGS, D), low),
            pltpu.VMEM((2, SEGS, D), low),
            pltpu.SemaphoreType.DMA((5,)),
        ],
        compiler_params=params(),
        cost_estimate=cost(20e9, 40e6),
        name="middle",
    )(
        patches,
        att,
        tokens,
        *[weights] * 5,
        vectors,
        segments,
        cot_pair,
        cot_out,
    )


def head_sums(values):
    rows = lax.broadcasted_iota(jnp.int32, (GW, GW), 0)
    cols = lax.broadcasted_iota(jnp.int32, (GW, GW), 1)
    takes = (rows // PAIR == cols // PAIR) & (rows // HDIM != cols // HDIM)
    takes = takes.astype(jnp.float32).astype(jnp.bfloat16)
    sums = jnp.concatenate(
        [split_dot_left(values[:, at : at + GW], takes, NN) for at in range(0, D, GW)], axis=1
    )
    high = sums.astype(jnp.bfloat16).astype(jnp.float32)
    middle = (sums - high).astype(jnp.bfloat16).astype(jnp.float32)
    place = lax.broadcasted_iota(jnp.int32, (1, D), 1) % HDIM
    terms = jnp.where(place == 0, high, jnp.where(place == 1, middle, sums - high - middle))
    return jnp.where(place < 3, terms, 0.0).astype(jnp.bfloat16)


def feed_backward_kernel(
    low_ref,
    hidden_ref,
    inv1_ref,
    vectors_ref,
    slope_ref,
    wd_ref,
    wu_ref,
    wo_ref,
    start_in,
    normed1_in,
    att_in,
    inv_sum_in,
    exact_in,
    early_ref,
    dbu_ref,
    sums_ref,
    dres_out,
    datt_out,
    terms_out,
    total_ref,
    normed1_ref,
    att_ref,
    inv_sum_ref,
    exact_ref,
    grad_ref,
    datt_ref,
    terms_ref,
    sems,
):
    step = pl.program_id(0)
    slots = low_ref.shape[0]
    last = pl.num_programs(0) - 1
    loads = [
        pltpu.make_async_copy(src, dst, sems.at[i])
        for i, (src, dst) in enumerate(
            (
                (start_in, total_ref),
                (normed1_in, normed1_ref),
                (att_in, att_ref),
                (inv_sum_in, inv_sum_ref),
                (exact_in, exact_ref),
            )
        )
    ]

    @pl.when(step == 0)
    def _():
        for load in loads:
            load.start()

    @pl.when(step < last)
    def _():
        dact = dot(low_ref[...], wd_ref[...], NT)
        dpre = (dact * slope_ref[...].astype(jnp.float32)).astype(jnp.bfloat16)
        dbu_ref[...] = jnp.sum(dpre.astype(jnp.float32), axis=0, keepdims=True)
        store_halves(early_ref, dot(dpre, hidden_ref[...], TN))
        pl.when(step == 0)(loads[0].wait)
        total_ref[...] += dot(dpre, wu_ref[...], NN)

    @pl.when(step == last)
    def _():
        sums_ref[...] = jnp.zeros_like(sums_ref)
        for load in loads[1:]:
            load.wait()

        def rows_step(at):
            rows = tile_rows(at)
            grad = total_ref[rows, :]
            normed = normed1_ref[rows, :]
            sums_ref[0:1, :] += jnp.sum(grad * normed, axis=0, keepdims=True)
            sums_ref[1:2, :] += jnp.sum(grad, axis=0, keepdims=True)
            dres = normalize_back(grad * vectors_ref[0:1, :], normed, inv1_ref[rows, :])
            low = dres.astype(jnp.bfloat16)
            sums_ref[4:5, :] += jnp.sum(low.astype(jnp.float32), axis=0, keepdims=True)
            total_ref[rows, :] = dres
            grad_ref[rows, :] = low
            datt = dot(low, wo_ref[...], NN).astype(jnp.bfloat16).astype(jnp.float32)
            datt = (datt * inv_sum_ref[rows, :]).astype(jnp.bfloat16)
            datt_ref[rows, :] = datt
            terms_ref[rows, :] = head_sums(datt.astype(jnp.float32) * exact_ref[rows, :])

        pl.loop(0, slots // TILE)(rows_step)
        sends = [
            pltpu.make_async_copy(src, dst, sems.at[5 + i])
            for i, (src, dst) in enumerate(
                ((total_ref, dres_out), (datt_ref, datt_out), (terms_ref, terms_out))
            )
        ]
        for send in sends:
            send.start()
        store_halves(early_ref, dot(grad_ref[...], att_ref[...], TN))
        for send in sends:
            send.wait()


def feed_backward(low, start, normed1, inv1, hidden, slope, att, inv_sum, exact, vectors, weights):
    slots = low.shape[0]
    last = PARTS - 1
    full = once((slots, D))
    anywhere = pl.BlockSpec(memory_space=pl.ANY)

    def at(i):
        return jnp.minimum(i, last - 1)

    return pl.pallas_call(
        feed_backward_kernel,
        grid=(PARTS,),
        in_specs=[
            full,
            full,
            once((slots, 1)),
            once(vectors.shape),
            pl.BlockSpec((slots, D), lambda i: (0, at(i))),
            pl.BlockSpec((D, D), lambda i: (4 + PARTS + at(i), 0)),
            pl.BlockSpec((D, D), lambda i: (4 + at(i), 0)),
            square(3),
        ]
        + [anywhere] * 5,
        out_specs=[
            pl.BlockSpec(HALF_BLOCK, lambda i: (0, jnp.where(i == last, 0, 1 + i), 0)),
            pl.BlockSpec((1, D), lambda i: (0, at(i))),
            fixed((8, D)),
        ]
        + [anywhere] * 3,
        out_shape=[
            shape_of((2, FF, D // 2), jnp.bfloat16),
            shape_of((1, FF - D)),
            shape_of((8, D)),
            shape_of((slots, D)),
            shape_of((slots, D), jnp.bfloat16),
            shape_of((slots, D), jnp.bfloat16),
        ],
        scratch_shapes=[
            pltpu.VMEM((slots, D), jnp.float32),
            pltpu.VMEM((slots, D), jnp.float32),
            pltpu.VMEM((slots, D), jnp.bfloat16),
            pltpu.VMEM((slots, D), jnp.float32),
            pltpu.VMEM((slots, D), jnp.float32),
            pltpu.VMEM((slots, D), jnp.bfloat16),
            pltpu.VMEM((slots, D), jnp.bfloat16),
            pltpu.VMEM((slots, D), jnp.bfloat16),
            pltpu.SemaphoreType.DMA((8,)),
        ],
        compiler_params=params(),
        cost_estimate=cost(17e9, 40e6),
        name="feed_backward",
    )(low, hidden, inv1, vectors, slope, weights, weights, weights, start, normed1, att, inv_sum, exact)


def attention_backward_kernel(
    patches_ref,
    grown_ref,
    datt_ref,
    terms_ref,
    v_ref,
    k_ref,
    q_ref,
    box_row_ref,
    dqkv_ref,
    dcoef_ref,
    box_col_ref,
    bucket0_ref,
    bucket1_ref,
    dscore_ref,
):
    pair = pl.program_id(0)
    slots = datt_ref.shape[0]
    low = jnp.bfloat16
    live_row = lax.broadcasted_iota(jnp.int32, (1, slots), 1) < TEXT + patches_ref[0]

    @pl.when(pair == 0)
    def _():
        write_buckets(box_row_ref, box_col_ref, (bucket0_ref, bucket1_ref), live_row)

    query_t = q_ref[...].astype(jnp.float32).T.astype(low)
    key_t = (k_ref[...].astype(jnp.float32) * HDIM ** (-0.5)).T
    key_t = jnp.where(live_row, key_t, 0.0).astype(low)
    datt_t = datt_ref[...].astype(jnp.float32).T.astype(low)
    lanes = lax.broadcasted_iota(jnp.int32, (1, PAIR), 1)
    second = lanes >= HDIM
    masks = [jnp.where(second, 0.0, 1.0), jnp.where(second, 1.0, 0.0)]
    masks = [mask.astype(low) for mask in masks]
    dcoef_ref[...] = jnp.zeros_like(dcoef_ref)
    leads = []
    values = []
    for j in range(2):
        at = HDIM * (1 - j)
        minus = jnp.where((lanes >= at) & (lanes < at + 3), -1.0, 0.0).astype(low)
        leads.append(datt_ref[...] * masks[j] + terms_ref[...] * masks[1 - j])
        values.append(v_ref[...] * masks[j] + minus)

    for j in range(2):
        head_rows = slice(j * HDIM, (j + 1) * HDIM)
        for step in range(slots // TILE):
            rows = slice(step * TILE, (step + 1) * TILE)
            diff = dot(leads[j][rows], values[j], NT)
            dscore = grown_ref[j, rows, :].astype(jnp.float32) * diff
            dscore_ref[j, rows, :] = dscore.astype(low)
            dcoef_ref[j, 0:1, :] += jnp.sum(dscore * bucket0_ref[rows, :], axis=0, keepdims=True)
            dcoef_ref[j, 1:2, :] += jnp.sum(dscore * bucket1_ref[rows, :], axis=0, keepdims=True)
        dqkv_ref[0, head_rows] = dot(key_t[head_rows], dscore_ref[j], NT).astype(low)
        dkey = dot(query_t[head_rows], dscore_ref[j], NN) * (1.0 / LOG2E)
        dqkv_ref[1, head_rows] = jnp.where(live_row, dkey, 0.0).astype(low)
        dvalue = dot(datt_t[head_rows], grown_ref[j], NN)
        dqkv_ref[2, head_rows] = jnp.where(live_row, dvalue, 0.0).astype(low)


def attention_backward(grown, datt, terms, q, k, v, boxes, patches):
    slots = datt.shape[0]
    pair_block = pl.BlockSpec((slots, PAIR), lambda h: (0, h))
    return pl.pallas_call(
        attention_backward_kernel,
        grid=(HEADS // 2,),
        in_specs=[
            pl.BlockSpec(memory_space=pltpu.SMEM),
            pl.BlockSpec((2, slots, slots), lambda h: (h, 0, 0)),
        ]
        + [pair_block] * 5
        + [fixed((2, slots))],
        out_specs=[
            pl.BlockSpec((3, PAIR, slots), lambda h: (0, h, 0)),
            pl.BlockSpec((2, 2, slots), lambda h: (h, 0, 0)),
        ],
        out_shape=[
            shape_of((3, D, slots), jnp.bfloat16),
            shape_of((HEADS, 2, slots)),
        ],
        scratch_shapes=[pltpu.VMEM((slots, 8), jnp.int32)]
        + [pltpu.VMEM((slots, slots), jnp.float32)] * 2
        + [pltpu.VMEM((2, slots, slots), jnp.bfloat16)],
        compiler_params=params(),
        cost_estimate=cost(15e9, 40e6),
        name="attention_backward",
    )(patches, grown, datt, terms, v, k, q, boxes)


def qkv_weights_kernel(dqkv_ref, tokens_ref, rest_ref, first_ref, sums_ref):
    step = pl.program_id(0)
    last = pl.num_programs(0) - 1

    @pl.when(step < last)
    def _():
        part = dqkv_ref[0]
        store_halves(first_ref, dot(part, tokens_ref[...], NN))
        sums_ref[0] = dot(jnp.ones((8, part.shape[1]), jnp.bfloat16), part, NT)

    @pl.when(step == last)
    def _():
        first_ref[...] = rest_ref[...]


def qkv_weights(dqkv, tokens, rest):
    slots = tokens.shape[0]
    block = D // 2
    parts = 3 * D // block

    def at(i):
        return jnp.minimum(i, parts - 1)

    return pl.pallas_call(
        qkv_weights_kernel,
        grid=(parts + 1,),
        in_specs=[
            pl.BlockSpec((1, block, slots), lambda i: (at(i) // 2, at(i) % 2, 0)),
            once((slots, D)),
            once((2, block, D // 2)),
        ],
        out_specs=[
            pl.BlockSpec((2, block, D // 2), lambda i: (0, i, 0)),
            pl.BlockSpec((1, 8, block), lambda i: (at(i) // 2, 0, at(i) % 2)),
        ],
        out_shape=[
            shape_of((2, (parts + 1) * block, D // 2), jnp.bfloat16),
            shape_of((3, 8, D)),
        ],
        compiler_params=params(),
        cost_estimate=cost(3.6e9, 10e6),
        name="qkv_weights",
    )(dqkv, tokens, rest)


def token_gradient_kernel(dqkv_ref, weight_ref, dres_ref, grad_ref):
    total = dres_ref[...]
    for part in range(3):
        total = total + dot(dqkv_ref[part], weight_ref[part * D : (part + 1) * D, :], TN)
    grad_ref[...] = total.astype(jnp.bfloat16)


def token_gradient(dqkv, weights, dres):
    slots = dres.shape[0]
    tile = pl.BlockSpec((TILE, D), lambda i: (i, 0))
    return pl.pallas_call(
        token_gradient_kernel,
        grid=(slots // TILE,),
        in_specs=[
            pl.BlockSpec((3, D, TILE), lambda i: (0, 0, i)),
            pl.BlockSpec((3 * D, D), lambda i: (0, 0), pipeline_mode=pl.Buffered(1)),
            tile,
        ],
        out_specs=tile,
        out_shape=shape_of((slots, D), jnp.bfloat16),
        compiler_params=params(),
        cost_estimate=cost(3.6e9, 12e6),
        name="token_gradient",
    )(dqkv, weights, dres)


def page_step(
    tokens, boxes, segments, patches, cot_out, cot_pair, pieces, layout, vectors, box_coef
):
    (q, k, v, grown, att, inv_sum, exact), weights = attention_forward(
        tokens, pieces, layout, vectors, boxes, patches, box_coef
    )
    slope, late, pair_scores, sums2, dbu_tail, inv1, mixed, normed1, hidden, low, start = middle(
        att, tokens, weights, vectors, segments, cot_pair, cot_out, patches
    )
    early, dbu_head, sums1, dres, datt, terms = feed_backward(
        low, start, normed1, inv1, hidden, slope, att, inv_sum, exact, vectors, weights
    )
    dqkv, dcoef = attention_backward(grown, datt, terms, q, k, v, boxes, patches)
    dqkv, middle_rows = lax.optimization_barrier((dqkv, core_sum(early)))
    first_rows, bias_sums = qkv_weights(dqkv, tokens, early)
    first_rows, late = lax.optimization_barrier((first_rows, scatter_dp(late)))
    token_grad = token_gradient(dqkv, weights, dres)
    early, late, token_grad = scatter_first(first_rows, early, middle_rows, scatter_grid(late), token_grad)
    vector_part = jnp.concatenate(
        [
            sums1[:2],
            bias_sums[0, :1],
            bias_sums[2, :1],
            sums1[4:5],
            sums2[:3],
            dbu_head.reshape(FF // D - 1, D),
            dbu_tail,
        ],
        axis=0,
    )
    coef_part = jnp.sum(dcoef, axis=2).T
    return (mixed, pair_scores, token_grad, early, late, vector_part, coef_part)


def exchange_sum(values):
    steps = [(axis, 1 << bit) for axis in ("grid", "dp") for bit in range(lax.axis_size(axis).bit_length() - 1)]
    steps.sort(key=lambda step: step != ("dp", 1))
    for axis, reach in steps:
        values = values + lax.ppermute(values, axis, [(i, i ^ reach) for i in range(lax.axis_size(axis))])
    return values


def scatter_dp(halves):
    return lax.psum_scatter(
        halves.reshape(-1, D // 2), "dp", scatter_dimension=0, tiled=True
    )


SPLIT_AT = 2 * HALF_ROWS // 4 - 3 * D


def by_links():
    return (lax.axis_size("dp"), lax.axis_size("grid")) == (8, 4)


def exchange(values, reach):
    return lax.ppermute(values, "dp", [(i, i ^ reach) for i in range(lax.axis_size("dp"))])


def add_low(a, b):
    return (a.astype(jnp.float32) + b.astype(jnp.float32)).astype(jnp.bfloat16)


def core_rows(take):
    core = lax.axis_index("dp") % 2
    rows = add_low(take(core), exchange(take(1 - core), 1))
    return rows.reshape(2, lax.axis_size("grid"), -1, D // 2)


def core_sum(rest):
    if not by_links():
        return rest
    count = HALF_ROWS // 4
    return core_rows(lambda core: lax.dynamic_slice_in_dim(rest, SPLIT_AT + core * count, count, 1))


def scatter_first(first_rows, rest, summed, late, token_grad):
    if not by_links():
        return scatter_dp(jnp.concatenate([first_rows, rest[:, SPLIT_AT:]], axis=1)), late, token_grad
    count = HALF_ROWS // 4
    zero = core_rows(lambda core: lax.dynamic_slice_in_dim(first_rows, core * count, count, 1))
    place = lax.axis_index("dp")
    x, y = place // 2 % 2, place // 4
    both = jnp.stack([zero, summed])
    half = zero.shape[1] // 2

    def pick(values, at, axis=0):
        return lax.dynamic_index_in_dim(values, at, axis, keepdims=False)

    by_x, by_y = both[:, :, :half], both[:, :, half:]
    sent_x = exchange(pick(by_x, 1 - x), 2)
    sent_y = exchange(pick(by_y, 1 - y, 1), 4)
    sent_x, sent_y, late, token_grad = lax.optimization_barrier((sent_x, sent_y, late, token_grad))
    by_x = add_low(pick(by_x, x), sent_x)
    by_y = add_low(pick(by_y, y, 1), sent_y)
    sent_x = exchange(pick(by_y, 1 - x), 2)
    sent_y = exchange(pick(by_x, 1 - y), 4)
    by_x = add_low(pick(by_x, y), sent_y)
    by_y = add_low(pick(by_y, x), sent_x)
    return jnp.concatenate([by_x, by_y]).reshape(-1, D // 2), late, token_grad


def scatter_grid(rows):
    size = lax.axis_size("grid")
    place = lax.axis_index("grid")
    blocks = rows.reshape(size, -1, D // 2)

    def block(at):
        return lax.dynamic_index_in_dim(blocks, at % size, 0, keepdims=False)

    got = [
        lax.ppermute(block(place + s), "grid", [(i, (i + s) % size) for i in range(size)])
        for s in range(1, size)
    ]
    return sum((g.astype(jnp.float32) for g in got), block(place).astype(jnp.float32))


def swap_halves(first, second):
    size = lax.axis_size("dp")
    low = lax.axis_index("dp") < size // 2
    other = lax.ppermute(
        jnp.where(low, second, first).astype(jnp.bfloat16), "dp", [(i, (i + size // 2) % size) for i in range(size)]
    ).astype(jnp.float32)
    kept = jnp.where(low, first, second)
    return jnp.concatenate([jnp.where(low, kept, other), jnp.where(low, other, kept)], axis=1)


def gather_weights(shard, ready):
    dp_size, grid_size = lax.axis_size("dp"), lax.axis_size("grid")
    rows = shard.shape[0]
    if (dp_size, grid_size) != (8, 4) or rows != 336:
        return [lax.all_gather(shard, ("dp", "grid"), axis=0, tiled=True)], None
    barrier = lax.optimization_barrier

    def over(values, reach):
        return lax.ppermute(values, "dp", [(i, i ^ reach) for i in range(dp_size)])

    def up(values, reach):
        return lax.ppermute(values, "grid", [(i, (i + reach) % grid_size) for i in range(grid_size)])

    cuts = (0, *CUTS)
    one, two = (shard[a:b] for a, b in zip(cuts, cuts[1:]))
    rest = lax.all_gather(shard[cuts[-1] :], ("dp", "grid"), axis=0)
    hops = (1, 2, 3)
    one_grid = jnp.stack([one] + [up(one, s) for s in hops])
    one_grid, two, *_ = barrier((one_grid, two, *ready))
    one_x, one_y = over(one_grid, 2), over(one_grid, 4)
    two_grid = jnp.stack([two] + [up(two, s) for s in hops])
    one_x, one_y, two_grid = barrier((one_x, one_y, two_grid))
    two_x, two_y = over(two_grid, 2), over(two_grid, 4)
    two_x, two_y = barrier((two_x, two_y))
    xy = over(jnp.concatenate([one_y[:2], two_y[:2]], axis=1), 2)
    yx = over(jnp.concatenate([one_x[2:], two_x[2:]], axis=1), 4)
    own = [one_grid, one_x, one_y, two_grid, two_x, two_y, xy, yx]
    every = tuple(range(grid_size))
    layout = [(cuts[part], [(r, s) for s in every]) for part in (0, 1) for r in (0, 2, 4)]
    layout += [(0, [(6, s) for s in (0, 1)]), (0, [(6, s) for s in (2, 3)])]
    layout += [(start, [(r ^ 1, s) for r, s in entries]) for start, entries in layout]
    pieces = own + [over(piece, 1) for piece in own]
    return pieces + [rest], layout + [(cuts[-1], None)]


CUTS = (96, 208)


def momentum_step(grad, param, moment, average, rate):
    new_moment = 0.5 * moment + grad
    new_param = param - rate * (grad + 0.5 * new_moment)
    new_average = 0.5 * average + 0.5 * new_param
    return (new_moment, new_param, new_average)


def on_device(
    tokens,
    boxes,
    segments,
    patches,
    cot_out,
    cot_pair,
    weights,
    weight_momentum,
    weight_average,
    vectors,
    vector_momentum,
    vector_average,
    box_coef,
    coef_momentum,
    coef_average,
):
    axes = ("dp", "grid")
    page_count, slot_count = tokens.shape[:2]
    device_count = lax.axis_size(axes)
    segments = jnp.pad(segments, ((0, 0), (0, slot_count - segments.shape[1])), constant_values=SEGS)
    pieces, layout = gather_weights(weights.astype(jnp.bfloat16), (segments,))
    pages = [
        page_step(
            tokens[p],
            boxes[p],
            segments[p : p + 1],
            patches[p : p + 1],
            cot_out[p],
            cot_pair[p],
            pieces,
            layout,
            vectors,
            box_coef,
        )
        for p in range(page_count)
    ]
    mixed, pair_scores, token_grad = (jnp.stack([page[i] for page in pages]) for i in range(3))
    early, late = (sum(page[i] for page in pages) for i in (3, 4))
    small = sum(
        jnp.concatenate([page[5], jnp.pad(page[6].reshape(1, 2 * HEADS), ((0, 3), (0, D - 2 * HEADS)))], axis=0)
        for page in pages
    )
    late_rows = late
    early_rows = scatter_grid(early)
    small = exchange_sum(small)
    weight_grad = swap_halves(early_rows, late_rows)
    vector_rows = vectors.shape[0]
    vector_grad = small[:vector_rows]
    coef_grad = small[vector_rows, : 2 * HEADS].reshape(2, HEADS)
    rate_scale = (device_count * page_count * slot_count) ** (-0.5)
    new_weight_momentum, new_weights, new_weight_average = momentum_step(
        weight_grad, weights, weight_momentum, weight_average, 0.1 * rate_scale
    )
    new_vector_momentum, new_vectors, new_vector_average = momentum_step(
        vector_grad, vectors, vector_momentum, vector_average, 0.1 * rate_scale
    )
    new_coef_momentum, new_coef, new_coef_average = momentum_step(
        coef_grad, box_coef, coef_momentum, coef_average, 0.01 * rate_scale
    )
    return (
        mixed,
        pair_scores,
        token_grad,
        weight_grad,
        new_weights,
        new_weight_momentum,
        new_weight_average,
        new_weights.astype(jnp.bfloat16),
        vector_grad,
        new_vectors,
        new_vector_momentum,
        new_vector_average,
        coef_grad,
        new_coef,
        new_coef_momentum,
        new_coef_average,
    )


def solution(mesh):
    rows = P(("dp", "grid"))
    return jax.shard_map(
        on_device,
        mesh=mesh,
        in_specs=(rows,) * 9 + (P(),) * 6,
        out_specs=(rows,) * 8 + (P(),) * 8,
        check_vma=False,
    )
```
